32 devices in a mesh: pb: 2 (over x), pa: 16 (over z, y, core).
Axes of the slice: x: 2, y: 2, z: 4, core: 2. Of those that a mesh axis runs over, the one named last changes fastest.
Arguments:
- question_rows: bfloat16 [256, 64, 768], P(('pb', 'pa')), may hold values from -6 to 6
- passage_rows: bfloat16 [128, 256, 768], P(('pb', 'pa')), may hold values from -6 to 6
- segment_lengths: int32 [128, 3], P(('pb', 'pa')), may hold values from 1 to 128, 256 in all within a row
- positives: int32 [256], P('pb'), may hold values from 0 to 383
- negatives: bfloat16 [4096, 768], P('pa'), may hold values from -6 to 6
- question_cotangent: bfloat16 [256, 64, 768], P(('pb', 'pa')), may hold values from -12 to 12
- passage_cotangent: bfloat16 [128, 256, 768], P(('pb', 'pa')), may hold values from -12 to 12
- loss_weight: float32 [256], P('pb'), may hold values from 4 to 12
- projection: bfloat16 [2, 768, 2304], replicated, may hold values from -0.21875 to 0.21875
- mixing: bfloat16 [2, 768, 768], replicated, may hold values from -1.75 to 1.75
- expand: bfloat16 [2, 768, 3072], replicated, may hold values from -0.21875 to 0.21875
- shrink: bfloat16 [2, 3072, 768], replicated, may hold values from -0.109375 to 0.109375
- biases: bfloat16 [2, 6, 768], replicated, may hold values from -1.75 to 1.75
- gains: bfloat16 [2, 2, 768], replicated, may hold values from 0.5 to 1.5
- widening: bfloat16 [2, 3072], replicated, may hold values from -1.75 to 1.75
Outputs:
- question_states: bfloat16 [256, 64, 768], P(('pb', 'pa'))
- passage_states: bfloat16 [128, 256, 768], P(('pb', 'pa'))
- question_loss: float32 [256], P('pb')
- question_grad: float32 [256, 64, 768], P(('pb', 'pa'))
- passage_grad: float32 [128, 256, 768], P(('pb', 'pa'))
- projection_grad: float32 [2, 768, 2304], P(None, 'pa')
- mixing_grad: float32 [2, 768, 768], P(None, 'pa')
- expand_grad: float32 [2, 768, 3072], P(None, 'pa')
- shrink_grad: float32 [2, 3072, 768], P(None, 'pa')
- biases_grad: float32 [2, 6, 768], P(None, None, 'pa')
- gains_grad: float32 [2, 2, 768], P(None, None, 'pa')
- widening_grad: float32 [2, 3072], P(None, 'pa')
The draws below stay inside these ranges and needn't reach their ends.
Inputs may be any that keep to these rules, and one draw needn't show every extreme that they name: `segment_lengths`: each row's 3 passage lengths sum to 256; the longest in each row has exactly 128 tokens.
All inputs are finite; a program needn't handle non-finite values.
Results may differ from the reference program's by a relative error of at most 0.012.
Values may be sent and summed in bfloat16 or wider, within the bound.
A program may use at most 320 MiB of HBM per device.

```python
import math
import jax
import jax.numpy as jnp
import numpy as np
from jax import lax

D = 768
HEADS = 12
HEAD_DIM = 64
FF = 3072
LQ = 64
LP = 256
SEGS = 3
LONGEST = 128
NQ = 256
NPR = 128
NPASS = 384
NBANK = 4096


def plant(result, key, smallest, largest):
    dims = result.shape
    place = [jax.random.randint(jax.random.fold_in(key, axis), (), 0, dims[axis]) for axis in range(len(dims))]
    result = result.at[tuple(place)].set(smallest)
    longest = dims.index(max(dims))
    place[longest] = (place[longest] + 1) % dims[longest]
    return result.at[tuple(place)].set(largest)


def raised(entries, stream_key, source, target, blocks, factor):
    owner, partner = [(jnp.arange(entries.shape[axis_at]) // (entries.shape[axis_at] // blocks)).reshape([-1 if axis == axis_at else 1 for axis in range(entries.ndim)]) for axis_at in (source, target)]
    chosen = jax.random.permutation(stream_key, blocks)[partner]
    strong = (owner == chosen) | (owner == (partner + blocks // 2) % blocks)
    return jnp.where(strong, factor * entries, entries)


def steps_of(key, shape, split, least, top_value):
    factor_of, own = 1.0, jax.random.fold_in(key, 6)
    for position, shards_of in split:
        heights = jnp.exp(jax.random.uniform(jax.random.fold_in(own, position), (shards_of,), jnp.float32, least / len(split), top_value / len(split)))
        factor_of = factor_of * jnp.repeat(heights, shape[position] // shards_of).reshape([-1 if axis == position else 1 for axis in range(len(shape))])
    return factor_of


def profile(count, total, most, lean):
    weights = [(1 << 20) // math.isqrt(rank ** lean) + 1 for rank in range(2, count + 1)]
    rest, holding = total - most - (count - 1), [1] * (count - 1)
    while rest > 0:
        movable = [i for i in range(count - 1) if holding[i] < most]
        mass, remaining = sum([weights[i] for i in movable]), rest
        for i in movable:
            more = min(most - holding[i], max(1, remaining * weights[i] // mass), rest)
            holding[i] = holding[i] + more
            rest = rest - more
    return np.array([most] + holding)


def uneven(key, amount, total, limit, slope):
    if amount == 2:
        one = jax.random.randint(key, (), max(1, total - limit), min(limit, total - 1) + 1)
        return jnp.stack([one, total - one])
    tallies = jnp.asarray(profile(amount, total, limit, slope), jnp.int32)
    pairs = (amount - 1) // 2
    donor, taker = tallies[1:1 + 2 * pairs:2], tallies[2:2 + 2 * pairs:2]
    margin = jnp.minimum(donor - 1, limit - taker)
    passed = jax.random.randint(jax.random.fold_in(key, 1), (pairs,), 0, 1 << 20) % (margin + 1)
    tallies = tallies.at[1:1 + 2 * pairs:2].set(donor - passed).at[2:2 + 2 * pairs:2].set(taker + passed)
    return tallies[jax.random.permutation(jax.random.fold_in(key, 2), amount)]


def gaussian(stream_key, shape, scale, limit, pieces=(), kind=jnp.bfloat16):
    result = scale * jax.random.normal(stream_key, shape, jnp.float32)
    if pieces:
        result = result * steps_of(stream_key, shape, pieces, -0.22, 0.18)
    return jnp.clip(result, -limit, limit).astype(kind)


def noise_with(stream_key, shape, scale, bound, cuts, heavy, kind=jnp.bfloat16):
    array = scale * jax.random.normal(stream_key, shape, jnp.float32)
    if cuts:
        array = array * steps_of(stream_key, shape, cuts, -0.22, 0.18)
    return jnp.clip(raised(array, jax.random.fold_in(stream_key, 3), *heavy), -bound, bound).astype(kind)


def setup_inputs(seed: int = 0) -> dict:
    seeds = jax.random.split(jax.random.key(seed), 16)
    question_rows = gaussian(seeds[0], (NQ, LQ, D), 1.0, 6.0, ((0, 32),))
    passage_rows = gaussian(seeds[1], (NPR, LP, D), 1.0, 6.0, ((0, 32),))
    segment_lengths = jax.vmap(lambda own: uneven(own, SEGS, LP, LONGEST, 2))(jax.random.split(seeds[2], NPR)).reshape((NPR, SEGS)).astype(jnp.int32)
    positives = plant(jax.random.randint(seeds[3], (NQ,), 0, NPASS), jax.random.fold_in(seeds[3], 1), 0, NPASS - 1).astype(jnp.int32)
    negatives = gaussian(seeds[4], (NBANK, D), 1.0, 6.0, ((0, 16),))
    question_cotangent = noise_with(seeds[5], (NQ, LQ, D), 1.0, 12.0, ((0, 32),), (0, 2, 32, 2.75))
    passage_cotangent = noise_with(seeds[6], (NPR, LP, D), 1.0, 12.0, ((0, 32),), (0, 2, 32, 2.75))
    loss_weight = jnp.clip(4.0 + 8.0 * jax.random.uniform(seeds[7], (NQ,), jnp.float32) ** steps_of(seeds[7], (NQ,), ((0, 2),), -0.2, 0.2), 4.0, 12.0)
    projection = gaussian(seeds[8], (2, D, 3 * D), D ** -0.5, 0.21875)
    mixing = gaussian(seeds[9], (2, D, D), (max(D // 64, 1)) ** -0.5, 1.75)
    expand = gaussian(seeds[10], (2, D, FF), D ** -0.5, 0.21875)
    shrink = gaussian(seeds[11], (2, FF, D), FF ** -0.5, 0.109375)
    biases = gaussian(seeds[12], (2, 6, D), 0.3, 1.75)
    gains = jnp.clip(1.0 + 0.1 * jax.random.normal(seeds[13], (2, 2, D), jnp.float32), 0.5, 1.5).astype(jnp.bfloat16)
    widening = gaussian(seeds[14], (2, FF), 0.3, 1.75)
    return dict(question_rows=question_rows, passage_rows=passage_rows, segment_lengths=segment_lengths, positives=positives, negatives=negatives, question_cotangent=question_cotangent, passage_cotangent=passage_cotangent, loss_weight=loss_weight, projection=projection, mixing=mixing, expand=expand, shrink=shrink, biases=biases, gains=gains, widening=widening)


@jax.custom_vjp
def low(v):
    return lax.optimization_barrier(v.astype(jnp.bfloat16)).astype(jnp.float32)

@jax.custom_vjp
def low_back(v):
    return v

def low_keep(v):
    return (low(v), None)

def low_pass(kept, grad):
    return (grad,)

def back_keep(v):
    return (v, None)

def back_low(kept, grad):
    return (low(grad),)
low.defvjp(low_keep, low_pass)
low_back.defvjp(back_keep, back_low)
highest = lax.Precision.HIGHEST
masked_score = -1000000000.0

def matmul(left_side, right_side):
    return jnp.dot(left_side, right_side, precision=highest, preferred_element_type=jnp.float32)

def normed(values, gain_row, shift_row):
    centre = values - lax.optimization_barrier(jnp.mean(values, axis=-1, keepdims=True))
    spread = lax.optimization_barrier(jnp.mean(centre * centre, axis=-1, keepdims=True))
    return centre * lax.rsqrt(spread + 1e-12) * gain_row + shift_row

def layout(lengths, length):
    segment_ends = jnp.cumsum(lengths, axis=-1, dtype=jnp.int32)
    starts = segment_ends - lengths
    positions = jnp.arange(length, dtype=jnp.int32)
    segment = lax.optimization_barrier(jnp.sum((positions[None, :, None] >= segment_ends[:, None, :]).astype(jnp.int32), axis=-1, dtype=jnp.int32))
    return (segment, starts)

def encode(weights, tokens, segment):
    projection, mixing, expand, shrink, biases, gains, widening = weights
    row_count, length, features = tokens.shape
    flattened = tokens.reshape(row_count * length, features)
    packed_bias = jnp.concatenate([biases[0], jnp.zeros_like(biases[0]), biases[1]])
    packed = low(low_back(matmul(flattened, projection) + packed_bias))
    head_split = packed.reshape(row_count, length, 3, HEADS, HEAD_DIM)
    scores = jnp.einsum('rqhd,rkhd->rhqk', head_split[:, :, 0], head_split[:, :, 1], precision=highest) * HEAD_DIM ** (-0.5)
    scores = low_back(scores)
    allowed = segment[:, None, :, None] == segment[:, None, None, :]
    scores = jnp.where(allowed, scores, masked_score)
    attention = low(jax.nn.softmax(scores, axis=-1))
    context = jnp.einsum('rhqk,rkhd->rqhd', attention, head_split[:, :, 2], precision=highest)
    context = low(low_back(context.reshape(row_count * length, features)))
    branch = low_back(matmul(context, mixing) + biases[2])
    first_out = normed(flattened + branch, gains[0], biases[3])
    hidden = low_back(matmul(low(first_out), expand) + widening)
    active = low(jax.nn.gelu(hidden, approximate=False))
    second = low_back(matmul(active, shrink) + biases[4])
    return normed(first_out + second, gains[1], biases[5]).reshape(row_count, length, features)

def run_encoder(weights, tokens, segment, block_rows):
    groups = tokens.shape[0] // block_rows
    shaped = tokens.reshape((groups, block_rows) + tokens.shape[1:])
    grouped = segment.reshape((groups, block_rows) + segment.shape[1:])

    def encode_block(inputs):
        return encode(weights, inputs[0], inputs[1])
    return lax.map(jax.checkpoint(encode_block), (shaped, grouped)).reshape(tokens.shape)

def reference(question_rows, passage_rows, segment_lengths, positives, negatives, question_cotangent, passage_cotangent, loss_weight, projection, mixing, expand, shrink, biases, gains, widening):
    segment_ids, starts = layout(segment_lengths, LP)
    positions = jnp.arange(LP, dtype=jnp.int32)
    select = (positions[None, None, :] == starts[:, :, None]).astype(jnp.float32)
    question_block = math.gcd(NQ, max(4096 // LQ, 1))
    passage_block = math.gcd(NPR, max(4096 // LP, 1))
    question_segment = jnp.zeros((NQ, LQ), jnp.int32)
    bank_rows = negatives.astype(jnp.float32)
    column_ids = jnp.arange(NPASS + NBANK, dtype=jnp.int32)
    chosen_mask = (positives[:, None] == column_ids[None, :]).astype(jnp.float32)
    tile_scale = 2.0 / math.sqrt(D)

    def forward(question_in, passage_in, weights):
        question_weights = tuple((member[0] for member in weights))
        passage_weights = tuple((member[1] for member in weights))
        question_out = run_encoder(question_weights, question_in, question_segment, question_block)
        passage_out = run_encoder(passage_weights, passage_in, segment_ids, passage_block)
        question_cls = low(question_out[:, 0, :])
        passage_cls = low(jnp.einsum('rsl,rld->rsd', select, passage_out, precision=highest).reshape(NPASS, D))
        columns = jnp.concatenate([passage_cls, bank_rows], axis=0)
        scores = low_back(matmul(question_cls, columns.T) * tile_scale)
        highest_score = lax.optimization_barrier(jnp.max(scores, axis=1, keepdims=True))
        logsum = highest_score[:, 0] + jnp.log(lax.optimization_barrier(jnp.sum(jnp.exp(scores - highest_score), axis=1)))
        losses = logsum - lax.optimization_barrier(jnp.sum(scores * chosen_mask, axis=1))
        return (question_out, passage_out, losses)
    weights = tuple((member.astype(jnp.float32) for member in (projection, mixing, expand, shrink, biases, gains, widening)))
    question_in = question_rows.astype(jnp.float32)
    passage_in = passage_rows.astype(jnp.float32)
    outputs, pullback = jax.vjp(forward, question_in, passage_in, weights)
    question_out, passage_out, losses = outputs
    question_grad, passage_grad, weight_grads = pullback((question_cotangent.astype(jnp.float32), passage_cotangent.astype(jnp.float32), loss_weight))
    return (question_out.astype(jnp.bfloat16), passage_out.astype(jnp.bfloat16), losses, question_grad, passage_grad, weight_grads[0], weight_grads[1], weight_grads[2], weight_grads[3], weight_grads[4], weight_grads[5], weight_grads[6])
```

```python
from functools import partial
import math

import jax
import jax.numpy as jnp
from jax import lax
from jax.experimental import pallas as pl
from jax.experimental.pallas import tpu as pltpu
from jax.sharding import PartitionSpec as P

HEADS = 12
HEAD_DIM = 64


eps_norm = 1e-12
masked_score = -1000000000.0
highest = lax.Precision.HIGHEST


def matmul(left_side, right_side):
    return jnp.dot(left_side, right_side, preferred_element_type=jnp.float32)


def contract_rows(left_side, right_side):
    return lax.dot_general(
        left_side, right_side, (((0,), (0,)), ((), ())), preferred_element_type=jnp.float32
    )


def contract_cols(left_side, right_side):
    return lax.dot_general(
        left_side, right_side, (((1,), (1,)), ((), ())), preferred_element_type=jnp.float32
    )


def layout(lengths, length):
    segment_ends = jnp.cumsum(lengths, axis=-1, dtype=jnp.int32)
    starts = segment_ends - lengths
    positions = jnp.arange(length, dtype=jnp.int32)
    segment = jnp.sum(
        (positions[None, :, None] >= segment_ends[:, None, :]).astype(jnp.int32),
        axis=-1,
        dtype=jnp.int32,
    )
    return (segment, starts)


def norm_forward(total_in, gain_row, shift_row):
    centre = total_in - jnp.mean(total_in, axis=-1, keepdims=True)
    inverse = lax.rsqrt(jnp.mean(centre * centre, axis=-1, keepdims=True) + eps_norm)
    normal = centre * inverse
    return (normal * gain_row + shift_row, normal, inverse)


def norm_backward(gradient, normal, inverse, gain_row):
    gain_grad = jnp.sum(gradient * normal, axis=0)
    shift_grad = jnp.sum(gradient, axis=0)
    scaled = gradient * gain_row
    inner_mean = jnp.mean(scaled, axis=-1, keepdims=True)
    projected = jnp.mean(scaled * normal, axis=-1, keepdims=True)
    return (inverse * (scaled - inner_mean - normal * projected), gain_grad, shift_grad)


def attention_scores(queries, key_heads, segment):
    scores = jnp.einsum(
        "rqhd,rkhd->rhqk", queries, key_heads, preferred_element_type=jnp.float32
    ) * HEAD_DIM ** (-0.5)
    allowed = segment[:, None, :, None] == segment[:, None, None, :]
    return jnp.where(allowed, scores, masked_score)


def encode_forward(weights, tokens, segment):
    projection, mixing, expand, shrink, biases, gains, widening = weights
    row_count, length, features = tokens.shape
    flattened = tokens.reshape(row_count * length, features)
    shifts = biases.astype(jnp.float32)
    gain_rows = gains.astype(jnp.float32)
    packed_bias = jnp.concatenate([shifts[0], jnp.zeros_like(shifts[0]), shifts[1]])
    packed = (matmul(flattened, projection) + packed_bias).astype(jnp.bfloat16)
    head_split = packed.reshape(row_count, length, 3, HEADS, HEAD_DIM)
    scores = attention_scores(head_split[:, :, 0], head_split[:, :, 1], segment)
    row_top = jnp.max(scores, axis=-1, keepdims=True)
    logsum = row_top + jnp.log(jnp.sum(jnp.exp(scores - row_top), axis=-1, keepdims=True))
    attention = jnp.exp(scores - logsum).astype(jnp.bfloat16)
    context = jnp.einsum(
        "rhqk,rkhd->rqhd", attention, head_split[:, :, 2], preferred_element_type=jnp.float32
    )
    context = context.reshape(row_count * length, features).astype(jnp.bfloat16)
    branch = matmul(context, mixing) + shifts[2]
    first_out, first_normal, first_inverse = norm_forward(
        flattened.astype(jnp.float32) + branch, gain_rows[0], shifts[3]
    )
    first_low = first_out.astype(jnp.bfloat16)
    hidden = matmul(first_low, expand) + widening.astype(jnp.float32)
    active = jax.nn.gelu(hidden, approximate=False).astype(jnp.bfloat16)
    second = matmul(active, shrink) + shifts[4]
    final_out, final_normal, final_inverse = norm_forward(
        first_out + second, gain_rows[1], shifts[5]
    )
    saved_state = (
        flattened,
        packed,
        logsum,
        context,
        first_normal,
        first_inverse,
        first_low,
        hidden,
        active,
        final_normal,
        final_inverse,
    )
    return (final_out.reshape(row_count, length, features), saved_state)


def encode_backward(weights, segment, saved_state, final_grad):
    projection, mixing, expand, shrink, biases, gains, widening = weights
    (
        flattened,
        packed,
        logsum,
        context,
        first_normal,
        first_inverse,
        first_low,
        hidden,
        active,
        final_normal,
        final_inverse,
    ) = saved_state
    row_count, length = segment.shape
    features = flattened.shape[1]
    gain_rows = gains.astype(jnp.float32)
    total_grad, final_gain, final_shift = norm_backward(
        final_grad, final_normal, final_inverse, gain_rows[1]
    )
    second_low = total_grad.astype(jnp.bfloat16)
    shrink_bias = jnp.sum(second_low.astype(jnp.float32), axis=0)
    active_grad = contract_cols(second_low, shrink)
    gelu_back = jax.vjp(partial(jax.nn.gelu, approximate=False), hidden)[1]
    hidden_low = gelu_back(active_grad)[0].astype(jnp.bfloat16)
    widening_grad = jnp.sum(hidden_low.astype(jnp.float32), axis=0)
    first_grad = total_grad + contract_cols(hidden_low, expand)
    branch_grad, first_gain, first_shift = norm_backward(
        first_grad, first_normal, first_inverse, gain_rows[0]
    )
    branch_low = branch_grad.astype(jnp.bfloat16)
    mixing_bias = jnp.sum(branch_low.astype(jnp.float32), axis=0)
    context_low = (
        contract_cols(branch_low, mixing)
        .astype(jnp.bfloat16)
        .reshape(row_count, length, HEADS, HEAD_DIM)
    )
    head_split = packed.reshape(row_count, length, 3, HEADS, HEAD_DIM)
    scores = attention_scores(head_split[:, :, 0], head_split[:, :, 1], segment)
    attention = jnp.exp(scores - logsum)
    attention_low = attention.astype(jnp.bfloat16)
    weight_grad = jnp.einsum(
        "rqhd,rkhd->rhqk", context_low, head_split[:, :, 2], preferred_element_type=jnp.float32
    )
    value_grad = jnp.einsum(
        "rhqk,rqhd->rkhd", attention_low, context_low, preferred_element_type=jnp.float32
    )
    score_grad = attention * (
        weight_grad - jnp.sum(attention * weight_grad, axis=-1, keepdims=True)
    )
    score_low = score_grad.astype(jnp.bfloat16)
    query_grad = jnp.einsum(
        "rhqk,rkhd->rqhd", score_low, head_split[:, :, 1], preferred_element_type=jnp.float32
    ) * HEAD_DIM ** (-0.5)
    key_grad = jnp.einsum(
        "rhqk,rqhd->rkhd", score_low, head_split[:, :, 0], preferred_element_type=jnp.float32
    ) * HEAD_DIM ** (-0.5)
    packed_grad = (
        jnp.stack([query_grad, key_grad, value_grad], axis=2)
        .astype(jnp.bfloat16)
        .reshape(row_count * length, 3 * features)
    )
    packed_sum = jnp.sum(packed_grad.astype(jnp.float32), axis=0)
    input_grad = branch_grad + contract_cols(packed_grad, projection)
    small = jnp.stack(
        [
            packed_sum[:features],
            packed_sum[2 * features :],
            mixing_bias,
            first_shift,
            shrink_bias,
            final_shift,
            first_gain,
            final_gain,
        ]
    )
    small = jnp.concatenate([small, widening_grad.reshape(-1, features)])
    operands = (
        active, second_low, first_low, hidden_low, flattened, packed_grad, context, branch_low
    )
    weight_grads = (operands, small)
    return (input_grad.reshape(row_count, length, features), weight_grads)


panel_rows = 48
chunk_panels = 8
encoder_chunks = 9
lane = 128
MESH = pl.DeviceIdType.MESH


def reduce_kernel(
    tokens,
    q_active, q_second, q_first, q_hidden, q_rows, q_packed, q_context, q_branch,
    p_active, p_second, p_first, p_hidden, p_rows, p_packed, p_context, p_branch,
    small_ref,
    out_ref, small_out,
    keep, core_send, core_recv, recv_x, recv_ya, recv_za, recv_yb, recv_zb, fin_a, fin_b,
    left_buf, left_t, right_buf, product, small_recv, small_sum,
    load_sem, core_ss, core_rs, xa_ss, xa_rs, ya_ss, ya_rs, za_ss, za_rs, ag_ss, ag_rs,
    yb_ss, yb_rs, zb_ss, zb_rs, xb_ss, xb_rs, small_ss, small_rs, credit,
):
    chunks = 2 * encoder_chunks
    pb, pa = lax.axis_index("pb"), lax.axis_index("pa")
    core, y, z, x = pa % 2, pa // 2 % 2, pa // 4, pb
    at_core = (pb, pa + 1 - 2 * core)
    at_y = (pb, pa + 2 - 4 * y)
    at_x = (1 - pb, pa)
    far_z = [(z + d) % 4 for d in (1, 2, 3)]
    at_z = [(pb, t * 4 + y * 2 + core) for t in far_z]

    barrier = pltpu.get_barrier_semaphore()
    for device in [at_core, at_y, at_x] + at_z:
        pl.semaphore_signal(barrier, inc=1, device_id=device, device_id_type=MESH)
    pl.semaphore_wait(barrier, 6)

    def remote(src, dst, ss, rs, device):
        return pltpu.make_async_remote_copy(
            src_ref=src, dst_ref=dst, send_sem=ss, recv_sem=rs, device_id=device, device_id_type=MESH
        )

    def copy_core(c):
        return remote(core_send.at[c % 2], core_recv.at[c % 3], core_ss.at[c], core_rs.at[c], at_core)

    def copy_xa(c):
        return remote(keep.at[c, pl.ds(2 * (1 - x), 2)], recv_x.at[c], xa_ss.at[c], xa_rs.at[c], at_x)

    def copy_ya(c):
        return remote(
            keep.at[c, pl.ds(2 * x, 2), :, 1 - y], recv_ya.at[c], ya_ss.at[c], ya_rs.at[c], at_y
        )

    def copy_za(c, d):
        return remote(
            keep.at[c, pl.ds(2 * x, 2), far_z[d], y], recv_za.at[c, d], za_ss.at[c, d], za_rs.at[c, d], at_z[d]
        )

    def copy_ag(c):
        half = fin_a.at[c, pl.ds(2 * x, 2)]
        return remote(half, half, ag_ss.at[c], ag_rs.at[c], at_x)

    def copy_yb(c):
        return remote(keep.at[c, pl.ds(4, 4), :, 1 - y], recv_yb.at[c], yb_ss.at[c], yb_rs.at[c], at_y)

    def copy_zb(c, d):
        return remote(
            keep.at[c, pl.ds(4, 4), far_z[d], y], recv_zb.at[c, d], zb_ss.at[c, d], zb_rs.at[c, d], at_z[d]
        )

    def copy_xb(c):
        return remote(fin_b.at[c, x], fin_b.at[c, x], xb_ss.at[c], xb_rs.at[c], at_x)

    def small_copy(stage, device):
        source = small_sum.at[max(stage - 3, 0) if stage >= 3 else stage]
        return remote(source, small_recv.at[stage], small_ss.at[stage], small_rs.at[stage], device)

    sources = (
        (q_active, q_second, q_first, q_hidden, q_rows, q_packed, q_context, q_branch),
        (p_active, p_second, p_first, p_hidden, p_rows, p_packed, p_context, p_branch),
    )

    def left_loads(e, part):
        active, second, first, hidden, rows, packed, context, branch = sources[e]
        count = tokens[e]
        features = rows.shape[1]
        if part == 0:
            pairs = [(active, 0)]
        elif part == 1:
            pairs = [(first, 0)]
        else:
            pairs = [(rows, 0), (context, features)]
        return [
            pltpu.make_async_copy(
                ref,
                left_buf.at[pl.ds(0, count), pl.ds(at, ref.shape[1])],
                load_sem.at[2 + i],
            )
            for i, (ref, at) in enumerate(pairs)
        ]

    def right_loads(e, k):
        active, second, first, hidden, rows, packed, context, branch = sources[e]
        count = tokens[e]
        slot = (e * encoder_chunks + k) % 2
        if k < 3:
            pairs = [(second, 256 * k, 256, 0)]
        elif k < 6:
            pairs = [(hidden, 1024 * (k - 3), 1024, 0)]
        elif k < 8:
            pairs = [(packed, 1024 * (k - 6), 1024, 0)]
        else:
            pairs = [(packed, 2048, 256, 0), (branch, 0, 768, 256)]
        return [
            pltpu.make_async_copy(
                ref.at[:, pl.ds(start, width)],
                right_buf.at[slot, pl.ds(0, count), pl.ds(at, width)],
                load_sem.at[slot] if i == 0 else load_sem.at[4],
            )
            for i, (ref, start, width, at) in enumerate(pairs)
        ]

    def begin(copies):
        for copy in copies:
            copy.start()

    def finish(copies):
        for copy in copies:
            copy.wait()

    def transpose_left(e, part):
        count = tokens[e]
        width = (3072, 768, 1536)[part]

        def step(i, carry):
            at = pl.multiple_of(i * 256, 256)
            left_t[pl.ds(at, 256), pl.ds(0, count)] = left_buf[pl.ds(0, count), pl.ds(at, 256)].T
            return carry

        lax.fori_loop(0, width // 256, step, 0)

    def compute(e, k):
        count = tokens[e]
        c = e * encoder_chunks + k
        slot = c % 2

        def step(q, carry):
            if k < 3:
                rows_at, columns_at = q * 768, 0
            elif k < 8:
                rows_at, columns_at = 0, q * 256
            else:
                rows_at, columns_at = jnp.where(q > 0, 768, 0), q * 256
            rows_at = pl.multiple_of(rows_at, 256)
            columns_at = pl.multiple_of(columns_at, 256)
            product[...] = jnp.dot(
                left_t[pl.ds(rows_at, 768), pl.ds(0, count)],
                right_buf[slot, pl.ds(0, count), pl.ds(columns_at, 256)],
                preferred_element_type=jnp.float32,
            )
            if k < 3:
                for iy in range(2):
                    for sub in range(4):
                        for which, target in ((core, keep.at[c]), (1 - core, core_send.at[slot])):
                            at = pl.multiple_of((2 * iy + which) * 192 + sub * 48, 16)
                            block = product[pl.ds(at, 48), :].astype(jnp.bfloat16)
                            target[sub * 2, q, iy] = block[:, :lane]
                            target[sub * 2 + 1, q, iy] = block[:, lane:]
            else:
                for iz in range(4):
                    for iy in range(2):
                        for which, target in ((core, keep.at[c]), (1 - core, core_send.at[slot])):
                            at = pl.multiple_of((4 * iz + 2 * iy + which) * 48, 16)
                            block = product[pl.ds(at, 48), :].astype(jnp.bfloat16)
                            target[2 * q, iz, iy] = block[:, :lane]
                            target[2 * q + 1, iz, iy] = block[:, lane:]
            return carry

        lax.fori_loop(0, 4, step, 0)

    order = [(e, k) for e in range(2) for k in range(encoder_chunks)]
    part_of = lambda k: 0 if k < 3 else 1 if k < 6 else 2

    def produce(c):
        e, k = order[c]
        if c >= 2:
            copy_core(c - 2).wait_send()
        if k % 3 == 0:
            finish(left_loads(e, part_of(k)))
            transpose_left(e, part_of(k))
            if c + 3 < chunks:
                e2, k2 = order[c + 3]
                begin(left_loads(e2, part_of(k2)))
        finish(right_loads(e, k))
        if c + 1 < chunks:
            begin(right_loads(*order[c + 1]))
        compute(e, k)
        if c >= 3:
            pl.semaphore_wait(credit, 1)
        copy_core(c).start()

    def after_core(c):
        copy_core(c).wait_recv()

        def step(p, carry):
            keep[c, p] = keep[c, p] + core_recv[c % 3, p]
            return carry

        lax.fori_loop(0, chunk_panels, step, 0)
        copy_xa(c).start()
        copy_yb(c).start()

        @pl.when(c < chunks - 3)
        def _():
            pl.semaphore_signal(credit, inc=1, device_id=at_core, device_id_type=MESH)

    def after_first(c):
        copy_yb(c).wait_recv()

        def step_b(p, carry):
            for iz in range(4):
                keep[c, 4 + p, iz, y] = keep[c, 4 + p, iz, y] + recv_yb[c, p, iz]
            return carry

        lax.fori_loop(0, 4, step_b, 0)
        for d in range(3):
            copy_zb(c, d).start()
        copy_xa(c).wait_recv()

        def step_a(p, carry):
            keep[c, 2 * x + p] = keep[c, 2 * x + p] + recv_x[c, p]
            return carry

        lax.fori_loop(0, 2, step_a, 0)
        copy_ya(c).start()

    def widen(value):
        return value.astype(jnp.float32)

    def after_second(c):
        copy_ya(c).wait_recv()

        def step_a(p, carry):
            for iz in range(4):
                keep[c, 2 * x + p, iz, y] = keep[c, 2 * x + p, iz, y] + recv_ya[c, p, iz]
            return carry

        lax.fori_loop(0, 2, step_a, 0)
        for d in range(3):
            copy_za(c, d).start()
        for d in range(3):
            copy_zb(c, d).wait_recv()

        def step_b(p, carry):
            fin_b[c, x, p] = (
                widen(keep[c, 4 + p, z, y])
                + widen(recv_zb[c, 0, p])
                + widen(recv_zb[c, 1, p])
                + widen(recv_zb[c, 2, p])
            ).astype(jnp.bfloat16)
            return carry

        lax.fori_loop(0, 4, step_b, 0)
        copy_xb(c).start()

    def after_third(c):
        for d in range(3):
            copy_za(c, d).wait_recv()

        def step_a(p, carry):
            fin_a[c, 2 * x + p] = (
                widen(keep[c, 2 * x + p, z, y])
                + widen(recv_za[c, 0, p])
                + widen(recv_za[c, 1, p])
                + widen(recv_za[c, 2, p])
            ).astype(jnp.bfloat16)
            return carry

        lax.fori_loop(0, 2, step_a, 0)
        copy_ag(c).start()
        copy_xb(c).wait_recv()

        def step_b(p, carry):
            out_ref[c, 4 + p] = widen(fin_b[c, 0, p]) + widen(fin_b[c, 1, p])
            return carry

        lax.fori_loop(0, 4, step_b, 0)

    def after_last(c):
        copy_ag(c).wait_recv()

        def step(p, carry):
            out_ref[c, p] = widen(fin_a[c, p])
            return carry

        lax.fori_loop(0, 4, step, 0)

    begin(left_loads(0, 0))
    begin(right_loads(0, 0))
    small_sum[0] = small_ref[...]
    small_copy(0, at_core).start()
    for c in range(chunks + 5):
        if c < chunks:
            produce(c)
        if 0 <= c - 1 < chunks:
            after_core(c - 1)
        if 0 <= c - 2 < chunks:
            after_first(c - 2)
        if 0 <= c - 3 < chunks:
            after_second(c - 3)
        if 0 <= c - 4 < chunks:
            after_third(c - 4)
        if 0 <= c - 5 < chunks:
            after_last(c - 5)
        if c == 1:
            small_copy(0, at_core).wait_recv()
            small_sum[1] = small_sum[0] + small_recv[0]
            small_copy(1, at_x).start()
        if c == 2:
            small_copy(1, at_x).wait_recv()
            small_sum[2] = small_sum[1] + small_recv[1]
            small_copy(2, at_y).start()
        if c == 3:
            small_copy(2, at_y).wait_recv()
            small_sum[3] = small_sum[2] + small_recv[2]
            for d in range(3):
                remote(small_sum.at[3], small_recv.at[3 + d], small_ss.at[3 + d], small_rs.at[3 + d], at_z[d]).start()
        if c == 4:
            for d in range(3):
                remote(small_sum.at[3], small_recv.at[3 + d], small_ss.at[3 + d], small_rs.at[3 + d], at_z[d]).wait_recv()
            result = jnp.zeros_like(small_ref)
            for iz in range(4):
                back = (z - iz + 4) % 4
                value = jnp.where(back == 0, small_sum[3], 0.0)
                for d in range(3):
                    value = jnp.where(back == d + 1, small_recv[3 + d], value)
                result = result + value
            small_out[...] = result

    copy_core(chunks - 2).wait_send()
    copy_core(chunks - 1).wait_send()

    def drain(c, carry):
        copy_xa(c).wait_send()
        copy_ya(c).wait_send()
        copy_ag(c).wait_send()
        copy_yb(c).wait_send()
        copy_xb(c).wait_send()
        for d in range(3):
            copy_za(c, d).wait_send()
            copy_zb(c, d).wait_send()
        return carry

    lax.fori_loop(0, chunks, drain, 0)
    small_copy(0, at_core).wait_send()
    small_copy(1, at_x).wait_send()
    small_copy(2, at_y).wait_send()
    for d in range(3):
        remote(small_sum.at[3], small_recv.at[3 + d], small_ss.at[3 + d], small_rs.at[3 + d], at_z[d]).wait_send()


def reduce_by_kernel(question, passage, small):
    tokens = (question[0].shape[0], passage[0].shape[0])
    most = max(tokens)
    chunks = 2 * encoder_chunks
    tile = (panel_rows, lane)
    low = jnp.bfloat16
    dma = pltpu.SemaphoreType.DMA
    one, three = dma((chunks,)), dma((chunks, 3))
    raw, small_total = pl.pallas_call(
        partial(reduce_kernel, tokens),
        out_shape=[
            jax.ShapeDtypeStruct((chunks, chunk_panels) + tile, jnp.float32),
            jax.ShapeDtypeStruct(small.shape, jnp.float32),
        ],
        in_specs=[pl.BlockSpec(memory_space=pl.ANY)] * 16 + [pl.BlockSpec(memory_space=pltpu.VMEM)],
        out_specs=[pl.BlockSpec(memory_space=pltpu.VMEM)] * 2,
        scratch_shapes=[
            pltpu.VMEM((chunks, chunk_panels, 4, 2) + tile, low),
            pltpu.VMEM((2, chunk_panels, 4, 2) + tile, low),
            pltpu.VMEM((3, chunk_panels, 4, 2) + tile, low),
            pltpu.VMEM((chunks, 2, 4, 2) + tile, low),
            pltpu.VMEM((chunks, 2, 4) + tile, low),
            pltpu.VMEM((chunks, 3, 2) + tile, low),
            pltpu.VMEM((chunks, 4, 4) + tile, low),
            pltpu.VMEM((chunks, 3, 4) + tile, low),
            pltpu.VMEM((chunks, 4) + tile, low),
            pltpu.VMEM((chunks, 2, 4) + tile, low),
            pltpu.VMEM((most, 3072), low),
            pltpu.VMEM((3072, most), low),
            pltpu.VMEM((2, most, 1024), low),
            pltpu.VMEM((768, 256), jnp.float32),
            pltpu.VMEM((6,) + small.shape, jnp.float32),
            pltpu.VMEM((4,) + small.shape, jnp.float32),
            dma((5,)),
            one, one, one, one, one, one, three, three, one, one,
            one, one, three, three, one, one, dma((6,)), dma((6,)),
            pltpu.SemaphoreType.REGULAR,
        ],
        compiler_params=pltpu.CompilerParams(
            collective_id=1, has_side_effects=True, vmem_limit_bytes=63 * 1024 * 1024
        ),
        cost_estimate=pl.CostEstimate(flops=22 * 10**9, bytes_accessed=60 * 10**6, transcendentals=0),
    )(*question, *passage, small)
    raw = raw.reshape(2, encoder_chunks, chunk_panels, panel_rows, lane)
    shrink = raw[:, :3].reshape(2, 3, 4, 2, 48, lane).transpose(0, 2, 4, 1, 3, 5).reshape(2, 192, 768)
    expand = raw[:, 3:6].transpose(0, 3, 1, 2, 4).reshape(2, 48, 3072)
    rest = raw[:, 6:].transpose(0, 3, 1, 2, 4).reshape(2, 48, 3072)
    return rest[:, :, :2304], rest[:, :, 2304:], expand, shrink, small_total


def share_gradients(question_side, passage_side):
    size_pa, size_pb = lax.axis_size("pa"), lax.axis_size("pb")
    operands, small = zip(question_side, passage_side)
    features = operands[0][4].shape[1]
    if size_pa == 16 and size_pb == 2:
        projection, mixing, expand, shrink, small = reduce_by_kernel(
            operands[0], operands[1], jnp.concatenate(small)
        )
        small = small.reshape(2, -1, features)
    else:
        products = []
        for e in range(2):
            active, second, first, hidden, rows, packed, context, branch = operands[e]
            products.append(
                [
                    contract_rows(*pair)
                    for pair in ((rows, packed), (context, branch), (first, hidden), (active, second))
                ]
            )
        projection, mixing, expand, shrink = (
            lax.psum(
                jnp.stack(
                    [
                        lax.psum_scatter(products[e][i], "pa", scatter_dimension=0, tiled=True)
                        for e in range(2)
                    ]
                ),
                "pb",
            )
            for i in range(4)
        )
        small = lax.psum(jnp.stack(small), ("pb", "pa"))
    mine = lax.axis_index("pa")
    share = features // size_pa
    columns = lax.dynamic_slice_in_dim(small[:, :8], mine * share, share, 2)
    widening = small[:, 8:].reshape(2, -1)
    wide = widening.shape[1] // size_pa
    widening = lax.dynamic_slice_in_dim(widening, mine * wide, wide, 1)
    return (projection, mixing, expand, shrink, columns[:, :6], columns[:, 6:], widening)


def body(
    question_rows,
    passage_rows,
    segment_lengths,
    positives,
    negatives,
    question_cotangent,
    passage_cotangent,
    loss_weight,
    projection,
    mixing,
    expand,
    shrink,
    biases,
    gains,
    widening,
):
    stacked = (projection, mixing, expand, shrink, biases, gains, widening)
    question_weights = tuple((member[0] for member in stacked))
    passage_weights = tuple((member[1] for member in stacked))
    question_count, question_length, features = question_rows.shape
    passage_count, passage_length = (passage_rows.shape[0], passage_rows.shape[1])
    packed_count = segment_lengths.shape[1]
    segment_ids, starts = layout(segment_lengths, passage_length)
    question_segment = jnp.zeros((question_count, question_length), jnp.int32)
    question_final, question_saved = encode_forward(
        question_weights, question_rows, question_segment
    )
    passage_final, passage_saved = encode_forward(passage_weights, passage_rows, segment_ids)
    positions = jnp.arange(passage_length, dtype=jnp.int32)
    select = (positions[None, None, :] == starts[:, :, None]).astype(jnp.float32)
    question_cls = question_final[:, 0, :].astype(jnp.bfloat16)
    passage_cls = (
        jnp.einsum("rsl,rld->rsd", select, passage_final, precision=highest)
        .reshape(passage_count * packed_count, features)
        .astype(jnp.bfloat16)
    )
    row_block = lax.all_gather(question_cls, "pa", axis=0, tiled=True)
    col_block = lax.all_gather(passage_cls, "pb", axis=0, tiled=True)
    columns = jnp.concatenate([col_block, negatives], axis=0)
    tile_scale = 2.0 / math.sqrt(features)
    scores = contract_cols(row_block, columns) * tile_scale
    per_device = passage_cls.shape[0]
    passage_columns = col_block.shape[0]
    column_ids = jnp.arange(passage_columns, dtype=jnp.int32)
    owner_index = column_ids // per_device
    global_ids = (
        owner_index * lax.axis_size("pa") + lax.axis_index("pa")
    ) * per_device + column_ids % per_device
    chosen_mask = jnp.concatenate(
        [
            (positives[:, None] == global_ids[None, :]).astype(jnp.float32),
            jnp.zeros((row_block.shape[0], negatives.shape[0]), jnp.float32),
        ],
        axis=1,
    )
    row_top = jnp.max(scores, axis=1)
    exp_total = jnp.sum(jnp.exp(scores - row_top[:, None]), axis=1)
    chosen = jnp.sum(scores * chosen_mask, axis=1)
    global_top = lax.pmax(row_top, "pa")
    exp_total, chosen = lax.psum((exp_total * jnp.exp(row_top - global_top), chosen), "pa")
    row_top = global_top
    logsum = row_top + jnp.log(exp_total)
    question_loss = logsum - chosen
    tile_grad = (loss_weight[:, None] * (jnp.exp(scores - logsum[:, None]) - chosen_mask)).astype(
        jnp.bfloat16
    )
    row_terms = matmul(tile_grad, columns) * tile_scale
    row_mine = lax.psum_scatter(row_terms, "pa", scatter_dimension=0, tiled=True)
    col_terms = contract_rows(tile_grad[:, :passage_columns], row_block) * tile_scale
    col_mine = lax.psum_scatter(col_terms, "pb", scatter_dimension=0, tiled=True)
    question_positions = jnp.arange(question_length, dtype=jnp.int32)
    question_in_grad = question_cotangent.astype(jnp.float32) + jnp.where(
        question_positions[None, :, None] == 0, row_mine[:, None, :], 0.0
    )
    passage_in_grad = passage_cotangent.astype(jnp.float32) + jnp.einsum(
        "rsl,rsd->rld",
        select,
        col_mine.reshape(passage_count, packed_count, features),
        precision=highest,
    )
    question_grad, question_weight_grads = encode_backward(
        question_weights,
        question_segment,
        question_saved,
        question_in_grad.reshape(question_count * question_length, features),
    )
    passage_grad, passage_weight_grads = encode_backward(
        passage_weights,
        segment_ids,
        passage_saved,
        passage_in_grad.reshape(passage_count * passage_length, features),
    )
    totals = share_gradients(question_weight_grads, passage_weight_grads)
    return (
        question_final.astype(jnp.bfloat16),
        passage_final.astype(jnp.bfloat16),
        question_loss,
        question_grad,
        passage_grad,
        totals[0],
        totals[1],
        totals[2],
        totals[3],
        totals[4],
        totals[5],
        totals[6],
    )


def solution(mesh):
    return jax.shard_map(
        body,
        mesh=mesh,
        in_specs=(
            P(("pb", "pa"), None, None),
            P(("pb", "pa"), None, None),
            P(("pb", "pa"), None),
            P("pb"),
            P("pa", None),
            P(("pb", "pa"), None, None),
            P(("pb", "pa"), None, None),
            P("pb"),
            P(),
            P(),
            P(),
            P(),
            P(),
            P(),
            P(),
        ),
        out_specs=(
            P(("pb", "pa"), None, None),
            P(("pb", "pa"), None, None),
            P("pb"),
            P(("pb", "pa"), None, None),
            P(("pb", "pa"), None, None),
            P(None, "pa", None),
            P(None, "pa", None),
            P(None, "pa", None),
            P(None, "pa", None),
            P(None, None, "pa"),
            P(None, None, "pa"),
            P(None, "pa"),
        ),
        check_vma=False,
    )
```

```python
from functools import partial
import math

import jax
import jax.numpy as jnp
from jax import lax
from jax.experimental import pallas as pl
from jax.experimental.pallas import tpu as pltpu
from jax.sharding import PartitionSpec as P

HEADS = 12
HEAD_DIM = 64


eps_norm = 1e-12
masked_score = -1000000000.0


def matmul(left_side, right_side):
    return jnp.dot(left_side, right_side, preferred_element_type=jnp.float32)


def contract_rows(left_side, right_side):
    return lax.dot_general(
        left_side, right_side, (((0,), (0,)), ((), ())), preferred_element_type=jnp.float32
    )


def contract_cols(left_side, right_side):
    return lax.dot_general(
        left_side, right_side, (((1,), (1,)), ((), ())), preferred_element_type=jnp.float32
    )


lane = 128
block_tokens = 256
cls_slots = 4
stat_first, stat_final = HEADS, HEADS + 1
vmem_bytes = 63 * 1024 * 1024


def dot_nn(left_side, right_side):
    return jnp.dot(left_side, right_side, preferred_element_type=jnp.float32)


def dot_nt(left_side, right_side):
    return lax.dot_general(
        left_side, right_side, (((1,), (1,)), ((), ())), preferred_element_type=jnp.float32
    )


def dot_tn(left_side, right_side):
    return lax.dot_general(
        left_side, right_side, (((0,), (0,)), ((), ())), preferred_element_type=jnp.float32
    )


def gelu_and_slope(hidden):
    size = jnp.abs(hidden)
    t = 1.0 / (1.0 + (0.3275911 * math.sqrt(0.5)) * size)
    bell = jnp.exp(-0.5 * hidden * hidden)
    tail = 1.061405429 * t - 1.453152027
    tail = tail * t + 1.421413741
    tail = tail * t - 0.284496736
    tail = (tail * t + 0.254829592) * (0.5 * t) * bell
    below = jnp.where(hidden < 0.0, tail, 1.0 - tail)
    return hidden * below, below + hidden * bell * (1.0 / math.sqrt(2.0 * math.pi))


def normalize(values):
    centre = values - jnp.mean(values, axis=-1, keepdims=True)
    inverse = lax.rsqrt(jnp.mean(centre * centre, axis=-1, keepdims=True) + eps_norm)
    return centre * inverse, inverse


def normalize_back(gradient, normal, inverse, gain_row):
    scaled = gradient * gain_row
    inner_mean = jnp.mean(scaled, axis=-1, keepdims=True)
    projected = jnp.mean(scaled * normal, axis=-1, keepdims=True)
    return inverse * (scaled - inner_mean - normal * projected)


class Weights:
    def __init__(self, sources, buffers, sems, step, first_passage, order):
        self.sources, self.buffers, self.sems, self.order = sources, buffers, sems, order
        self.step, self.first_passage = step, first_passage
        self.encoder = (step >= first_passage).astype(jnp.int32)

    def copy(self, which, e):
        return pltpu.make_async_copy(
            self.sources[which].at[e], self.buffers[which].at[e], self.sems.at[which, e]
        )

    def begin(self):
        @pl.when(self.step == 0)
        def _():
            for e in range(2):
                for which in self.order:
                    self.copy(which, e).start()

    def get(self, which):
        for e, at in ((0, 0), (1, self.first_passage)):

            @pl.when(self.step == at)
            def _():
                self.copy(which, e).wait()

        return self.buffers[which].at[self.encoder]


def forward_kernel(
    first_passage,
    starts,
    q_rows, p_rows, projection, mixing, expand, shrink, biases, gains, widening,
    q_states, p_states, cls, chances, stats, packed_ref, context_ref, first_ref, n1_ref, n2_ref,
    active_ref, slope_ref,
    w0, w1, w2, w3, sems, final_buf, x_buf,
):
    i = pl.program_id(0)
    weights = Weights((projection, mixing, expand, shrink), (w0, w1, w2, w3), sems, i, first_passage, (0, 1, 2, 3))
    weights.begin()
    e = weights.encoder
    features = q_rows.shape[1]
    shifts = biases[e].astype(jnp.float32)
    gain_rows = gains[e].astype(jnp.float32)
    x_buf[...] = jnp.where(i < first_passage, q_rows[...], p_rows[...])

    weight = weights.get(0)
    x_low = x_buf[...]
    for part in range(3):
        columns = pl.ds(part * features, features)
        value = dot_nn(x_low, weight[:, columns])
        if part != 1:
            value = value + shifts[part // 2 : part // 2 + 1]
        packed_ref[:, columns] = value.astype(jnp.bfloat16)

    tokens = q_rows.shape[0]
    row_at = lax.broadcasted_iota(jnp.int32, (tokens, tokens), 0)
    col_at = lax.broadcasted_iota(jnp.int32, (tokens, tokens), 1)
    row_segment = jnp.zeros_like(row_at)
    col_segment = jnp.zeros_like(col_at)
    for k in range(1, cls_slots):
        row_segment = row_segment + (row_at >= starts[i, k]).astype(jnp.int32)
        col_segment = col_segment + (col_at >= starts[i, k]).astype(jnp.int32)
    penalty = jnp.where(row_segment == col_segment, 0.0, masked_score)
    lanes = lax.broadcasted_iota(jnp.int32, stats.shape, 1)
    stat = jnp.zeros(stats.shape, jnp.float32)
    for h in range(HEADS):
        part = lambda j: packed_ref[:, pl.ds(j * features + h * HEAD_DIM, HEAD_DIM)]
        queries = part(0) * jnp.asarray(HEAD_DIM ** (-0.5), jnp.bfloat16)
        scores = dot_nt(queries, part(1)) + penalty
        top = jnp.max(scores, axis=-1, keepdims=True)
        chance = jnp.exp(scores - top)
        inverse = 1.0 / jnp.sum(chance, axis=-1, keepdims=True)
        chance_low = chance.astype(jnp.bfloat16)
        chances[0, h] = chance_low
        stat = jnp.where(lanes == h, inverse, stat)
        mixed = dot_nn(chance_low, part(2)) * inverse
        context_ref[:, pl.ds(h * HEAD_DIM, HEAD_DIM)] = mixed.astype(jnp.bfloat16)

    weight = weights.get(1)
    branch = dot_nn(context_ref[...], weight[...]) + shifts[2:3]
    normal, inverse = normalize(x_buf[...].astype(jnp.float32) + branch)
    n1_ref[...] = normal.astype(jnp.bfloat16)
    stat = jnp.where(lanes == stat_first, inverse, stat)
    first = normal * gain_rows[0:1] + shifts[3:4]
    first_low = first.astype(jnp.bfloat16)
    first_ref[...] = first_low
    final_buf[...] = first

    up, down = weights.get(2), weights.get(3)
    second = jnp.broadcast_to(shifts[4:5], (tokens, features))
    for j in range(up.shape[1] // features):
        columns = pl.ds(j * features, features)
        hidden = dot_nn(first_low, up[:, columns]) + widening[e, :, columns].astype(jnp.float32)
        active, slope = gelu_and_slope(hidden)
        active_low = active.astype(jnp.bfloat16)
        active_ref[:, columns] = active_low
        slope_ref[:, columns] = slope.astype(jnp.bfloat16)
        second = second + dot_nn(active_low, down[columns, :])

    normal, inverse = normalize(final_buf[...] + second)
    n2_ref[...] = normal.astype(jnp.bfloat16)
    stats[...] = jnp.where(lanes == stat_final, inverse, stat)
    final = normal * gain_rows[1:2] + shifts[5:6]
    final_buf[...] = final

    @pl.when(i < first_passage)
    def _():
        q_states[...] = final.astype(jnp.bfloat16)

    @pl.when(i >= first_passage)
    def _():
        p_states[...] = final.astype(jnp.bfloat16)

    for k in range(cls_slots):
        at = jnp.minimum(starts[i, k], tokens - 1)
        cls[0, pl.ds(k, 1), :] = final_buf[pl.ds(at, 1), :]


def backward_kernel(
    first_passage,
    starts,
    q_cot, p_cot, cls_grad, chances, stats, packed_ref, context_ref, n1_ref, n2_ref, slope_ref,
    projection, mixing, expand, shrink, gains,
    q_grad, p_grad, second_ref, hidden_ref, branch_ref, packed_grad, small,
    w0, w1, w2, w3, sems, total_buf, context_grad,
):
    i = pl.program_id(0)
    weights = Weights((projection, mixing, expand, shrink), (w0, w1, w2, w3), sems, i, first_passage, (3, 2, 1, 0))
    weights.begin()
    e = weights.encoder
    tokens, features = q_cot.shape
    gain_rows = gains[e].astype(jnp.float32)

    @pl.when((i == 0) | (i == first_passage))
    def _():
        small[...] = jnp.zeros_like(small)

    def add_small(row, value):
        small[0, pl.ds(row, 1), :] += jnp.sum(value, axis=0, keepdims=True)

    gradient = jnp.where(i < first_passage, q_cot[...], p_cot[...]).astype(jnp.float32)
    row_at = lax.broadcasted_iota(jnp.int32, (tokens, 1), 0)
    for k in range(cls_slots):
        gradient = gradient + jnp.where(row_at == starts[i, k], cls_grad[0, pl.ds(k, 1), :], 0.0)
    normal = n2_ref[...].astype(jnp.float32)
    add_small(5, gradient)
    add_small(7, gradient * normal)
    total_grad = normalize_back(
        gradient, normal, stats[:, stat_final : stat_final + 1], gain_rows[1:2]
    )
    total_buf[...] = total_grad
    second_low = total_grad.astype(jnp.bfloat16)
    second_ref[...] = second_low
    add_small(4, second_low.astype(jnp.float32))

    down, up = weights.get(3), weights.get(2)
    first_grad = total_buf[...]
    for j in range(up.shape[1] // features):
        columns = pl.ds(j * features, features)
        hidden_grad = dot_nt(second_low, down[columns, :]) * slope_ref[:, columns].astype(jnp.float32)
        hidden_low = hidden_grad.astype(jnp.bfloat16)
        hidden_ref[:, columns] = hidden_low
        add_small(8 + j, hidden_low.astype(jnp.float32))
        first_grad = first_grad + dot_nt(hidden_low, up[:, columns])

    normal = n1_ref[...].astype(jnp.float32)
    add_small(3, first_grad)
    add_small(6, first_grad * normal)
    branch_grad = normalize_back(
        first_grad, normal, stats[:, stat_first : stat_first + 1], gain_rows[0:1]
    )
    total_buf[...] = branch_grad
    branch_low = branch_grad.astype(jnp.bfloat16)
    branch_ref[...] = branch_low
    add_small(2, branch_low.astype(jnp.float32))
    weight = weights.get(1)
    context_grad[...] = dot_nt(branch_low, weight[...])

    for h in range(HEADS):
        head = pl.ds(h * HEAD_DIM, HEAD_DIM)
        part = lambda j: packed_ref[:, pl.ds(j * features + h * HEAD_DIM, HEAD_DIM)]
        scaled = context_grad[:, head] * stats[:, h : h + 1]
        inner = jnp.sum(scaled * context_ref[:, head].astype(jnp.float32), axis=-1, keepdims=True)
        scaled_low = scaled.astype(jnp.bfloat16)
        chance_low = chances[0, h]
        weight_grad = dot_nt(scaled_low, part(2))
        score_low = (chance_low.astype(jnp.float32) * (weight_grad - inner)).astype(jnp.bfloat16)
        for j, value in (
            (0, dot_nn(score_low, part(1)) * HEAD_DIM ** (-0.5)),
            (1, dot_tn(score_low, part(0)) * HEAD_DIM ** (-0.5)),
            (2, dot_tn(chance_low, scaled_low)),
        ):
            packed_grad[:, pl.ds(j * features + h * HEAD_DIM, HEAD_DIM)] = value.astype(jnp.bfloat16)
    add_small(0, packed_grad[:, :features].astype(jnp.float32))
    add_small(1, packed_grad[:, 2 * features :].astype(jnp.float32))

    weight = weights.get(0)
    input_grad = total_buf[...] + dot_nt(packed_grad[...], weight[...])

    @pl.when(i < first_passage)
    def _():
        q_grad[...] = input_grad

    @pl.when(i >= first_passage)
    def _():
        p_grad[...] = input_grad


def block_specs(first_passage):
    q_at = lambda i, starts: (jnp.minimum(i, first_passage - 1), 0)
    p_at = lambda i, starts: (jnp.maximum(i - first_passage, 0), 0)
    at = lambda i, starts: (i, 0)

    def rows(width, index=at):
        return pl.BlockSpec((block_tokens, width), index)

    def lead(*shape):
        return pl.BlockSpec((1,) + shape, lambda i, starts: (i,) + (0,) * len(shape))

    def whole(array):
        return pl.BlockSpec(array.shape, lambda i, starts: (0,) * array.ndim)

    anywhere = pl.BlockSpec(memory_space=pl.ANY)
    return q_at, p_at, rows, lead, whole, anywhere


def weight_scratch(stacked):
    return [pltpu.VMEM(w.shape, w.dtype) for w in stacked[:4]] + [pltpu.SemaphoreType.DMA((4, 2))]


def encode_all(starts, q_rows, p_rows, stacked):
    projection, mixing, expand, shrink, biases, gains, widening = stacked
    features, wide = projection.shape[1], expand.shape[2]
    first_passage, blocks = q_rows.shape[0] // block_tokens, starts.shape[0]
    q_at, p_at, rows, lead, whole, anywhere = block_specs(first_passage)
    low, tokens = jnp.bfloat16, blocks * block_tokens
    widening = widening[:, None, :]
    shape = jax.ShapeDtypeStruct
    return pl.pallas_call(
        partial(forward_kernel, first_passage),
        out_shape=[
            shape(q_rows.shape, low), shape(p_rows.shape, low),
            shape((blocks, cls_slots, features), jnp.float32),
            shape((blocks, HEADS, block_tokens, block_tokens), low),
            shape((tokens, lane), jnp.float32),
            shape((tokens, 3 * features), low),
            shape((tokens, features), low), shape((tokens, features), low),
            shape((tokens, features), low), shape((tokens, features), low),
            shape((tokens, wide), low), shape((tokens, wide), low),
        ],
        grid_spec=pltpu.PrefetchScalarGridSpec(
            num_scalar_prefetch=1,
            grid=(blocks,),
            in_specs=[
                rows(features, q_at), rows(features, p_at), anywhere, anywhere, anywhere, anywhere,
                whole(biases), whole(gains), whole(widening),
            ],
            out_specs=[
                rows(features, q_at), rows(features, p_at), lead(cls_slots, features),
                lead(HEADS, block_tokens, block_tokens), rows(lane), rows(3 * features),
                rows(features), rows(features), rows(features), rows(features), rows(wide), rows(wide),
            ],
            scratch_shapes=weight_scratch(stacked) + [
                pltpu.VMEM((block_tokens, features), jnp.float32),
                pltpu.VMEM((block_tokens, features), low),
            ],
        ),
        compiler_params=pltpu.CompilerParams(
            dimension_semantics=("arbitrary",), vmem_limit_bytes=vmem_bytes
        ),
    )(starts, q_rows, p_rows, projection, mixing, expand, shrink, biases, gains, widening)


def encode_all_back(starts, q_cot, p_cot, cls_grad, saved, stacked):
    projection, mixing, expand, shrink, biases, gains, widening = stacked
    chances, stats, packed, context, first, n1, n2, active, slope = saved
    features, wide = projection.shape[1], expand.shape[2]
    first_passage, blocks = q_cot.shape[0] // block_tokens, starts.shape[0]
    q_at, p_at, rows, lead, whole, anywhere = block_specs(first_passage)
    low, tokens = jnp.bfloat16, blocks * block_tokens
    shape = jax.ShapeDtypeStruct
    small_rows = 8 + wide // features
    return pl.pallas_call(
        partial(backward_kernel, first_passage),
        out_shape=[
            shape(q_cot.shape, jnp.float32), shape(p_cot.shape, jnp.float32),
            shape((tokens, features), low), shape((tokens, wide), low),
            shape((tokens, features), low), shape((tokens, 3 * features), low),
            shape((2, small_rows, features), jnp.float32),
        ],
        grid_spec=pltpu.PrefetchScalarGridSpec(
            num_scalar_prefetch=1,
            grid=(blocks,),
            in_specs=[
                rows(features, q_at), rows(features, p_at), lead(cls_slots, features),
                lead(HEADS, block_tokens, block_tokens), rows(lane), rows(3 * features),
                rows(features), rows(features), rows(features), rows(wide),
                anywhere, anywhere, anywhere, anywhere, whole(gains),
            ],
            out_specs=[
                rows(features, q_at), rows(features, p_at), rows(features), rows(wide),
                rows(features), rows(3 * features),
                pl.BlockSpec(
                    (1, small_rows, features),
                    lambda i, starts: ((i >= first_passage).astype(jnp.int32), 0, 0),
                ),
            ],
            scratch_shapes=weight_scratch(stacked) + [
                pltpu.VMEM((block_tokens, features), jnp.float32),
                pltpu.VMEM((block_tokens, features), jnp.float32),
            ],
        ),
        compiler_params=pltpu.CompilerParams(
            dimension_semantics=("arbitrary",), vmem_limit_bytes=vmem_bytes
        ),
    )(
        starts, q_cot, p_cot, cls_grad, chances, stats, packed, context, n1, n2, slope,
        projection, mixing, expand, shrink, gains,
    )


panel_rows = 48
chunk_panels = 8
encoder_chunks = 9
MESH = pl.DeviceIdType.MESH


def reduce_kernel(
    tokens,
    active, second, first, hidden, packed, context, branch, q_rows, p_rows,
    small_ref,
    out_ref, small_out,
    keep, core_send, core_recv, recv_x, recv_ya, recv_za, recv_yb, recv_zb, fin_a, fin_b,
    left_buf, left_t, right_buf, product, small_recv, small_sum,
    load_sem, core_ss, core_rs, xa_ss, xa_rs, ya_ss, ya_rs, za_ss, za_rs, ag_ss, ag_rs,
    yb_ss, yb_rs, zb_ss, zb_rs, xb_ss, xb_rs, small_ss, small_rs, credit,
):
    chunks = 2 * encoder_chunks
    pb, pa = lax.axis_index("pb"), lax.axis_index("pa")
    core, y, z, x = pa % 2, pa // 2 % 2, pa // 4, pb
    at_core = (pb, pa + 1 - 2 * core)
    at_y = (pb, pa + 2 - 4 * y)
    at_x = (1 - pb, pa)
    far_z = [(z + d) % 4 for d in (1, 2, 3)]
    at_z = [(pb, t * 4 + y * 2 + core) for t in far_z]

    barrier = pltpu.get_barrier_semaphore()
    for device in [at_core, at_y, at_x] + at_z:
        pl.semaphore_signal(barrier, inc=1, device_id=device, device_id_type=MESH)
    pl.semaphore_wait(barrier, 6)

    def remote(src, dst, ss, rs, device):
        return pltpu.make_async_remote_copy(
            src_ref=src, dst_ref=dst, send_sem=ss, recv_sem=rs, device_id=device, device_id_type=MESH
        )

    def copy_core(c):
        return remote(core_send.at[c % 2], core_recv.at[c % 3], core_ss.at[c], core_rs.at[c], at_core)

    def copy_xa(c):
        return remote(keep.at[c, pl.ds(2 * (1 - x), 2)], recv_x.at[c], xa_ss.at[c], xa_rs.at[c], at_x)

    def copy_ya(c):
        return remote(
            keep.at[c, pl.ds(2 * x, 2), :, 1 - y], recv_ya.at[c], ya_ss.at[c], ya_rs.at[c], at_y
        )

    def copy_za(c, d):
        return remote(
            keep.at[c, pl.ds(2 * x, 2), far_z[d], y], recv_za.at[c, d], za_ss.at[c, d], za_rs.at[c, d], at_z[d]
        )

    def copy_ag(c):
        half = fin_a.at[c, pl.ds(2 * x, 2)]
        return remote(half, half, ag_ss.at[c], ag_rs.at[c], at_x)

    def copy_yb(c):
        return remote(keep.at[c, pl.ds(4, 4), :, 1 - y], recv_yb.at[c], yb_ss.at[c], yb_rs.at[c], at_y)

    def copy_zb(c, d):
        return remote(
            keep.at[c, pl.ds(4, 4), far_z[d], y], recv_zb.at[c, d], zb_ss.at[c, d], zb_rs.at[c, d], at_z[d]
        )

    def copy_xb(c):
        return remote(fin_b.at[c, x], fin_b.at[c, x], xb_ss.at[c], xb_rs.at[c], at_x)

    def small_copy(stage, device):
        source = small_sum.at[max(stage - 3, 0) if stage >= 3 else stage]
        return remote(source, small_recv.at[stage], small_ss.at[stage], small_rs.at[stage], device)

    def own(e, ref):
        return ref.at[pl.ds(0 if e == 0 else tokens[0], tokens[e])]

    def left_loads(e, part):
        count = tokens[e]
        features = q_rows.shape[1]
        if part == 0:
            pairs = [(own(e, active), 0)]
        elif part == 1:
            pairs = [(own(e, first), 0)]
        else:
            pairs = [((q_rows, p_rows)[e], 0), (own(e, context), features)]
        return [
            pltpu.make_async_copy(
                ref,
                left_buf.at[pl.ds(0, count), pl.ds(at, ref.shape[1])],
                load_sem.at[2 + i],
            )
            for i, (ref, at) in enumerate(pairs)
        ]

    def right_loads(e, k):
        count = tokens[e]
        slot = (e * encoder_chunks + k) % 2
        if k < 3:
            pairs = [(second, 256 * k, 256, 0)]
        elif k < 6:
            pairs = [(hidden, 1024 * (k - 3), 1024, 0)]
        elif k < 8:
            pairs = [(packed, 1024 * (k - 6), 1024, 0)]
        else:
            pairs = [(packed, 2048, 256, 0), (branch, 0, 768, 256)]
        return [
            pltpu.make_async_copy(
                own(e, ref).at[:, pl.ds(start, width)],
                right_buf.at[slot, pl.ds(0, count), pl.ds(at, width)],
                load_sem.at[slot] if i == 0 else load_sem.at[4],
            )
            for i, (ref, start, width, at) in enumerate(pairs)
        ]

    def begin(copies):
        for copy in copies:
            copy.start()

    def finish(copies):
        for copy in copies:
            copy.wait()

    def transpose_left(e, part):
        count = tokens[e]
        width = (3072, 768, 1536)[part]

        def step(i, carry):
            at = pl.multiple_of(i * 256, 256)
            left_t[pl.ds(at, 256), pl.ds(0, count)] = left_buf[pl.ds(0, count), pl.ds(at, 256)].T
            return carry

        lax.fori_loop(0, width // 256, step, 0)

    def compute(e, k):
        count = tokens[e]
        c = e * encoder_chunks + k
        slot = c % 2

        def step(q, carry):
            if k < 3:
                rows_at, columns_at = q * 768, 0
            elif k < 8:
                rows_at, columns_at = 0, q * 256
            else:
                rows_at, columns_at = jnp.where(q > 0, 768, 0), q * 256
            rows_at = pl.multiple_of(rows_at, 256)
            columns_at = pl.multiple_of(columns_at, 256)
            product[...] = jnp.dot(
                left_t[pl.ds(rows_at, 768), pl.ds(0, count)],
                right_buf[slot, pl.ds(0, count), pl.ds(columns_at, 256)],
                preferred_element_type=jnp.float32,
            )
            if k < 3:
                for iy in range(2):
                    for sub in range(4):
                        for which, target in ((core, keep.at[c]), (1 - core, core_send.at[slot])):
                            at = pl.multiple_of((2 * iy + which) * 192 + sub * 48, 16)
                            block = product[pl.ds(at, 48), :].astype(jnp.bfloat16)
                            target[sub * 2, q, iy] = block[:, :lane]
                            target[sub * 2 + 1, q, iy] = block[:, lane:]
            else:
                for iz in range(4):
                    for iy in range(2):
                        for which, target in ((core, keep.at[c]), (1 - core, core_send.at[slot])):
                            at = pl.multiple_of((4 * iz + 2 * iy + which) * 48, 16)
                            block = product[pl.ds(at, 48), :].astype(jnp.bfloat16)
                            target[2 * q, iz, iy] = block[:, :lane]
                            target[2 * q + 1, iz, iy] = block[:, lane:]
            return carry

        lax.fori_loop(0, 4, step, 0)

    order = [(e, k) for e in range(2) for k in range(encoder_chunks)]
    part_of = lambda k: 0 if k < 3 else 1 if k < 6 else 2

    def produce(c):
        e, k = order[c]
        if c >= 2:
            copy_core(c - 2).wait_send()
        if k % 3 == 0:
            finish(left_loads(e, part_of(k)))
            transpose_left(e, part_of(k))
            if c + 3 < chunks:
                e2, k2 = order[c + 3]
                begin(left_loads(e2, part_of(k2)))
        finish(right_loads(e, k))
        if c + 1 < chunks:
            begin(right_loads(*order[c + 1]))
        compute(e, k)
        if c >= 3:
            pl.semaphore_wait(credit, 1)
        copy_core(c).start()

    def after_core(c):
        copy_core(c).wait_recv()

        def step(p, carry):
            keep[c, p] = keep[c, p] + core_recv[c % 3, p]
            return carry

        lax.fori_loop(0, chunk_panels, step, 0)
        copy_xa(c).start()
        copy_yb(c).start()

        @pl.when(c < chunks - 3)
        def _():
            pl.semaphore_signal(credit, inc=1, device_id=at_core, device_id_type=MESH)

    def after_first(c):
        copy_yb(c).wait_recv()

        def step_b(p, carry):
            for iz in range(4):
                keep[c, 4 + p, iz, y] = keep[c, 4 + p, iz, y] + recv_yb[c, p, iz]
            return carry

        lax.fori_loop(0, 4, step_b, 0)
        for d in range(3):
            copy_zb(c, d).start()
        copy_xa(c).wait_recv()

        def step_a(p, carry):
            keep[c, 2 * x + p] = keep[c, 2 * x + p] + recv_x[c, p]
            return carry

        lax.fori_loop(0, 2, step_a, 0)
        copy_ya(c).start()

    def widen(value):
        return value.astype(jnp.float32)

    def after_second(c):
        copy_ya(c).wait_recv()

        def step_a(p, carry):
            for iz in range(4):
                keep[c, 2 * x + p, iz, y] = keep[c, 2 * x + p, iz, y] + recv_ya[c, p, iz]
            return carry

        lax.fori_loop(0, 2, step_a, 0)
        for d in range(3):
            copy_za(c, d).start()
        for d in range(3):
            copy_zb(c, d).wait_recv()

        def step_b(p, carry):
            fin_b[c, x, p] = (
                widen(keep[c, 4 + p, z, y])
                + widen(recv_zb[c, 0, p])
                + widen(recv_zb[c, 1, p])
                + widen(recv_zb[c, 2, p])
            ).astype(jnp.bfloat16)
            return carry

        lax.fori_loop(0, 4, step_b, 0)
        copy_xb(c).start()

    def after_third(c):
        for d in range(3):
            copy_za(c, d).wait_recv()

        def step_a(p, carry):
            fin_a[c, 2 * x + p] = (
                widen(keep[c, 2 * x + p, z, y])
                + widen(recv_za[c, 0, p])
                + widen(recv_za[c, 1, p])
                + widen(recv_za[c, 2, p])
            ).astype(jnp.bfloat16)
            return carry

        lax.fori_loop(0, 2, step_a, 0)
        copy_ag(c).start()
        copy_xb(c).wait_recv()

        def step_b(p, carry):
            out_ref[c, 4 + p] = widen(fin_b[c, 0, p]) + widen(fin_b[c, 1, p])
            return carry

        lax.fori_loop(0, 4, step_b, 0)

    def after_last(c):
        copy_ag(c).wait_recv()

        def step(p, carry):
            out_ref[c, p] = widen(fin_a[c, p])
            return carry

        lax.fori_loop(0, 4, step, 0)

    begin(left_loads(0, 0))
    begin(right_loads(0, 0))
    small_sum[0] = small_ref[...]
    small_copy(0, at_core).start()
    for c in range(chunks + 5):
        if c < chunks:
            produce(c)
        if 0 <= c - 1 < chunks:
            after_core(c - 1)
        if 0 <= c - 2 < chunks:
            after_first(c - 2)
        if 0 <= c - 3 < chunks:
            after_second(c - 3)
        if 0 <= c - 4 < chunks:
            after_third(c - 4)
        if 0 <= c - 5 < chunks:
            after_last(c - 5)
        if c == 1:
            small_copy(0, at_core).wait_recv()
            small_sum[1] = small_sum[0] + small_recv[0]
            small_copy(1, at_x).start()
        if c == 2:
            small_copy(1, at_x).wait_recv()
            small_sum[2] = small_sum[1] + small_recv[1]
            small_copy(2, at_y).start()
        if c == 3:
            small_copy(2, at_y).wait_recv()
            small_sum[3] = small_sum[2] + small_recv[2]
            for d in range(3):
                remote(small_sum.at[3], small_recv.at[3 + d], small_ss.at[3 + d], small_rs.at[3 + d], at_z[d]).start()
        if c == 4:
            for d in range(3):
                remote(small_sum.at[3], small_recv.at[3 + d], small_ss.at[3 + d], small_rs.at[3 + d], at_z[d]).wait_recv()
            result = jnp.zeros_like(small_ref)
            for iz in range(4):
                back = (z - iz + 4) % 4
                value = jnp.where(back == 0, small_sum[3], 0.0)
                for d in range(3):
                    value = jnp.where(back == d + 1, small_recv[3 + d], value)
                result = result + value
            small_out[...] = result

    copy_core(chunks - 2).wait_send()
    copy_core(chunks - 1).wait_send()

    def drain(c, carry):
        copy_xa(c).wait_send()
        copy_ya(c).wait_send()
        copy_ag(c).wait_send()
        copy_yb(c).wait_send()
        copy_xb(c).wait_send()
        for d in range(3):
            copy_za(c, d).wait_send()
            copy_zb(c, d).wait_send()
        return carry

    lax.fori_loop(0, chunks, drain, 0)
    small_copy(0, at_core).wait_send()
    small_copy(1, at_x).wait_send()
    small_copy(2, at_y).wait_send()
    for d in range(3):
        remote(small_sum.at[3], small_recv.at[3 + d], small_ss.at[3 + d], small_rs.at[3 + d], at_z[d]).wait_send()


def reduce_by_kernel(operands, small):
    tokens = (operands[-2].shape[0], operands[-1].shape[0])
    most = max(tokens)
    chunks = 2 * encoder_chunks
    tile = (panel_rows, lane)
    low = jnp.bfloat16
    dma = pltpu.SemaphoreType.DMA
    one, three = dma((chunks,)), dma((chunks, 3))
    raw, small_total = pl.pallas_call(
        partial(reduce_kernel, tokens),
        out_shape=[
            jax.ShapeDtypeStruct((chunks, chunk_panels) + tile, jnp.float32),
            jax.ShapeDtypeStruct(small.shape, jnp.float32),
        ],
        in_specs=[pl.BlockSpec(memory_space=pl.ANY)] * 9 + [pl.BlockSpec(memory_space=pltpu.VMEM)],
        out_specs=[pl.BlockSpec(memory_space=pltpu.VMEM)] * 2,
        scratch_shapes=[
            pltpu.VMEM((chunks, chunk_panels, 4, 2) + tile, low),
            pltpu.VMEM((2, chunk_panels, 4, 2) + tile, low),
            pltpu.VMEM((3, chunk_panels, 4, 2) + tile, low),
            pltpu.VMEM((chunks, 2, 4, 2) + tile, low),
            pltpu.VMEM((chunks, 2, 4) + tile, low),
            pltpu.VMEM((chunks, 3, 2) + tile, low),
            pltpu.VMEM((chunks, 4, 4) + tile, low),
            pltpu.VMEM((chunks, 3, 4) + tile, low),
            pltpu.VMEM((chunks, 4) + tile, low),
            pltpu.VMEM((chunks, 2, 4) + tile, low),
            pltpu.VMEM((most, 3072), low),
            pltpu.VMEM((3072, most), low),
            pltpu.VMEM((2, most, 1024), low),
            pltpu.VMEM((768, 256), jnp.float32),
            pltpu.VMEM((6,) + small.shape, jnp.float32),
            pltpu.VMEM((4,) + small.shape, jnp.float32),
            dma((5,)),
            one, one, one, one, one, one, three, three, one, one,
            one, one, three, three, one, one, dma((6,)), dma((6,)),
            pltpu.SemaphoreType.REGULAR,
        ],
        compiler_params=pltpu.CompilerParams(
            collective_id=1, has_side_effects=True, vmem_limit_bytes=63 * 1024 * 1024
        ),
        cost_estimate=pl.CostEstimate(flops=22 * 10**9, bytes_accessed=60 * 10**6, transcendentals=0),
    )(*operands, small)
    raw = raw.reshape(2, encoder_chunks, chunk_panels, panel_rows, lane)
    shrink = raw[:, :3].reshape(2, 3, 4, 2, 48, lane).transpose(0, 2, 4, 1, 3, 5).reshape(2, 192, 768)
    expand = raw[:, 3:6].transpose(0, 3, 1, 2, 4).reshape(2, 48, 3072)
    rest = raw[:, 6:].transpose(0, 3, 1, 2, 4).reshape(2, 48, 3072)
    return rest[:, :, :2304], rest[:, :, 2304:], expand, shrink, small_total


def share_gradients(operands, small):
    size_pa, size_pb = lax.axis_size("pa"), lax.axis_size("pb")
    active, second, first, hidden, packed, context, branch, q_rows, p_rows = operands
    features = q_rows.shape[1]
    if size_pa == 16 and size_pb == 2:
        projection, mixing, expand, shrink, small = reduce_by_kernel(
            operands, small.reshape(-1, features)
        )
        small = small.reshape(2, -1, features)
    else:
        products = []
        cut = q_rows.shape[0]
        for rows, part in ((q_rows, slice(None, cut)), (p_rows, slice(cut, None))):
            pairs = ((rows, packed[part]), (context[part], branch[part]), (first[part], hidden[part]), (active[part], second[part]))
            products.append([contract_rows(*pair) for pair in pairs])
        projection, mixing, expand, shrink = (
            lax.psum(
                jnp.stack(
                    [
                        lax.psum_scatter(products[e][i], "pa", scatter_dimension=0, tiled=True)
                        for e in range(2)
                    ]
                ),
                "pb",
            )
            for i in range(4)
        )
        small = lax.psum(small, ("pb", "pa"))
    mine = lax.axis_index("pa")
    share = features // size_pa
    columns = lax.dynamic_slice_in_dim(small[:, :8], mine * share, share, 2)
    widening = small[:, 8:].reshape(2, -1)
    wide = widening.shape[1] // size_pa
    widening = lax.dynamic_slice_in_dim(widening, mine * wide, wide, 1)
    return (projection, mixing, expand, shrink, columns[:, :6], columns[:, 6:], widening)


def body(
    question_rows,
    passage_rows,
    segment_lengths,
    positives,
    negatives,
    question_cotangent,
    passage_cotangent,
    loss_weight,
    projection,
    mixing,
    expand,
    shrink,
    biases,
    gains,
    widening,
):
    stacked = (projection, mixing, expand, shrink, biases, gains, widening)
    question_count, question_length, features = question_rows.shape
    passage_count, passage_length = (passage_rows.shape[0], passage_rows.shape[1])
    packed_count = segment_lengths.shape[1]
    per_block = block_tokens // question_length
    q_rows = question_rows.reshape(-1, features)
    p_rows = passage_rows.reshape(-1, features)
    question_starts = jnp.broadcast_to(
        jnp.arange(cls_slots, dtype=jnp.int32) * question_length, (question_count // per_block, cls_slots)
    )
    passage_ends = jnp.cumsum(segment_lengths, axis=-1, dtype=jnp.int32)
    passage_starts = jnp.concatenate([jnp.zeros_like(passage_ends[:, :1]), passage_ends], axis=1)
    starts = jnp.concatenate([question_starts, passage_starts])
    q_states, p_states, cls, *saved = encode_all(starts, q_rows, p_rows, stacked)
    q_blocks = question_starts.shape[0]
    question_cls = cls[:q_blocks].reshape(question_count, features).astype(jnp.bfloat16)
    passage_cls = (
        cls[q_blocks:, :packed_count].reshape(passage_count * packed_count, features).astype(jnp.bfloat16)
    )
    row_block = lax.all_gather(question_cls, "pa", axis=0, tiled=True)
    col_block = lax.all_gather(passage_cls, "pb", axis=0, tiled=True)
    columns = jnp.concatenate([col_block, negatives], axis=0)
    tile_scale = 2.0 / math.sqrt(features)
    scores = contract_cols(row_block, columns) * tile_scale
    per_device = passage_cls.shape[0]
    passage_columns = col_block.shape[0]
    column_ids = jnp.arange(passage_columns, dtype=jnp.int32)
    owner_index = column_ids // per_device
    global_ids = (
        owner_index * lax.axis_size("pa") + lax.axis_index("pa")
    ) * per_device + column_ids % per_device
    chosen_mask = jnp.concatenate(
        [
            (positives[:, None] == global_ids[None, :]).astype(jnp.float32),
            jnp.zeros((row_block.shape[0], negatives.shape[0]), jnp.float32),
        ],
        axis=1,
    )
    row_top = jnp.max(scores, axis=1)
    exp_total = jnp.sum(jnp.exp(scores - row_top[:, None]), axis=1)
    chosen = jnp.sum(scores * chosen_mask, axis=1)
    global_top = lax.pmax(row_top, "pa")
    exp_total, chosen = lax.psum((exp_total * jnp.exp(row_top - global_top), chosen), "pa")
    row_top = global_top
    logsum = row_top + jnp.log(exp_total)
    question_loss = logsum - chosen
    tile_grad = (loss_weight[:, None] * (jnp.exp(scores - logsum[:, None]) - chosen_mask)).astype(
        jnp.bfloat16
    )
    row_terms = matmul(tile_grad, columns) * tile_scale
    row_mine = lax.psum_scatter(row_terms, "pa", scatter_dimension=0, tiled=True)
    col_terms = contract_rows(tile_grad[:, :passage_columns], row_block) * tile_scale
    col_mine = lax.psum_scatter(col_terms, "pb", scatter_dimension=0, tiled=True)
    cls_grad = jnp.concatenate(
        [
            row_mine.reshape(q_blocks, cls_slots, features),
            jnp.pad(
                col_mine.reshape(passage_count, packed_count, features),
                ((0, 0), (0, cls_slots - packed_count), (0, 0)),
            ),
        ]
    )
    q_grad, p_grad, second, hidden, branch, packed_grad, small = encode_all_back(
        starts,
        question_cotangent.reshape(-1, features),
        passage_cotangent.reshape(-1, features),
        cls_grad,
        saved,
        stacked,
    )
    chances, stats, packed, context, first, n1, n2, active, slope = saved
    totals = share_gradients(
        (active, second, first, hidden, packed_grad, context, branch, q_rows, p_rows), small
    )
    return (
        q_states.reshape(question_rows.shape),
        p_states.reshape(passage_rows.shape),
        question_loss,
        q_grad.reshape(question_rows.shape),
        p_grad.reshape(passage_rows.shape),
    ) + totals


def solution(mesh):
    return jax.shard_map(
        body,
        mesh=mesh,
        in_specs=(
            P(("pb", "pa"), None, None),
            P(("pb", "pa"), None, None),
            P(("pb", "pa"), None),
            P("pb"),
            P("pa", None),
            P(("pb", "pa"), None, None),
            P(("pb", "pa"), None, None),
            P("pb"),
            P(),
            P(),
            P(),
            P(),
            P(),
            P(),
            P(),
        ),
        out_specs=(
            P(("pb", "pa"), None, None),
            P(("pb", "pa"), None, None),
            P("pb"),
            P(("pb", "pa"), None, None),
            P(("pb", "pa"), None, None),
            P(None, "pa", None),
            P(None, "pa", None),
            P(None, "pa", None),
            P(None, "pa", None),
            P(None, None, "pa"),
            P(None, None, "pa"),
            P(None, "pa"),
        ),
        check_vma=False,
    )
```

```python
from functools import partial
import math

import jax
import jax.numpy as jnp
from jax import lax
from jax.experimental import pallas as pl
from jax.experimental.pallas import tpu as pltpu
from jax.sharding import PartitionSpec as P

HEADS = 12
HEAD_DIM = 64


eps_norm = 1e-12
masked_score = -1000000000.0


def matmul(left_side, right_side):
    return jnp.dot(left_side, right_side, preferred_element_type=jnp.float32)


def contract_rows(left_side, right_side):
    return lax.dot_general(
        left_side, right_side, (((0,), (0,)), ((), ())), preferred_element_type=jnp.float32
    )


def contract_cols(left_side, right_side):
    return lax.dot_general(
        left_side, right_side, (((1,), (1,)), ((), ())), preferred_element_type=jnp.float32
    )


MESH = pl.DeviceIdType.MESH
lane = 128
block_tokens = 256
cls_slots = 4
stat_first, stat_final = HEADS, HEADS + 1
vmem_bytes = 63 * 1024 * 1024


def dot_nn(left_side, right_side):
    return jnp.dot(left_side, right_side, preferred_element_type=jnp.float32)


def dot_nt(left_side, right_side):
    return lax.dot_general(
        left_side, right_side, (((1,), (1,)), ((), ())), preferred_element_type=jnp.float32
    )


def dot_tn(left_side, right_side):
    return lax.dot_general(
        left_side, right_side, (((0,), (0,)), ((), ())), preferred_element_type=jnp.float32
    )


def gelu_and_slope(hidden):
    size = jnp.abs(hidden)
    t = 1.0 / (1.0 + (0.3275911 * math.sqrt(0.5)) * size)
    bell = jnp.exp(-0.5 * hidden * hidden)
    tail = 1.061405429 * t - 1.453152027
    tail = tail * t + 1.421413741
    tail = tail * t - 0.284496736
    tail = (tail * t + 0.254829592) * (0.5 * t) * bell
    below = jnp.where(hidden < 0.0, tail, 1.0 - tail)
    return hidden * below, below + hidden * bell * (1.0 / math.sqrt(2.0 * math.pi))


def normalize(values):
    centre = values - jnp.mean(values, axis=-1, keepdims=True)
    inverse = lax.rsqrt(jnp.mean(centre * centre, axis=-1, keepdims=True) + eps_norm)
    return centre * inverse, inverse


def normalize_back(gradient, normal, inverse, gain_row):
    scaled = gradient * gain_row
    inner_mean = jnp.mean(scaled, axis=-1, keepdims=True)
    projected = jnp.mean(scaled * normal, axis=-1, keepdims=True)
    return inverse * (scaled - inner_mean - normal * projected)


class Weights:
    def __init__(self, sources, buffers, sems, step, first_passage, order):
        self.sources, self.buffers, self.sems, self.order = sources, buffers, sems, order
        self.step, self.first_passage = step, first_passage
        self.encoder = (step >= first_passage).astype(jnp.int32)

    def copy(self, which, e):
        return pltpu.make_async_copy(
            self.sources[which].at[e], self.buffers[which].at[e], self.sems.at[which, e]
        )

    def begin(self):
        @pl.when(self.step == 0)
        def _():
            for e in range(2):
                for which in self.order:
                    self.copy(which, e).start()

    def get(self, which):
        for e, at in ((0, 0), (1, self.first_passage)):

            @pl.when(self.step == at)
            def _():
                self.copy(which, e).wait()

        return self.buffers[which].at[self.encoder]


def forward_kernel(
    first_passage,
    starts,
    q_rows, p_rows, projection, mixing, expand, shrink, biases, gains, widening,
    q_states, p_states, cls, chances, stats, packed_ref, context_ref, first_ref, n1_ref, n2_ref,
    active_ref, slope_ref,
    w0, w1, w2, w3, sems, final_buf, x_buf,
):
    i = pl.program_id(0)
    weights = Weights((projection, mixing, expand, shrink), (w0, w1, w2, w3), sems, i, first_passage, (0, 1, 2, 3))
    weights.begin()
    e = weights.encoder
    features = q_rows.shape[1]
    shifts = biases[e].astype(jnp.float32)
    gain_rows = gains[e].astype(jnp.float32)
    x_buf[...] = jnp.where(i < first_passage, q_rows[...], p_rows[...])

    weight = weights.get(0)
    x_low = x_buf[...]
    for part in range(3):
        columns = pl.ds(part * features, features)
        value = dot_nn(x_low, weight[:, columns])
        if part != 1:
            value = value + shifts[part // 2 : part // 2 + 1]
        packed_ref[:, columns] = value.astype(jnp.bfloat16)

    tokens = q_rows.shape[0]
    row_at = lax.broadcasted_iota(jnp.int32, (tokens, tokens), 0)
    col_at = lax.broadcasted_iota(jnp.int32, (tokens, tokens), 1)
    row_segment = jnp.zeros_like(row_at)
    col_segment = jnp.zeros_like(col_at)
    for k in range(1, cls_slots):
        row_segment = row_segment + (row_at >= starts[i, k]).astype(jnp.int32)
        col_segment = col_segment + (col_at >= starts[i, k]).astype(jnp.int32)
    penalty = jnp.where(row_segment == col_segment, 0.0, masked_score)
    lanes = lax.broadcasted_iota(jnp.int32, stats.shape, 1)
    stat = jnp.zeros(stats.shape, jnp.float32)
    for h in range(HEADS):
        part = lambda j: packed_ref[:, pl.ds(j * features + h * HEAD_DIM, HEAD_DIM)]
        queries = part(0) * jnp.asarray(HEAD_DIM ** (-0.5), jnp.bfloat16)
        scores = dot_nt(queries, part(1)) + penalty
        top = jnp.max(scores, axis=-1, keepdims=True)
        chance = jnp.exp(scores - top)
        inverse = 1.0 / jnp.sum(chance, axis=-1, keepdims=True)
        chance_low = chance.astype(jnp.bfloat16)
        chances[0, h] = chance_low
        stat = jnp.where(lanes == h, inverse, stat)
        mixed = dot_nn(chance_low, part(2)) * inverse
        context_ref[:, pl.ds(h * HEAD_DIM, HEAD_DIM)] = mixed.astype(jnp.bfloat16)

    weight = weights.get(1)
    branch = dot_nn(context_ref[...], weight[...]) + shifts[2:3]
    normal, inverse = normalize(x_buf[...].astype(jnp.float32) + branch)
    n1_ref[...] = normal.astype(jnp.bfloat16)
    stat = jnp.where(lanes == stat_first, inverse, stat)
    first = normal * gain_rows[0:1] + shifts[3:4]
    first_low = first.astype(jnp.bfloat16)
    first_ref[...] = first_low
    final_buf[...] = first

    up, down = weights.get(2), weights.get(3)
    second = jnp.broadcast_to(shifts[4:5], (tokens, features))
    for j in range(up.shape[1] // features):
        columns = pl.ds(j * features, features)
        hidden = dot_nn(first_low, up[:, columns]) + widening[e, :, columns].astype(jnp.float32)
        active, slope = gelu_and_slope(hidden)
        active_low = active.astype(jnp.bfloat16)
        active_ref[:, columns] = active_low
        slope_ref[:, columns] = slope.astype(jnp.bfloat16)
        second = second + dot_nn(active_low, down[columns, :])

    normal, inverse = normalize(final_buf[...] + second)
    n2_ref[...] = normal.astype(jnp.bfloat16)
    stats[...] = jnp.where(lanes == stat_final, inverse, stat)
    final = normal * gain_rows[1:2] + shifts[5:6]
    final_buf[...] = final

    @pl.when(i < first_passage)
    def _():
        q_states[...] = final.astype(jnp.bfloat16)

    @pl.when(i >= first_passage)
    def _():
        p_states[...] = final.astype(jnp.bfloat16)

    for k in range(cls_slots):
        at = jnp.minimum(starts[i, k], tokens - 1)
        cls[pl.ds(i * cls_slots + k, 1), :] = final_buf[pl.ds(at, 1), :]


def backward_kernel(
    first_passage,
    starts,
    q_cot, p_cot, cls_grad, chances, stats, packed_ref, context_ref, n1_ref, n2_ref, slope_ref,
    projection, mixing, expand, shrink, gains,
    q_grad, p_grad, second_ref, hidden_ref, branch_ref, packed_grad, small,
    w0, w1, w2, w3, sems, total_buf, context_grad,
):
    i = pl.program_id(0)
    weights = Weights((projection, mixing, expand, shrink), (w0, w1, w2, w3), sems, i, first_passage, (3, 2, 1, 0))
    weights.begin()
    e = weights.encoder
    tokens, features = q_cot.shape
    gain_rows = gains[e].astype(jnp.float32)

    @pl.when((i == 0) | (i == first_passage))
    def _():
        small[...] = jnp.zeros_like(small)

    def add_small(row, value):
        small[0, pl.ds(row, 1), :] += jnp.sum(value, axis=0, keepdims=True)

    gradient = jnp.where(i < first_passage, q_cot[...], p_cot[...]).astype(jnp.float32)
    row_at = lax.broadcasted_iota(jnp.int32, (tokens, 1), 0)
    for k in range(cls_slots):
        gradient = gradient + jnp.where(row_at == starts[i, k], cls_grad[pl.ds(i * cls_slots + k, 1), :], 0.0)
    normal = n2_ref[...].astype(jnp.float32)
    add_small(5, gradient)
    add_small(7, gradient * normal)
    total_grad = normalize_back(
        gradient, normal, stats[:, stat_final : stat_final + 1], gain_rows[1:2]
    )
    total_buf[...] = total_grad
    second_low = total_grad.astype(jnp.bfloat16)
    second_ref[...] = second_low
    add_small(4, second_low.astype(jnp.float32))

    down, up = weights.get(3), weights.get(2)
    first_grad = total_buf[...]
    for j in range(up.shape[1] // features):
        columns = pl.ds(j * features, features)
        hidden_grad = dot_nt(second_low, down[columns, :]) * slope_ref[:, columns].astype(jnp.float32)
        hidden_low = hidden_grad.astype(jnp.bfloat16)
        hidden_ref[:, columns] = hidden_low
        add_small(8 + j, hidden_low.astype(jnp.float32))
        first_grad = first_grad + dot_nt(hidden_low, up[:, columns])

    normal = n1_ref[...].astype(jnp.float32)
    add_small(3, first_grad)
    add_small(6, first_grad * normal)
    branch_grad = normalize_back(
        first_grad, normal, stats[:, stat_first : stat_first + 1], gain_rows[0:1]
    )
    total_buf[...] = branch_grad
    branch_low = branch_grad.astype(jnp.bfloat16)
    branch_ref[...] = branch_low
    add_small(2, branch_low.astype(jnp.float32))
    weight = weights.get(1)
    context_grad[...] = dot_nt(branch_low, weight[...])

    for h in range(HEADS):
        head = pl.ds(h * HEAD_DIM, HEAD_DIM)
        part = lambda j: packed_ref[:, pl.ds(j * features + h * HEAD_DIM, HEAD_DIM)]
        scaled = context_grad[:, head] * stats[:, h : h + 1]
        inner = jnp.sum(scaled * context_ref[:, head].astype(jnp.float32), axis=-1, keepdims=True)
        scaled_low = scaled.astype(jnp.bfloat16)
        chance_low = chances[0, h]
        weight_grad = dot_nt(scaled_low, part(2))
        score_low = (chance_low.astype(jnp.float32) * (weight_grad - inner)).astype(jnp.bfloat16)
        for j, value in (
            (0, dot_nn(score_low, part(1)) * HEAD_DIM ** (-0.5)),
            (1, dot_tn(score_low, part(0)) * HEAD_DIM ** (-0.5)),
            (2, dot_tn(chance_low, scaled_low)),
        ):
            packed_grad[:, pl.ds(j * features + h * HEAD_DIM, HEAD_DIM)] = value.astype(jnp.bfloat16)
    add_small(0, packed_grad[:, :features].astype(jnp.float32))
    add_small(1, packed_grad[:, 2 * features :].astype(jnp.float32))

    weight = weights.get(0)
    input_grad = total_buf[...] + dot_nt(packed_grad[...], weight[...])

    @pl.when(i < first_passage)
    def _():
        q_grad[...] = input_grad

    @pl.when(i >= first_passage)
    def _():
        p_grad[...] = input_grad


def block_specs(first_passage):
    q_at = lambda i, starts: (jnp.minimum(i, first_passage - 1), 0)
    p_at = lambda i, starts: (jnp.maximum(i - first_passage, 0), 0)
    at = lambda i, starts: (i, 0)

    def rows(width, index=at):
        return pl.BlockSpec((block_tokens, width), index)

    def lead(*shape):
        return pl.BlockSpec((1,) + shape, lambda i, starts: (i,) + (0,) * len(shape))

    def whole(array):
        return pl.BlockSpec(array.shape, lambda i, starts: (0,) * array.ndim)

    anywhere = pl.BlockSpec(memory_space=pl.ANY)
    return q_at, p_at, rows, lead, whole, anywhere


def weight_scratch(stacked):
    return [pltpu.VMEM(w.shape, w.dtype) for w in stacked[:4]] + [pltpu.SemaphoreType.DMA((4, 2))]


def encode_all(starts, q_rows, p_rows, stacked):
    projection, mixing, expand, shrink, biases, gains, widening = stacked
    features, wide = projection.shape[1], expand.shape[2]
    first_passage, blocks = q_rows.shape[0] // block_tokens, starts.shape[0]
    q_at, p_at, rows, lead, whole, anywhere = block_specs(first_passage)
    low, tokens = jnp.bfloat16, blocks * block_tokens
    widening = widening[:, None, :]
    shape = jax.ShapeDtypeStruct
    return pl.pallas_call(
        partial(forward_kernel, first_passage),
        out_shape=[
            shape(q_rows.shape, low), shape(p_rows.shape, low),
            shape((blocks * cls_slots, features), jnp.float32),
            shape((blocks, HEADS, block_tokens, block_tokens), low),
            shape((tokens, lane), jnp.float32),
            shape((tokens, 3 * features), low),
            shape((tokens, features), low), shape((tokens, features), low),
            shape((tokens, features), low), shape((tokens, features), low),
            shape((tokens, wide), low), shape((tokens, wide), low),
        ],
        grid_spec=pltpu.PrefetchScalarGridSpec(
            num_scalar_prefetch=1,
            grid=(blocks,),
            in_specs=[
                rows(features, q_at), rows(features, p_at), anywhere, anywhere, anywhere, anywhere,
                whole(biases), whole(gains), whole(widening),
            ],
            out_specs=[
                rows(features, q_at), rows(features, p_at),
                pl.BlockSpec((blocks * cls_slots, features), lambda i, starts: (0, 0)),
                lead(HEADS, block_tokens, block_tokens), rows(lane), rows(3 * features),
                rows(features), rows(features), rows(features), rows(features), rows(wide), rows(wide),
            ],
            scratch_shapes=weight_scratch(stacked) + [
                pltpu.VMEM((block_tokens, features), jnp.float32),
                pltpu.VMEM((block_tokens, features), low),
            ],
        ),
        compiler_params=pltpu.CompilerParams(
            dimension_semantics=("arbitrary",), vmem_limit_bytes=vmem_bytes
        ),
    )(starts, q_rows, p_rows, projection, mixing, expand, shrink, biases, gains, widening)


def encode_all_back(starts, q_cot, p_cot, cls_grad, saved, stacked):
    projection, mixing, expand, shrink, biases, gains, widening = stacked
    chances, stats, packed, context, first, n1, n2, active, slope = saved
    features, wide = projection.shape[1], expand.shape[2]
    first_passage, blocks = q_cot.shape[0] // block_tokens, starts.shape[0]
    q_at, p_at, rows, lead, whole, anywhere = block_specs(first_passage)
    low, tokens = jnp.bfloat16, blocks * block_tokens
    shape = jax.ShapeDtypeStruct
    small_rows = 8 + wide // features
    return pl.pallas_call(
        partial(backward_kernel, first_passage),
        out_shape=[
            shape(q_cot.shape, jnp.float32), shape(p_cot.shape, jnp.float32),
            shape((tokens, features), low), shape((tokens, wide), low),
            shape((tokens, features), low), shape((tokens, 3 * features), low),
            shape((2, small_rows, features), jnp.float32),
        ],
        grid_spec=pltpu.PrefetchScalarGridSpec(
            num_scalar_prefetch=1,
            grid=(blocks,),
            in_specs=[
                rows(features, q_at), rows(features, p_at), whole(cls_grad),
                lead(HEADS, block_tokens, block_tokens), rows(lane), rows(3 * features),
                rows(features), rows(features), rows(features), rows(wide),
                anywhere, anywhere, anywhere, anywhere, whole(gains),
            ],
            out_specs=[
                rows(features, q_at), rows(features, p_at), rows(features), rows(wide),
                rows(features), rows(3 * features),
                pl.BlockSpec(
                    (1, small_rows, features),
                    lambda i, starts: ((i >= first_passage).astype(jnp.int32), 0, 0),
                ),
            ],
            scratch_shapes=weight_scratch(stacked) + [
                pltpu.VMEM((block_tokens, features), jnp.float32),
                pltpu.VMEM((block_tokens, features), jnp.float32),
            ],
        ),
        compiler_params=pltpu.CompilerParams(
            dimension_semantics=("arbitrary",), vmem_limit_bytes=vmem_bytes
        ),
    )(
        starts, q_cot, p_cot, cls_grad, chances, stats, packed, context, n1, n2, slope,
        projection, mixing, expand, shrink, gains,
    )


def contrast_kernel(
    cls, positives, loss_weight, negatives,
    cls_grad, loss,
    q_all, p_all, stat_all, row_send, row_recv, col_send, col_recv, q_wide, q_low,
    q_ss, q_rs, p_ss, p_rs, stat_ss, stat_rs, row_ss, row_rs, col_ss, col_rs,
):
    size_pa, size_pb = lax.axis_size("pa"), lax.axis_size("pb")
    pa, pb = lax.axis_index("pa"), lax.axis_index("pb")
    features = cls.shape[1]
    half = features // 2
    own_q = q_all.shape[1] // 2
    own_p = p_all.shape[1]
    far_a = [(d, lax.rem(pa + d, size_pa)) for d in range(1, size_pa)]
    far_b = [(d, lax.rem(pb + d, size_pb)) for d in range(1, size_pb)]

    barrier = pltpu.get_barrier_semaphore()
    for _, a in far_a:
        pl.semaphore_signal(barrier, inc=1, device_id=(pb, a), device_id_type=MESH)
    for _, b in far_b:
        pl.semaphore_signal(barrier, inc=1, device_id=(b, pa), device_id_type=MESH)
    pl.semaphore_wait(barrier, size_pa + size_pb - 2)

    def to_a(src, dst, ss, rs, d, a):
        return pltpu.make_async_remote_copy(
            src_ref=src, dst_ref=dst, send_sem=ss.at[d], recv_sem=rs.at[d], device_id=(pb, a), device_id_type=MESH
        )

    def to_b(src, dst, ss, rs, d, b):
        return pltpu.make_async_remote_copy(
            src_ref=src, dst_ref=dst, send_sem=ss.at[d], recv_sem=rs.at[d], device_id=(b, pa), device_id_type=MESH
        )

    def fold(block):
        return jnp.concatenate([block[:, :half], block[:, half:]], axis=0).astype(jnp.bfloat16)

    q_all[pa] = fold(cls[:own_q, :])
    p_all[pb] = cls[own_q:, :].astype(jnp.bfloat16)
    copies = [to_a(q_all.at[pa], q_all.at[pa], q_ss, q_rs, d, a) for d, a in far_a]
    copies += [to_b(p_all.at[pb], p_all.at[pb], p_ss, p_rs, d, b) for d, b in far_b]
    for copy in copies:
        copy.start()
    for copy in copies:
        copy.wait()
    for a in range(size_pa):
        block = q_all[a].astype(jnp.float32)
        q_wide[pl.ds(a * own_q, own_q), :half] = block[:own_q]
        q_wide[pl.ds(a * own_q, own_q), half:] = block[own_q:]
    q_low[...] = q_wide[...].astype(jnp.bfloat16)

    tile_scale = 2.0 / math.sqrt(features)
    count = q_low.shape[0]
    p_rows = p_all[...].reshape(size_pb * own_p, features)
    row = lax.broadcasted_iota(jnp.int32, (size_pb * own_p, count), 0)
    slot = row % cls_slots
    valid = slot < cls_slots - 1
    place = row % own_p // cls_slots
    owner = row // own_p * size_pa + pa
    identity = (owner * (own_p // cls_slots) + place) * (cls_slots - 1) + slot
    chosen = jnp.where(valid & (identity == positives[...]), 1.0, 0.0)
    p_scores = dot_nt(p_rows, q_low[...]) * tile_scale
    p_scores = jnp.where(valid, p_scores, -1e30)
    n_scores = dot_nt(negatives[...], q_low[...]) * tile_scale
    top = jnp.maximum(
        jnp.max(p_scores, axis=0, keepdims=True), jnp.max(n_scores, axis=0, keepdims=True)
    )
    mass = jnp.sum(jnp.exp(p_scores - top), axis=0, keepdims=True)
    mass = mass + jnp.sum(jnp.exp(n_scores - top), axis=0, keepdims=True)
    picked = jnp.sum(jnp.where(chosen > 0.0, p_scores, 0.0), axis=0, keepdims=True)
    stat_all[pa] = jnp.concatenate([top, mass, picked] + [jnp.zeros_like(top)] * 5, axis=0)
    copies = [to_a(stat_all.at[pa], stat_all.at[pa], stat_ss, stat_rs, d, a) for d, a in far_a]
    for copy in copies:
        copy.start()
    for copy in copies:
        copy.wait()
    all_top = stat_all[0, 0:1]
    for a in range(1, size_pa):
        all_top = jnp.maximum(all_top, stat_all[a, 0:1])
    all_mass = jnp.zeros_like(all_top)
    all_picked = jnp.zeros_like(all_top)
    for a in range(size_pa):
        all_mass = all_mass + stat_all[a, 1:2] * jnp.exp(stat_all[a, 0:1] - all_top)
        all_picked = all_picked + stat_all[a, 2:3]
    logsum = all_top + jnp.log(all_mass)
    loss[...] = logsum - all_picked

    p_tile = (loss_weight[...] * (jnp.exp(p_scores - logsum) - chosen)).astype(jnp.bfloat16)
    n_tile = (loss_weight[...] * jnp.exp(n_scores - logsum)).astype(jnp.bfloat16)
    q_wide[...] = (dot_tn(p_tile, p_rows) + dot_tn(n_tile, negatives[...])) * tile_scale
    col_send[...] = (dot_nn(p_tile, q_low[...]) * tile_scale).reshape(col_send.shape)
    for a in range(size_pa):
        row_send[a] = fold(q_wide[pl.ds(a * own_q, own_q), :])
    copies = [to_a(row_send.at[a], row_recv.at[pa], row_ss, row_rs, d, a) for d, a in far_a]
    copies += [to_b(col_send.at[b], col_recv.at[pb], col_ss, col_rs, d, b) for d, b in far_b]
    for copy in copies:
        copy.start()
    for copy in copies:
        copy.wait()
    row_recv[pa] = row_send[pa]
    col_recv[pb] = col_send[pb]
    total = row_recv[0].astype(jnp.float32)
    for a in range(1, size_pa):
        total = total + row_recv[a].astype(jnp.float32)
    cls_grad[:own_q, :half] = total[:own_q]
    cls_grad[:own_q, half:] = total[own_q:]
    total = col_recv[0]
    for b in range(1, size_pb):
        total = total + col_recv[b]
    cls_grad[own_q:, :] = total


def contrast(cls, own_q, positives, loss_weight, negatives):
    size_pa, size_pb = lax.axis_size("pa"), lax.axis_size("pb")
    slots, features = cls.shape
    own_p, count = slots - own_q, positives.shape[0]
    low, dma = jnp.bfloat16, pltpu.SemaphoreType.DMA
    folded = (size_pa, 2 * own_q, features // 2)
    sems = [dma((size_pa,))] * 2 + [dma((size_pb,))] * 2 + [dma((size_pa,))] * 4 + [dma((size_pb,))] * 2
    cls_grad, loss = pl.pallas_call(
        contrast_kernel,
        out_shape=[
            jax.ShapeDtypeStruct(cls.shape, jnp.float32),
            jax.ShapeDtypeStruct((1, count), jnp.float32),
        ],
        in_specs=[pl.BlockSpec(memory_space=pltpu.VMEM)] * 4,
        out_specs=[pl.BlockSpec(memory_space=pltpu.VMEM)] * 2,
        scratch_shapes=[
            pltpu.VMEM(folded, low),
            pltpu.VMEM((size_pb, own_p, features), low),
            pltpu.VMEM((size_pa, 8, count), jnp.float32),
            pltpu.VMEM(folded, low),
            pltpu.VMEM(folded, low),
            pltpu.VMEM((size_pb, own_p, features), jnp.float32),
            pltpu.VMEM((size_pb, own_p, features), jnp.float32),
            pltpu.VMEM((count, features), jnp.float32),
            pltpu.VMEM((count, features), low),
        ] + sems,
        compiler_params=pltpu.CompilerParams(
            collective_id=2, has_side_effects=True, vmem_limit_bytes=vmem_bytes
        ),
    )(cls, positives[None, :], loss_weight[None, :], negatives)
    return cls_grad, loss[0]


panel_rows = 48
chunk_panels = 8
encoder_chunks = 9


def reduce_kernel(
    tokens,
    active, second, first, hidden, packed, context, branch, q_rows, p_rows,
    small_ref,
    out_ref, small_out,
    keep, core_send, core_recv, recv_x, recv_ya, recv_za, recv_yb, recv_zb, fin_a, fin_b,
    left_buf, left_t, right_buf, product, small_recv, small_sum,
    load_sem, core_ss, core_rs, xa_ss, xa_rs, ya_ss, ya_rs, za_ss, za_rs, ag_ss, ag_rs,
    yb_ss, yb_rs, zb_ss, zb_rs, xb_ss, xb_rs, small_ss, small_rs, credit,
):
    chunks = 2 * encoder_chunks
    pb, pa = lax.axis_index("pb"), lax.axis_index("pa")
    core, y, z, x = pa % 2, pa // 2 % 2, pa // 4, pb
    at_core = (pb, pa + 1 - 2 * core)
    at_y = (pb, pa + 2 - 4 * y)
    at_x = (1 - pb, pa)
    far_z = [(z + d) % 4 for d in (1, 2, 3)]
    at_z = [(pb, t * 4 + y * 2 + core) for t in far_z]

    barrier = pltpu.get_barrier_semaphore()
    for device in [at_core, at_y, at_x] + at_z:
        pl.semaphore_signal(barrier, inc=1, device_id=device, device_id_type=MESH)
    pl.semaphore_wait(barrier, 6)

    def remote(src, dst, ss, rs, device):
        return pltpu.make_async_remote_copy(
            src_ref=src, dst_ref=dst, send_sem=ss, recv_sem=rs, device_id=device, device_id_type=MESH
        )

    def copy_core(c):
        return remote(core_send.at[c % 2], core_recv.at[c % 3], core_ss.at[c], core_rs.at[c], at_core)

    def copy_xa(c):
        return remote(keep.at[c, pl.ds(2 * (1 - x), 2)], recv_x.at[c], xa_ss.at[c], xa_rs.at[c], at_x)

    def copy_ya(c):
        return remote(
            keep.at[c, pl.ds(2 * x, 2), :, 1 - y], recv_ya.at[c], ya_ss.at[c], ya_rs.at[c], at_y
        )

    def copy_za(c, d):
        return remote(
            keep.at[c, pl.ds(2 * x, 2), far_z[d], y], recv_za.at[c, d], za_ss.at[c, d], za_rs.at[c, d], at_z[d]
        )

    def copy_ag(c):
        half = fin_a.at[c, pl.ds(2 * x, 2)]
        return remote(half, half, ag_ss.at[c], ag_rs.at[c], at_x)

    def copy_yb(c):
        return remote(keep.at[c, pl.ds(4, 4), :, 1 - y], recv_yb.at[c], yb_ss.at[c], yb_rs.at[c], at_y)

    def copy_zb(c, d):
        return remote(
            keep.at[c, pl.ds(4, 4), far_z[d], y], recv_zb.at[c, d], zb_ss.at[c, d], zb_rs.at[c, d], at_z[d]
        )

    def copy_xb(c):
        return remote(fin_b.at[c, x], fin_b.at[c, x], xb_ss.at[c], xb_rs.at[c], at_x)

    def small_copy(stage, device):
        source = small_sum.at[max(stage - 3, 0) if stage >= 3 else stage]
        return remote(source, small_recv.at[stage], small_ss.at[stage], small_rs.at[stage], device)

    def own(e, ref):
        return ref.at[pl.ds(0 if e == 0 else tokens[0], tokens[e])]

    def left_loads(e, part):
        count = tokens[e]
        features = q_rows.shape[1]
        if part == 0:
            pairs = [(own(e, active), 0)]
        elif part == 1:
            pairs = [(own(e, first), 0)]
        else:
            pairs = [((q_rows, p_rows)[e], 0), (own(e, context), features)]
        return [
            pltpu.make_async_copy(
                ref,
                left_buf.at[pl.ds(0, count), pl.ds(at, ref.shape[1])],
                load_sem.at[2 + i],
            )
            for i, (ref, at) in enumerate(pairs)
        ]

    def right_loads(e, k):
        count = tokens[e]
        slot = (e * encoder_chunks + k) % 2
        if k < 3:
            pairs = [(second, 256 * k, 256, 0)]
        elif k < 6:
            pairs = [(hidden, 1024 * (k - 3), 1024, 0)]
        elif k < 8:
            pairs = [(packed, 1024 * (k - 6), 1024, 0)]
        else:
            pairs = [(packed, 2048, 256, 0), (branch, 0, 768, 256)]
        return [
            pltpu.make_async_copy(
                own(e, ref).at[:, pl.ds(start, width)],
                right_buf.at[slot, pl.ds(0, count), pl.ds(at, width)],
                load_sem.at[slot] if i == 0 else load_sem.at[4],
            )
            for i, (ref, start, width, at) in enumerate(pairs)
        ]

    def begin(copies):
        for copy in copies:
            copy.start()

    def finish(copies):
        for copy in copies:
            copy.wait()

    def transpose_left(e, part):
        count = tokens[e]
        width = (3072, 768, 1536)[part]

        def step(i, carry):
            at = pl.multiple_of(i * 256, 256)
            left_t[pl.ds(at, 256), pl.ds(0, count)] = left_buf[pl.ds(0, count), pl.ds(at, 256)].T
            return carry

        lax.fori_loop(0, width // 256, step, 0)

    def compute(e, k):
        count = tokens[e]
        c = e * encoder_chunks + k
        slot = c % 2

        def step(q, carry):
            if k < 3:
                rows_at, columns_at = q * 768, 0
            elif k < 8:
                rows_at, columns_at = 0, q * 256
            else:
                rows_at, columns_at = jnp.where(q > 0, 768, 0), q * 256
            rows_at = pl.multiple_of(rows_at, 256)
            columns_at = pl.multiple_of(columns_at, 256)
            product[...] = jnp.dot(
                left_t[pl.ds(rows_at, 768), pl.ds(0, count)],
                right_buf[slot, pl.ds(0, count), pl.ds(columns_at, 256)],
                preferred_element_type=jnp.float32,
            )
            if k < 3:
                for iy in range(2):
                    for sub in range(4):
                        for which, target in ((core, keep.at[c]), (1 - core, core_send.at[slot])):
                            at = pl.multiple_of((2 * iy + which) * 192 + sub * 48, 16)
                            block = product[pl.ds(at, 48), :].astype(jnp.bfloat16)
                            target[sub * 2, q, iy] = block[:, :lane]
                            target[sub * 2 + 1, q, iy] = block[:, lane:]
            else:
                for iz in range(4):
                    for iy in range(2):
                        for which, target in ((core, keep.at[c]), (1 - core, core_send.at[slot])):
                            at = pl.multiple_of((4 * iz + 2 * iy + which) * 48, 16)
                            block = product[pl.ds(at, 48), :].astype(jnp.bfloat16)
                            target[2 * q, iz, iy] = block[:, :lane]
                            target[2 * q + 1, iz, iy] = block[:, lane:]
            return carry

        lax.fori_loop(0, 4, step, 0)

    order = [(e, k) for e in range(2) for k in range(encoder_chunks)]
    part_of = lambda k: 0 if k < 3 else 1 if k < 6 else 2

    def produce(c):
        e, k = order[c]
        if c >= 2:
            copy_core(c - 2).wait_send()
        if k % 3 == 0:
            finish(left_loads(e, part_of(k)))
            transpose_left(e, part_of(k))
            if c + 3 < chunks:
                e2, k2 = order[c + 3]
                begin(left_loads(e2, part_of(k2)))
        finish(right_loads(e, k))
        if c + 1 < chunks:
            begin(right_loads(*order[c + 1]))
        compute(e, k)
        if c >= 3:
            pl.semaphore_wait(credit, 1)
        copy_core(c).start()

    def after_core(c):
        copy_core(c).wait_recv()

        def step(p, carry):
            keep[c, p] = keep[c, p] + core_recv[c % 3, p]
            return carry

        lax.fori_loop(0, chunk_panels, step, 0)
        copy_xa(c).start()
        copy_yb(c).start()

        @pl.when(c < chunks - 3)
        def _():
            pl.semaphore_signal(credit, inc=1, device_id=at_core, device_id_type=MESH)

    def after_first(c):
        copy_yb(c).wait_recv()

        def step_b(p, carry):
            for iz in range(4):
                keep[c, 4 + p, iz, y] = keep[c, 4 + p, iz, y] + recv_yb[c, p, iz]
            return carry

        lax.fori_loop(0, 4, step_b, 0)
        for d in range(3):
            copy_zb(c, d).start()
        copy_xa(c).wait_recv()

        def step_a(p, carry):
            keep[c, 2 * x + p] = keep[c, 2 * x + p] + recv_x[c, p]
            return carry

        lax.fori_loop(0, 2, step_a, 0)
        copy_ya(c).start()

    def widen(value):
        return value.astype(jnp.float32)

    def after_second(c):
        copy_ya(c).wait_recv()

        def step_a(p, carry):
            for iz in range(4):
                keep[c, 2 * x + p, iz, y] = keep[c, 2 * x + p, iz, y] + recv_ya[c, p, iz]
            return carry

        lax.fori_loop(0, 2, step_a, 0)
        for d in range(3):
            copy_za(c, d).start()
        for d in range(3):
            copy_zb(c, d).wait_recv()

        def step_b(p, carry):
            fin_b[c, x, p] = (
                widen(keep[c, 4 + p, z, y])
                + widen(recv_zb[c, 0, p])
                + widen(recv_zb[c, 1, p])
                + widen(recv_zb[c, 2, p])
            ).astype(jnp.bfloat16)
            return carry

        lax.fori_loop(0, 4, step_b, 0)
        copy_xb(c).start()

    def after_third(c):
        for d in range(3):
            copy_za(c, d).wait_recv()

        def step_a(p, carry):
            fin_a[c, 2 * x + p] = (
                widen(keep[c, 2 * x + p, z, y])
                + widen(recv_za[c, 0, p])
                + widen(recv_za[c, 1, p])
                + widen(recv_za[c, 2, p])
            ).astype(jnp.bfloat16)
            return carry

        lax.fori_loop(0, 2, step_a, 0)
        copy_ag(c).start()
        copy_xb(c).wait_recv()

        def step_b(p, carry):
            out_ref[c, 4 + p] = widen(fin_b[c, 0, p]) + widen(fin_b[c, 1, p])
            return carry

        lax.fori_loop(0, 4, step_b, 0)

    def after_last(c):
        copy_ag(c).wait_recv()

        def step(p, carry):
            out_ref[c, p] = widen(fin_a[c, p])
            return carry

        lax.fori_loop(0, 4, step, 0)

    begin(left_loads(0, 0))
    begin(right_loads(0, 0))
    small_sum[0] = small_ref[...]
    small_copy(0, at_core).start()
    for c in range(chunks + 5):
        if c < chunks:
            produce(c)
        if 0 <= c - 1 < chunks:
            after_core(c - 1)
        if 0 <= c - 2 < chunks:
            after_first(c - 2)
        if 0 <= c - 3 < chunks:
            after_second(c - 3)
        if 0 <= c - 4 < chunks:
            after_third(c - 4)
        if 0 <= c - 5 < chunks:
            after_last(c - 5)
        if c == 1:
            small_copy(0, at_core).wait_recv()
            small_sum[1] = small_sum[0] + small_recv[0]
            small_copy(1, at_x).start()
        if c == 2:
            small_copy(1, at_x).wait_recv()
            small_sum[2] = small_sum[1] + small_recv[1]
            small_copy(2, at_y).start()
        if c == 3:
            small_copy(2, at_y).wait_recv()
            small_sum[3] = small_sum[2] + small_recv[2]
            for d in range(3):
                remote(small_sum.at[3], small_recv.at[3 + d], small_ss.at[3 + d], small_rs.at[3 + d], at_z[d]).start()
        if c == 4:
            for d in range(3):
                remote(small_sum.at[3], small_recv.at[3 + d], small_ss.at[3 + d], small_rs.at[3 + d], at_z[d]).wait_recv()
            result = jnp.zeros_like(small_ref)
            for iz in range(4):
                back = (z - iz + 4) % 4
                value = jnp.where(back == 0, small_sum[3], 0.0)
                for d in range(3):
                    value = jnp.where(back == d + 1, small_recv[3 + d], value)
                result = result + value
            small_out[...] = result

    copy_core(chunks - 2).wait_send()
    copy_core(chunks - 1).wait_send()

    def drain(c, carry):
        copy_xa(c).wait_send()
        copy_ya(c).wait_send()
        copy_ag(c).wait_send()
        copy_yb(c).wait_send()
        copy_xb(c).wait_send()
        for d in range(3):
            copy_za(c, d).wait_send()
            copy_zb(c, d).wait_send()
        return carry

    lax.fori_loop(0, chunks, drain, 0)
    small_copy(0, at_core).wait_send()
    small_copy(1, at_x).wait_send()
    small_copy(2, at_y).wait_send()
    for d in range(3):
        remote(small_sum.at[3], small_recv.at[3 + d], small_ss.at[3 + d], small_rs.at[3 + d], at_z[d]).wait_send()


def reduce_by_kernel(operands, small):
    tokens = (operands[-2].shape[0], operands[-1].shape[0])
    most = max(tokens)
    chunks = 2 * encoder_chunks
    tile = (panel_rows, lane)
    low = jnp.bfloat16
    dma = pltpu.SemaphoreType.DMA
    one, three = dma((chunks,)), dma((chunks, 3))
    raw, small_total = pl.pallas_call(
        partial(reduce_kernel, tokens),
        out_shape=[
            jax.ShapeDtypeStruct((chunks, chunk_panels) + tile, jnp.float32),
            jax.ShapeDtypeStruct(small.shape, jnp.float32),
        ],
        in_specs=[pl.BlockSpec(memory_space=pl.ANY)] * 9 + [pl.BlockSpec(memory_space=pltpu.VMEM)],
        out_specs=[pl.BlockSpec(memory_space=pltpu.VMEM)] * 2,
        scratch_shapes=[
            pltpu.VMEM((chunks, chunk_panels, 4, 2) + tile, low),
            pltpu.VMEM((2, chunk_panels, 4, 2) + tile, low),
            pltpu.VMEM((3, chunk_panels, 4, 2) + tile, low),
            pltpu.VMEM((chunks, 2, 4, 2) + tile, low),
            pltpu.VMEM((chunks, 2, 4) + tile, low),
            pltpu.VMEM((chunks, 3, 2) + tile, low),
            pltpu.VMEM((chunks, 4, 4) + tile, low),
            pltpu.VMEM((chunks, 3, 4) + tile, low),
            pltpu.VMEM((chunks, 4) + tile, low),
            pltpu.VMEM((chunks, 2, 4) + tile, low),
            pltpu.VMEM((most, 3072), low),
            pltpu.VMEM((3072, most), low),
            pltpu.VMEM((2, most, 1024), low),
            pltpu.VMEM((768, 256), jnp.float32),
            pltpu.VMEM((6,) + small.shape, jnp.float32),
            pltpu.VMEM((4,) + small.shape, jnp.float32),
            dma((5,)),
            one, one, one, one, one, one, three, three, one, one,
            one, one, three, three, one, one, dma((6,)), dma((6,)),
            pltpu.SemaphoreType.REGULAR,
        ],
        compiler_params=pltpu.CompilerParams(
            collective_id=1, has_side_effects=True, vmem_limit_bytes=63 * 1024 * 1024
        ),
        cost_estimate=pl.CostEstimate(flops=22 * 10**9, bytes_accessed=60 * 10**6, transcendentals=0),
    )(*operands, small)
    raw = raw.reshape(2, encoder_chunks, chunk_panels, panel_rows, lane)
    shrink = raw[:, :3].reshape(2, 3, 4, 2, 48, lane).transpose(0, 2, 4, 1, 3, 5).reshape(2, 192, 768)
    expand = raw[:, 3:6].transpose(0, 3, 1, 2, 4).reshape(2, 48, 3072)
    rest = raw[:, 6:].transpose(0, 3, 1, 2, 4).reshape(2, 48, 3072)
    return rest[:, :, :2304], rest[:, :, 2304:], expand, shrink, small_total


def share_gradients(operands, small):
    size_pa, size_pb = lax.axis_size("pa"), lax.axis_size("pb")
    active, second, first, hidden, packed, context, branch, q_rows, p_rows = operands
    features = q_rows.shape[1]
    if size_pa == 16 and size_pb == 2:
        projection, mixing, expand, shrink, small = reduce_by_kernel(
            operands, small.reshape(-1, features)
        )
        small = small.reshape(2, -1, features)
    else:
        products = []
        cut = q_rows.shape[0]
        for rows, part in ((q_rows, slice(None, cut)), (p_rows, slice(cut, None))):
            pairs = ((rows, packed[part]), (context[part], branch[part]), (first[part], hidden[part]), (active[part], second[part]))
            products.append([contract_rows(*pair) for pair in pairs])
        projection, mixing, expand, shrink = (
            lax.psum(
                jnp.stack(
                    [
                        lax.psum_scatter(products[e][i], "pa", scatter_dimension=0, tiled=True)
                        for e in range(2)
                    ]
                ),
                "pb",
            )
            for i in range(4)
        )
        small = lax.psum(small, ("pb", "pa"))
    mine = lax.axis_index("pa")
    share = features // size_pa
    columns = lax.dynamic_slice_in_dim(small[:, :8], mine * share, share, 2)
    widening = small[:, 8:].reshape(2, -1)
    wide = widening.shape[1] // size_pa
    widening = lax.dynamic_slice_in_dim(widening, mine * wide, wide, 1)
    return (projection, mixing, expand, shrink, columns[:, :6], columns[:, 6:], widening)


def body(
    question_rows,
    passage_rows,
    segment_lengths,
    positives,
    negatives,
    question_cotangent,
    passage_cotangent,
    loss_weight,
    projection,
    mixing,
    expand,
    shrink,
    biases,
    gains,
    widening,
):
    stacked = (projection, mixing, expand, shrink, biases, gains, widening)
    question_count, question_length, features = question_rows.shape
    passage_count, passage_length = (passage_rows.shape[0], passage_rows.shape[1])
    per_block = block_tokens // question_length
    q_rows = question_rows.reshape(-1, features)
    p_rows = passage_rows.reshape(-1, features)
    question_starts = jnp.broadcast_to(
        jnp.arange(cls_slots, dtype=jnp.int32) * question_length, (question_count // per_block, cls_slots)
    )
    passage_ends = jnp.cumsum(segment_lengths, axis=-1, dtype=jnp.int32)
    passage_starts = jnp.concatenate([jnp.zeros_like(passage_ends[:, :1]), passage_ends], axis=1)
    starts = jnp.concatenate([question_starts, passage_starts])
    q_states, p_states, cls, *saved = encode_all(starts, q_rows, p_rows, stacked)
    cls_grad, question_loss = contrast(cls, question_count, positives, loss_weight, negatives)
    q_grad, p_grad, second, hidden, branch, packed_grad, small = encode_all_back(
        starts,
        question_cotangent.reshape(-1, features),
        passage_cotangent.reshape(-1, features),
        cls_grad,
        saved,
        stacked,
    )
    chances, stats, packed, context, first, n1, n2, active, slope = saved
    totals = share_gradients(
        (active, second, first, hidden, packed_grad, context, branch, q_rows, p_rows), small
    )
    return (
        q_states.reshape(question_rows.shape),
        p_states.reshape(passage_rows.shape),
        question_loss,
        q_grad.reshape(question_rows.shape),
        p_grad.reshape(passage_rows.shape),
    ) + totals


def solution(mesh):
    return jax.shard_map(
        body,
        mesh=mesh,
        in_specs=(
            P(("pb", "pa"), None, None),
            P(("pb", "pa"), None, None),
            P(("pb", "pa"), None),
            P("pb"),
            P("pa", None),
            P(("pb", "pa"), None, None),
            P(("pb", "pa"), None, None),
            P("pb"),
            P(),
            P(),
            P(),
            P(),
            P(),
            P(),
            P(),
        ),
        out_specs=(
            P(("pb", "pa"), None, None),
            P(("pb", "pa"), None, None),
            P("pb"),
            P(("pb", "pa"), None, None),
            P(("pb", "pa"), None, None),
            P(None, "pa", None),
            P(None, "pa", None),
            P(None, "pa", None),
            P(None, "pa", None),
            P(None, None, "pa"),
            P(None, None, "pa"),
            P(None, "pa"),
        ),
        check_vma=False,
    )
```

```python
from functools import partial
import math

import jax
import jax.numpy as jnp
from jax import lax
from jax.experimental import pallas as pl
from jax.experimental.pallas import tpu as pltpu
from jax.sharding import PartitionSpec as P

HEADS = 12
HEAD_DIM = 64


eps_norm = 1e-12
masked_score = -1000000000.0


def matmul(left_side, right_side):
    return jnp.dot(left_side, right_side, preferred_element_type=jnp.float32)


def contract_rows(left_side, right_side):
    return lax.dot_general(
        left_side, right_side, (((0,), (0,)), ((), ())), preferred_element_type=jnp.float32
    )


def contract_cols(left_side, right_side):
    return lax.dot_general(
        left_side, right_side, (((1,), (1,)), ((), ())), preferred_element_type=jnp.float32
    )


MESH = pl.DeviceIdType.MESH
lane = 128
block_tokens = 256
cls_slots = 4
stat_first, stat_final = 0, 1
vmem_bytes = 63 * 1024 * 1024


def dot_nn(left_side, right_side):
    return jnp.dot(left_side, right_side, preferred_element_type=jnp.float32)


def dot_nt(left_side, right_side):
    return lax.dot_general(
        left_side, right_side, (((1,), (1,)), ((), ())), preferred_element_type=jnp.float32
    )


def dot_tn(left_side, right_side):
    return lax.dot_general(
        left_side, right_side, (((0,), (0,)), ((), ())), preferred_element_type=jnp.float32
    )


def gelu_and_slope(hidden):
    size = jnp.abs(hidden)
    t = pl.reciprocal(1.0 + (0.3275911 * math.sqrt(0.5)) * size, approx=True)
    bell = jnp.exp2((hidden * hidden) * (-0.5 * math.log2(math.e)))
    tail = (0.5 * 1.061405429) * t - (0.5 * 1.453152027)
    tail = tail * t + (0.5 * 1.421413741)
    tail = tail * t - (0.5 * 0.284496736)
    tail = (tail * t + (0.5 * 0.254829592)) * (t * bell)
    below = jnp.where(hidden < 0.0, tail, 1.0 - tail)
    return hidden * below, below + (hidden * bell) * (1.0 / math.sqrt(2.0 * math.pi))


def normalize(values):
    centre = values - jnp.mean(values, axis=-1, keepdims=True)
    inverse = lax.rsqrt(jnp.mean(centre * centre, axis=-1, keepdims=True) + eps_norm)
    return centre * inverse, inverse


def normalize_back(gradient, normal, inverse, gain_row):
    scaled = gradient * gain_row
    inner_mean = jnp.mean(scaled, axis=-1, keepdims=True)
    projected = jnp.mean(scaled * normal, axis=-1, keepdims=True)
    return inverse * (scaled - inner_mean - normal * projected)


def head_pair(packed_ref, pair, features):
    return [packed_ref[:, pl.ds(j * features + pair * lane, lane)] for j in range(3)]


def side_mask(side, scale):
    at = lax.broadcasted_iota(jnp.int32, (1, lane), 1) // HEAD_DIM
    return jnp.where(at == side, scale, 0.0).astype(jnp.bfloat16)


def start_of(lengths, i, first_passage, k):
    row = jnp.maximum(i - first_passage, 0)
    at = 0
    for j in range(k):
        at = at + lengths[row, j]
    return jnp.where(i < first_passage, k * (block_tokens // cls_slots), at)


class Weights:
    def __init__(self, sources, buffers, sems, step, first_passage, order):
        self.sources, self.buffers, self.sems, self.order = sources, buffers, sems, order
        self.step, self.first_passage = step, first_passage
        self.encoder = (step >= first_passage).astype(jnp.int32)

    def copy(self, which, e):
        return pltpu.make_async_copy(
            self.sources[which].at[e], self.buffers[which].at[e], self.sems.at[which, e]
        )

    def begin(self):
        for e, at in ((0, 0), (1, self.first_passage - 1)):

            @pl.when(self.step == at)
            def _():
                for which in self.order:
                    self.copy(which, e).start()

    def get(self, which):
        for e, at in ((0, 0), (1, self.first_passage)):

            @pl.when(self.step == at)
            def _():
                self.copy(which, e).wait()

        return self.buffers[which].at[self.encoder]


def forward_kernel(
    first_passage,
    lengths,
    q_rows, p_rows, projection, mixing, expand, shrink, biases, gains, widening,
    q_states, p_states, cls, chances, stats, packed_ref, context_ref, first_ref, n1_ref, n2_ref,
    active_ref, slope_ref,
    w0, w1, w2, w3, sems, final_buf, x_buf,
):
    i = pl.program_id(0)
    weights = Weights((projection, mixing, expand, shrink), (w0, w1, w2, w3), sems, i, first_passage, (0, 1, 2, 3))
    weights.begin()
    e = weights.encoder
    features = q_rows.shape[1]
    shifts = biases[e].astype(jnp.float32)
    gain_rows = gains[e].astype(jnp.float32)
    both = widening[...].astype(jnp.float32)
    wide_shift = jnp.where(e == 0, both[0:1], both[1:2])
    x_buf[...] = jnp.where(i < first_passage, q_rows[...], p_rows[...])

    weight = weights.get(0)
    x_low = x_buf[...]
    for part in range(3):
        columns = pl.ds(part * features, features)
        value = dot_nn(x_low, weight[:, columns])
        if part != 1:
            value = value + shifts[part // 2 : part // 2 + 1]
        packed_ref[:, columns] = value.astype(jnp.bfloat16)

    tokens = q_rows.shape[0]
    row_at = lax.broadcasted_iota(jnp.int32, (tokens, tokens), 0)
    col_at = lax.broadcasted_iota(jnp.int32, (tokens, tokens), 1)
    starts = [start_of(lengths, i, first_passage, k) for k in range(cls_slots)]
    row_segment = jnp.zeros_like(row_at)
    col_segment = jnp.zeros_like(col_at)
    for k in range(1, cls_slots):
        row_segment = row_segment + (row_at >= starts[k]).astype(jnp.int32)
        col_segment = col_segment + (col_at >= starts[k]).astype(jnp.int32)
    penalty = jnp.where(row_segment == col_segment, 0.0, masked_score)
    def scores_of(pair):
        queries, keys, _ = head_pair(packed_ref, pair, features)
        both = [keys * side_mask(side, HEAD_DIM ** (-0.5)) for side in range(2)]
        return dot_nt(jnp.concatenate(both), queries)

    def chances_of(pair, scores):
        result = []
        for side in range(2):
            part = scores[side * tokens : (side + 1) * tokens] + penalty
            chance = jnp.exp(part - jnp.max(part, axis=0, keepdims=True))
            inverse = 1.0 / jnp.sum(chance, axis=0, keepdims=True)
            result.append((chance * inverse).astype(jnp.bfloat16))
            chances[0, 2 * pair + side] = result[side]
        return result

    def mix(pair, both):
        values_t = head_pair(packed_ref, pair, features)[2].T
        mixed = [
            dot_nn(values_t[side * HEAD_DIM : (side + 1) * HEAD_DIM], both[side])
            for side in range(2)
        ]
        context_ref[:, pl.ds(pair * lane, lane)] = jnp.concatenate(mixed).astype(jnp.bfloat16).T

    pairs = HEADS // 2
    scores, both = {}, {}
    for step in range(pairs + 2):
        if step < pairs:
            scores[step] = scores_of(step)
        if step >= 2:
            mix(step - 2, both.pop(step - 2))
        if 1 <= step <= pairs:
            both[step - 1] = chances_of(step - 1, scores.pop(step - 1))
    lanes = lax.broadcasted_iota(jnp.int32, stats.shape, 1)

    weight = weights.get(1)
    branch = dot_nn(context_ref[...], weight[...]) + shifts[2:3]
    normal, inverse = normalize(x_buf[...].astype(jnp.float32) + branch)
    n1_ref[...] = normal.astype(jnp.bfloat16)
    first_inverse = inverse
    first = normal * gain_rows[0:1] + shifts[3:4]
    first_low = first.astype(jnp.bfloat16)
    first_ref[...] = first_low
    final_buf[...] = first

    up, down = weights.get(2), weights.get(3)
    second = jnp.broadcast_to(shifts[4:5], (tokens, features))
    tile = 512

    def raised(j):
        columns = pl.ds(j * tile, tile)
        return dot_nn(first_low, up[:, columns]) + wide_shift[:, j * tile : (j + 1) * tile]

    ahead = raised(0)
    for j in range(up.shape[1] // tile):
        columns = pl.ds(j * tile, tile)
        hidden = ahead
        if (j + 1) * tile < up.shape[1]:
            ahead = raised(j + 1)
        active, slope = gelu_and_slope(hidden)
        active_low = active.astype(jnp.bfloat16)
        active_ref[:, columns] = active_low
        slope_ref[:, columns] = slope.astype(jnp.bfloat16)
        second = second + dot_nn(active_low, down[columns, :])

    normal, inverse = normalize(final_buf[...] + second)
    n2_ref[...] = normal.astype(jnp.bfloat16)
    stats[...] = jnp.where(lanes == stat_final, inverse, first_inverse)
    final = normal * gain_rows[1:2] + shifts[5:6]
    final_buf[...] = final

    @pl.when(i < first_passage)
    def _():
        q_states[...] = final.astype(jnp.bfloat16)

    @pl.when(i >= first_passage)
    def _():
        p_states[...] = final.astype(jnp.bfloat16)

    for k in range(cls_slots):
        at = jnp.minimum(starts[k], tokens - 1)
        cls[pl.ds(i * cls_slots + k, 1), :] = final_buf[pl.ds(at, 1), :]


def backward_kernel(
    first_passage,
    lengths,
    q_cot, p_cot, cls_grad, chances, stats, packed_ref, context_ref, n1_ref, n2_ref, slope_ref,
    projection, mixing, expand, shrink, gains,
    q_grad, p_grad, second_ref, hidden_ref, branch_ref, packed_grad, small,
    w0, w1, w2, w3, sems, total_buf, context_grad,
):
    i = pl.program_id(0)
    weights = Weights((projection, mixing, expand, shrink), (w0, w1, w2, w3), sems, i, first_passage, (3, 2, 1, 0))
    weights.begin()
    e = weights.encoder
    tokens, features = q_cot.shape
    gain_rows = gains[e].astype(jnp.float32)

    @pl.when((i == 0) | (i == first_passage))
    def _():
        small[...] = jnp.zeros_like(small)

    def add_small(row, value):
        small[0, pl.ds(row, 1), :] += jnp.sum(value, axis=0, keepdims=True)

    gradient = jnp.where(i < first_passage, q_cot[...], p_cot[...]).astype(jnp.float32)
    row_at = lax.broadcasted_iota(jnp.int32, (tokens, 1), 0)
    for k in range(cls_slots):
        gradient = gradient + jnp.where(row_at == start_of(lengths, i, first_passage, k), cls_grad[pl.ds(i * cls_slots + k, 1), :], 0.0)
    normal = n2_ref[...].astype(jnp.float32)
    add_small(5, gradient)
    add_small(7, gradient * normal)
    total_grad = normalize_back(
        gradient, normal, stats[:, stat_final : stat_final + 1], gain_rows[1:2]
    )
    total_buf[...] = total_grad
    second_low = total_grad.astype(jnp.bfloat16)
    second_ref[...] = second_low
    add_small(4, second_low.astype(jnp.float32))

    down, up = weights.get(3), weights.get(2)
    first_grad = total_buf[...]
    for j in range(up.shape[1] // features):
        columns = pl.ds(j * features, features)
        hidden_grad = dot_nt(second_low, down[columns, :]) * slope_ref[:, columns].astype(jnp.float32)
        hidden_low = hidden_grad.astype(jnp.bfloat16)
        hidden_ref[:, columns] = hidden_low
        add_small(8 + j, hidden_low.astype(jnp.float32))
        first_grad = first_grad + dot_nt(hidden_low, up[:, columns])

    normal = n1_ref[...].astype(jnp.float32)
    add_small(3, first_grad)
    add_small(6, first_grad * normal)
    branch_grad = normalize_back(
        first_grad, normal, stats[:, stat_first : stat_first + 1], gain_rows[0:1]
    )
    total_buf[...] = branch_grad
    branch_low = branch_grad.astype(jnp.bfloat16)
    branch_ref[...] = branch_low
    add_small(2, branch_low.astype(jnp.float32))
    weight = weights.get(1)
    mixed_grad = dot_nt(branch_low, weight[...])
    context_grad[...] = mixed_grad.astype(jnp.bfloat16)

    heads = lax.broadcasted_iota(jnp.int32, (16, features), 0)
    of_head = lax.broadcasted_iota(jnp.int32, (16, features), 1) // HEAD_DIM == heads
    of_head = jnp.where(of_head, 1.0, 0.0).astype(jnp.bfloat16)
    inner = mixed_grad * context_ref[...].astype(jnp.float32)
    inner_high = inner.astype(jnp.bfloat16)
    inner_low = (inner - inner_high.astype(jnp.float32)).astype(jnp.bfloat16)
    inner = dot_nt(of_head, inner_high) + dot_nt(of_head, inner_low)
    left_side = lax.broadcasted_iota(jnp.int32, (tokens, lane), 1) < HEAD_DIM
    def weight_grads(pair):
        values = head_pair(packed_ref, pair, features)[2]
        both = [values * side_mask(side, 1.0) for side in range(2)]
        return dot_nt(jnp.concatenate(both), context_grad[:, pl.ds(pair * lane, lane)])

    def score_grads(pair, weight_grad):
        result = []
        for side in range(2):
            h = 2 * pair + side
            part = weight_grad[side * tokens : (side + 1) * tokens] - inner[h : h + 1]
            result.append((chances[0, h].astype(jnp.float32) * part).astype(jnp.bfloat16))
        return result

    def head_grads(pair, score_low):
        queries, keys, _ = head_pair(packed_ref, pair, features)
        mixed_low = context_grad[:, pl.ds(pair * lane, lane)]
        keys_t = keys.T
        query_grad = [
            dot_nn(keys_t[side * HEAD_DIM : (side + 1) * HEAD_DIM], score_low[side])
            for side in range(2)
        ]
        key_grad = dot_nn(jnp.concatenate(score_low), queries)
        value_grad = dot_nn(chances[0, 2 * pair : 2 * pair + 2].reshape(2 * tokens, tokens), mixed_low)
        scale = HEAD_DIM ** (-0.5)
        for j, value in enumerate(
            (
                (jnp.concatenate(query_grad) * scale).astype(jnp.bfloat16).T,
                (jnp.where(left_side, key_grad[:tokens], key_grad[tokens:]) * scale).astype(jnp.bfloat16),
                jnp.where(left_side, value_grad[:tokens], value_grad[tokens:]).astype(jnp.bfloat16),
            )
        ):
            packed_grad[:, pl.ds(j * features + pair * lane, lane)] = value

    pairs = HEADS // 2
    raw, low_grads = {}, {}
    for step in range(pairs + 2):
        if step < pairs:
            raw[step] = weight_grads(step)
        if step >= 2:
            head_grads(step - 2, low_grads.pop(step - 2))
        if 1 <= step <= pairs:
            low_grads[step - 1] = score_grads(step - 1, raw.pop(step - 1))
    add_small(0, packed_grad[:, :features].astype(jnp.float32))
    add_small(1, packed_grad[:, 2 * features :].astype(jnp.float32))

    weight = weights.get(0)
    input_grad = total_buf[...] + dot_nt(packed_grad[...], weight[...])

    @pl.when(i < first_passage)
    def _():
        q_grad[...] = input_grad

    @pl.when(i >= first_passage)
    def _():
        p_grad[...] = input_grad


def block_specs(first_passage):
    q_at = lambda i, lengths: (jnp.minimum(i, first_passage - 1), 0)
    p_at = lambda i, lengths: (jnp.maximum(i - first_passage, 0), 0)
    at = lambda i, lengths: (i, 0)

    def rows(width, index=at):
        return pl.BlockSpec((block_tokens, width), index)

    def lead(*shape):
        return pl.BlockSpec((1,) + shape, lambda i, lengths: (i,) + (0,) * len(shape))

    def whole(array):
        return pl.BlockSpec(array.shape, lambda i, lengths: (0,) * array.ndim)

    anywhere = pl.BlockSpec(memory_space=pl.ANY)
    return q_at, p_at, rows, lead, whole, anywhere


def weight_scratch(stacked):
    return [pltpu.VMEM(w.shape, w.dtype) for w in stacked[:4]] + [pltpu.SemaphoreType.DMA((4, 2))]


def encode_all(lengths, q_rows, p_rows, stacked):
    projection, mixing, expand, shrink, biases, gains, widening = stacked
    features, wide = projection.shape[1], expand.shape[2]
    first_passage = q_rows.shape[0] // block_tokens
    blocks = first_passage + lengths.shape[0]
    q_at, p_at, rows, lead, whole, anywhere = block_specs(first_passage)
    low, tokens = jnp.bfloat16, blocks * block_tokens
    shape = jax.ShapeDtypeStruct
    return pl.pallas_call(
        partial(forward_kernel, first_passage),
        out_shape=[
            shape(q_rows.shape, low), shape(p_rows.shape, low),
            shape((blocks * cls_slots, features), jnp.float32),
            shape((blocks, HEADS, block_tokens, block_tokens), low),
            shape((tokens, lane), jnp.float32),
            shape((tokens, 3 * features), low),
            shape((tokens, features), low), shape((tokens, features), low),
            shape((tokens, features), low), shape((tokens, features), low),
            shape((tokens, wide), low), shape((tokens, wide), low),
        ],
        grid_spec=pltpu.PrefetchScalarGridSpec(
            num_scalar_prefetch=1,
            grid=(blocks,),
            in_specs=[
                rows(features, q_at), rows(features, p_at), anywhere, anywhere, anywhere, anywhere,
                whole(biases), whole(gains), whole(widening),
            ],
            out_specs=[
                rows(features, q_at), rows(features, p_at),
                pl.BlockSpec((blocks * cls_slots, features), lambda i, lengths: (0, 0)),
                lead(HEADS, block_tokens, block_tokens), rows(lane), rows(3 * features),
                rows(features), rows(features), rows(features), rows(features), rows(wide), rows(wide),
            ],
            scratch_shapes=weight_scratch(stacked) + [
                pltpu.VMEM((block_tokens, features), jnp.float32),
                pltpu.VMEM((block_tokens, features), low),
            ],
        ),
        compiler_params=pltpu.CompilerParams(
            dimension_semantics=("arbitrary",), vmem_limit_bytes=vmem_bytes
        ),
    )(lengths, q_rows, p_rows, projection, mixing, expand, shrink, biases, gains, widening)


def encode_all_back(lengths, q_cot, p_cot, cls_grad, saved, stacked):
    projection, mixing, expand, shrink, biases, gains, widening = stacked
    chances, stats, packed, context, first, n1, n2, active, slope = saved
    features, wide = projection.shape[1], expand.shape[2]
    first_passage = q_cot.shape[0] // block_tokens
    blocks = first_passage + lengths.shape[0]
    q_at, p_at, rows, lead, whole, anywhere = block_specs(first_passage)
    low, tokens = jnp.bfloat16, blocks * block_tokens
    shape = jax.ShapeDtypeStruct
    small_rows = 8 + wide // features
    return pl.pallas_call(
        partial(backward_kernel, first_passage),
        out_shape=[
            shape(q_cot.shape, jnp.float32), shape(p_cot.shape, jnp.float32),
            shape((tokens, features), low), shape((tokens, wide), low),
            shape((tokens, features), low), shape((tokens, 3 * features), low),
            shape((2, small_rows, features), jnp.float32),
        ],
        grid_spec=pltpu.PrefetchScalarGridSpec(
            num_scalar_prefetch=1,
            grid=(blocks,),
            in_specs=[
                rows(features, q_at), rows(features, p_at), whole(cls_grad),
                lead(HEADS, block_tokens, block_tokens), rows(lane), rows(3 * features),
                rows(features), rows(features), rows(features), rows(wide),
                anywhere, anywhere, anywhere, anywhere, whole(gains),
            ],
            out_specs=[
                rows(features, q_at), rows(features, p_at), rows(features), rows(wide),
                rows(features), rows(3 * features),
                pl.BlockSpec(
                    (1, small_rows, features),
                    lambda i, lengths: ((i >= first_passage).astype(jnp.int32), 0, 0),
                ),
            ],
            scratch_shapes=weight_scratch(stacked) + [
                pltpu.VMEM((block_tokens, features), jnp.float32),
                pltpu.VMEM((block_tokens, features), low),
            ],
        ),
        compiler_params=pltpu.CompilerParams(
            dimension_semantics=("arbitrary",), vmem_limit_bytes=vmem_bytes
        ),
    )(
        lengths, q_cot, p_cot, cls_grad, chances, stats, packed, context, n1, n2, slope,
        projection, mixing, expand, shrink, gains,
    )


def contrast_kernel(
    cls, positives, loss_weight, negatives,
    cls_grad, loss,
    q_all, p_all, stat_all, row_send, row_recv, col_send, col_recv, q_wide, q_low,
    q_ss, q_rs, p_ss, p_rs, stat_ss, stat_rs, row_ss, row_rs, col_ss, col_rs,
):
    size_pa, size_pb = lax.axis_size("pa"), lax.axis_size("pb")
    pa, pb = lax.axis_index("pa"), lax.axis_index("pb")
    features = cls.shape[1]
    half = features // 2
    own_q = q_all.shape[1] // 2
    own_p = p_all.shape[1]
    far_a = [(d, lax.rem(pa + d, size_pa)) for d in range(1, size_pa)]
    far_b = [(d, lax.rem(pb + d, size_pb)) for d in range(1, size_pb)]

    barrier = pltpu.get_barrier_semaphore()
    for _, a in far_a:
        pl.semaphore_signal(barrier, inc=1, device_id=(pb, a), device_id_type=MESH)
    for _, b in far_b:
        pl.semaphore_signal(barrier, inc=1, device_id=(b, pa), device_id_type=MESH)
    pl.semaphore_wait(barrier, size_pa + size_pb - 2)

    def to_a(src, dst, ss, rs, d, a):
        return pltpu.make_async_remote_copy(
            src_ref=src, dst_ref=dst, send_sem=ss.at[d], recv_sem=rs.at[d], device_id=(pb, a), device_id_type=MESH
        )

    def to_b(src, dst, ss, rs, d, b):
        return pltpu.make_async_remote_copy(
            src_ref=src, dst_ref=dst, send_sem=ss.at[d], recv_sem=rs.at[d], device_id=(b, pa), device_id_type=MESH
        )

    def fold(block):
        return jnp.concatenate([block[:, :half], block[:, half:]], axis=0).astype(jnp.bfloat16)

    q_all[pa] = fold(cls[:own_q, :])
    p_all[pb] = cls[own_q:, :].astype(jnp.bfloat16)
    copies = [to_a(q_all.at[pa], q_all.at[pa], q_ss, q_rs, d, a) for d, a in far_a]
    copies += [to_b(p_all.at[pb], p_all.at[pb], p_ss, p_rs, d, b) for d, b in far_b]
    for copy in copies:
        copy.start()
    for copy in copies:
        copy.wait()
    for a in range(size_pa):
        block = q_all[a].astype(jnp.float32)
        q_wide[pl.ds(a * own_q, own_q), :half] = block[:own_q]
        q_wide[pl.ds(a * own_q, own_q), half:] = block[own_q:]
    q_low[...] = q_wide[...].astype(jnp.bfloat16)

    tile_scale = 2.0 / math.sqrt(features)
    count = q_low.shape[0]
    p_rows = p_all[...].reshape(size_pb * own_p, features)
    row = lax.broadcasted_iota(jnp.int32, (size_pb * own_p, count), 0)
    slot = row % cls_slots
    valid = slot < cls_slots - 1
    place = row % own_p // cls_slots
    owner = row // own_p * size_pa + pa
    identity = (owner * (own_p // cls_slots) + place) * (cls_slots - 1) + slot
    chosen = jnp.where(valid & (identity == positives[...]), 1.0, 0.0)
    p_scores = dot_nt(p_rows, q_low[...]) * tile_scale
    p_scores = jnp.where(valid, p_scores, -1e30)
    n_scores = dot_nt(negatives[...], q_low[...]) * tile_scale
    top = jnp.maximum(
        jnp.max(p_scores, axis=0, keepdims=True), jnp.max(n_scores, axis=0, keepdims=True)
    )
    mass = jnp.sum(jnp.exp(p_scores - top), axis=0, keepdims=True)
    mass = mass + jnp.sum(jnp.exp(n_scores - top), axis=0, keepdims=True)
    picked = jnp.sum(jnp.where(chosen > 0.0, p_scores, 0.0), axis=0, keepdims=True)
    stat_all[pa] = jnp.concatenate([top, mass, picked] + [jnp.zeros_like(top)] * 5, axis=0)
    copies = [to_a(stat_all.at[pa], stat_all.at[pa], stat_ss, stat_rs, d, a) for d, a in far_a]
    for copy in copies:
        copy.start()
    for copy in copies:
        copy.wait()
    all_top = stat_all[0, 0:1]
    for a in range(1, size_pa):
        all_top = jnp.maximum(all_top, stat_all[a, 0:1])
    all_mass = jnp.zeros_like(all_top)
    all_picked = jnp.zeros_like(all_top)
    for a in range(size_pa):
        all_mass = all_mass + stat_all[a, 1:2] * jnp.exp(stat_all[a, 0:1] - all_top)
        all_picked = all_picked + stat_all[a, 2:3]
    logsum = all_top + jnp.log(all_mass)
    loss[...] = logsum - all_picked

    p_tile = (loss_weight[...] * (jnp.exp(p_scores - logsum) - chosen)).astype(jnp.bfloat16)
    n_tile = (loss_weight[...] * jnp.exp(n_scores - logsum)).astype(jnp.bfloat16)
    q_wide[...] = (dot_tn(p_tile, p_rows) + dot_tn(n_tile, negatives[...])) * tile_scale
    col_send[...] = (dot_nn(p_tile, q_low[...]) * tile_scale).reshape(col_send.shape)
    for a in range(size_pa):
        row_send[a] = fold(q_wide[pl.ds(a * own_q, own_q), :])
    copies = [to_a(row_send.at[a], row_recv.at[pa], row_ss, row_rs, d, a) for d, a in far_a]
    copies += [to_b(col_send.at[b], col_recv.at[pb], col_ss, col_rs, d, b) for d, b in far_b]
    for copy in copies:
        copy.start()
    for copy in copies:
        copy.wait()
    row_recv[pa] = row_send[pa]
    col_recv[pb] = col_send[pb]
    total = row_recv[0].astype(jnp.float32)
    for a in range(1, size_pa):
        total = total + row_recv[a].astype(jnp.float32)
    cls_grad[:own_q, :half] = total[:own_q]
    cls_grad[:own_q, half:] = total[own_q:]
    total = col_recv[0]
    for b in range(1, size_pb):
        total = total + col_recv[b]
    cls_grad[own_q:, :] = total


def contrast(cls, own_q, positives, loss_weight, negatives):
    size_pa, size_pb = lax.axis_size("pa"), lax.axis_size("pb")
    slots, features = cls.shape
    own_p, count = slots - own_q, positives.shape[0]
    low, dma = jnp.bfloat16, pltpu.SemaphoreType.DMA
    folded = (size_pa, 2 * own_q, features // 2)
    sems = [dma((size_pa,))] * 2 + [dma((size_pb,))] * 2 + [dma((size_pa,))] * 4 + [dma((size_pb,))] * 2
    cls_grad, loss = pl.pallas_call(
        contrast_kernel,
        out_shape=[
            jax.ShapeDtypeStruct(cls.shape, jnp.float32),
            jax.ShapeDtypeStruct((1, count), jnp.float32),
        ],
        in_specs=[pl.BlockSpec(memory_space=pltpu.VMEM)] * 4,
        out_specs=[pl.BlockSpec(memory_space=pltpu.VMEM)] * 2,
        scratch_shapes=[
            pltpu.VMEM(folded, low),
            pltpu.VMEM((size_pb, own_p, features), low),
            pltpu.VMEM((size_pa, 8, count), jnp.float32),
            pltpu.VMEM(folded, low),
            pltpu.VMEM(folded, low),
            pltpu.VMEM((size_pb, own_p, features), jnp.float32),
            pltpu.VMEM((size_pb, own_p, features), jnp.float32),
            pltpu.VMEM((count, features), jnp.float32),
            pltpu.VMEM((count, features), low),
        ] + sems,
        compiler_params=pltpu.CompilerParams(
            collective_id=2, has_side_effects=True, vmem_limit_bytes=vmem_bytes
        ),
    )(cls, positives[None, :], loss_weight[None, :], negatives)
    return cls_grad, loss[0]


panel_rows = 48
chunk_panels = 8
encoder_chunks = 9


def reduce_kernel(
    tokens,
    active, second, first, hidden, packed, context, branch, q_rows, p_rows,
    small_ref,
    projection_out, mixing_out, expand_out, shrink_out, small_out,
    keep, core_send, core_recv, recv_x, recv_ya, recv_za, recv_yb, recv_zb, fin_a, fin_b,
    left_buf, left_t, right_buf, product, small_recv, small_sum,
    load_sem, core_ss, core_rs, xa_ss, xa_rs, ya_ss, ya_rs, za_ss, za_rs, ag_ss, ag_rs,
    yb_ss, yb_rs, zb_ss, zb_rs, xb_ss, xb_rs, small_ss, small_rs, credit,
):
    chunks = 2 * encoder_chunks
    pb, pa = lax.axis_index("pb"), lax.axis_index("pa")
    core, y, z, x = pa % 2, pa // 2 % 2, pa // 4, pb
    at_core = (pb, pa + 1 - 2 * core)
    at_y = (pb, pa + 2 - 4 * y)
    at_x = (1 - pb, pa)
    far_z = [(z + d) % 4 for d in (1, 2, 3)]
    at_z = [(pb, t * 4 + y * 2 + core) for t in far_z]

    barrier = pltpu.get_barrier_semaphore()
    for device in [at_core, at_y, at_x] + at_z:
        pl.semaphore_signal(barrier, inc=1, device_id=device, device_id_type=MESH)
    pl.semaphore_wait(barrier, 6)

    def remote(src, dst, ss, rs, device):
        return pltpu.make_async_remote_copy(
            src_ref=src, dst_ref=dst, send_sem=ss, recv_sem=rs, device_id=device, device_id_type=MESH
        )

    def copy_core(c):
        return remote(core_send.at[c % 2], core_recv.at[c % 3], core_ss.at[c], core_rs.at[c], at_core)

    def copy_xa(c):
        return remote(keep.at[c, pl.ds(2 * (1 - x), 2)], recv_x.at[c], xa_ss.at[c], xa_rs.at[c], at_x)

    def copy_ya(c):
        return remote(
            keep.at[c, pl.ds(2 * x, 2), :, 1 - y], recv_ya.at[c], ya_ss.at[c], ya_rs.at[c], at_y
        )

    def copy_za(c, d):
        return remote(
            keep.at[c, pl.ds(2 * x, 2), far_z[d], y], recv_za.at[c, d], za_ss.at[c, d], za_rs.at[c, d], at_z[d]
        )

    def copy_ag(c):
        half = fin_a.at[c, pl.ds(2 * x, 2)]
        return remote(half, half, ag_ss.at[c], ag_rs.at[c], at_x)

    def copy_yb(c):
        return remote(keep.at[c, pl.ds(4, 4), :, 1 - y], recv_yb.at[c], yb_ss.at[c], yb_rs.at[c], at_y)

    def copy_zb(c, d):
        return remote(
            keep.at[c, pl.ds(4, 4), far_z[d], y], recv_zb.at[c, d], zb_ss.at[c, d], zb_rs.at[c, d], at_z[d]
        )

    def copy_xb(c):
        return remote(fin_b.at[c, x], fin_b.at[c, x], xb_ss.at[c], xb_rs.at[c], at_x)

    def small_copy(stage, device):
        source = small_sum.at[max(stage - 3, 0) if stage >= 3 else stage]
        return remote(source, small_recv.at[stage], small_ss.at[stage], small_rs.at[stage], device)

    def own(e, ref):
        return ref.at[pl.ds(0 if e == 0 else tokens[0], tokens[e])]

    def left_loads(e, part):
        count = tokens[e]
        features = q_rows.shape[1]
        if part == 0:
            pairs = [(own(e, active), 0)]
        elif part == 1:
            pairs = [(own(e, first), 0)]
        else:
            pairs = [((q_rows, p_rows)[e], 0), (own(e, context), features)]
        return [
            pltpu.make_async_copy(
                ref,
                left_buf.at[pl.ds(0, count), pl.ds(at, ref.shape[1])],
                load_sem.at[2 + i],
            )
            for i, (ref, at) in enumerate(pairs)
        ]

    def right_loads(e, k):
        count = tokens[e]
        slot = (e * encoder_chunks + k) % 2
        if k < 3:
            pairs = [(second, 256 * k, 256, 0)]
        elif k < 6:
            pairs = [(hidden, 1024 * (k - 3), 1024, 0)]
        elif k < 8:
            pairs = [(packed, 1024 * (k - 6), 1024, 0)]
        else:
            pairs = [(packed, 2048, 256, 0), (branch, 0, 768, 256)]
        return [
            pltpu.make_async_copy(
                own(e, ref).at[:, pl.ds(start, width)],
                right_buf.at[slot, pl.ds(0, count), pl.ds(at, width)],
                load_sem.at[slot] if i == 0 else load_sem.at[4],
            )
            for i, (ref, start, width, at) in enumerate(pairs)
        ]

    def begin(copies):
        for copy in copies:
            copy.start()

    def finish(copies):
        for copy in copies:
            copy.wait()

    def transpose_left(e, part):
        count = tokens[e]
        width = (3072, 768, 1536)[part]

        def step(i, carry):
            at = pl.multiple_of(i * 256, 256)
            left_t[pl.ds(at, 256), pl.ds(0, count)] = left_buf[pl.ds(0, count), pl.ds(at, 256)].T
            return carry

        lax.fori_loop(0, width // 256, step, 0)

    def compute(e, k):
        count = tokens[e]
        c = e * encoder_chunks + k
        slot = c % 2

        def step(q, carry):
            if k < 3:
                rows_at, columns_at = q * 768, 0
            elif k < 8:
                rows_at, columns_at = 0, q * 256
            else:
                rows_at, columns_at = jnp.where(q > 0, 768, 0), q * 256
            rows_at = pl.multiple_of(rows_at, 256)
            columns_at = pl.multiple_of(columns_at, 256)
            product[...] = jnp.dot(
                left_t[pl.ds(rows_at, 768), pl.ds(0, count)],
                right_buf[slot, pl.ds(0, count), pl.ds(columns_at, 256)],
                preferred_element_type=jnp.float32,
            )
            if k < 3:
                for iy in range(2):
                    for sub in range(4):
                        for which, target in ((core, keep.at[c]), (1 - core, core_send.at[slot])):
                            at = pl.multiple_of((2 * iy + which) * 192 + sub * 48, 16)
                            block = product[pl.ds(at, 48), :].astype(jnp.bfloat16)
                            target[sub * 2, q, iy] = block[:, :lane]
                            target[sub * 2 + 1, q, iy] = block[:, lane:]
            else:
                for iz in range(4):
                    for iy in range(2):
                        for which, target in ((core, keep.at[c]), (1 - core, core_send.at[slot])):
                            at = pl.multiple_of((4 * iz + 2 * iy + which) * 48, 16)
                            block = product[pl.ds(at, 48), :].astype(jnp.bfloat16)
                            target[2 * q, iz, iy] = block[:, :lane]
                            target[2 * q + 1, iz, iy] = block[:, lane:]
            return carry

        lax.fori_loop(0, 4, step, 0)

    order = [(e, k) for e in range(2) for k in range(encoder_chunks)]
    part_of = lambda k: 0 if k < 3 else 1 if k < 6 else 2

    def produce(c):
        e, k = order[c]
        if c >= 2:
            copy_core(c - 2).wait_send()
        if k % 3 == 0:
            finish(left_loads(e, part_of(k)))
            transpose_left(e, part_of(k))
            if c + 3 < chunks:
                e2, k2 = order[c + 3]
                begin(left_loads(e2, part_of(k2)))
        finish(right_loads(e, k))
        if c + 1 < chunks:
            begin(right_loads(*order[c + 1]))
        compute(e, k)
        if c >= 3:
            pl.semaphore_wait(credit, 1)
        copy_core(c).start()

    def write(c, panel, value):
        e, k = order[c]
        if k < 3:
            rows = pl.ds(panel // 2 * panel_rows, panel_rows)
            shrink_out[e, rows, pl.ds(256 * k + panel % 2 * lane, lane)] = value
        elif k < 6:
            expand_out[e, :, pl.ds(1024 * (k - 3) + panel * lane, lane)] = value
        else:
            at = 1024 * (k - 6) + panel * lane
            width = projection_out.shape[2]
            if at < width:
                projection_out[e, :, pl.ds(at, lane)] = value
            else:
                mixing_out[e, :, pl.ds(at - width, lane)] = value

    def after_core(c):
        copy_core(c).wait_recv()

        def step(p, carry):
            keep[c, p] = keep[c, p] + core_recv[c % 3, p]
            return carry

        lax.fori_loop(0, chunk_panels, step, 0)
        copy_xa(c).start()
        copy_yb(c).start()

        @pl.when(c < chunks - 3)
        def _():
            pl.semaphore_signal(credit, inc=1, device_id=at_core, device_id_type=MESH)

    def after_first(c):
        copy_yb(c).wait_recv()

        def step_b(p, carry):
            for iz in range(4):
                keep[c, 4 + p, iz, y] = keep[c, 4 + p, iz, y] + recv_yb[c, p, iz]
            return carry

        lax.fori_loop(0, 4, step_b, 0)
        for d in range(3):
            copy_zb(c, d).start()
        copy_xa(c).wait_recv()

        def step_a(p, carry):
            keep[c, 2 * x + p] = keep[c, 2 * x + p] + recv_x[c, p]
            return carry

        lax.fori_loop(0, 2, step_a, 0)
        copy_ya(c).start()

    def widen(value):
        return value.astype(jnp.float32)

    def after_second(c):
        copy_ya(c).wait_recv()

        def step_a(p, carry):
            for iz in range(4):
                keep[c, 2 * x + p, iz, y] = keep[c, 2 * x + p, iz, y] + recv_ya[c, p, iz]
            return carry

        lax.fori_loop(0, 2, step_a, 0)
        for d in range(3):
            copy_za(c, d).start()
        for d in range(3):
            copy_zb(c, d).wait_recv()

        def step_b(p, carry):
            fin_b[c, x, p] = (
                widen(keep[c, 4 + p, z, y])
                + widen(recv_zb[c, 0, p])
                + widen(recv_zb[c, 1, p])
                + widen(recv_zb[c, 2, p])
            ).astype(jnp.bfloat16)
            return carry

        lax.fori_loop(0, 4, step_b, 0)
        copy_xb(c).start()

    def after_third(c):
        for d in range(3):
            copy_za(c, d).wait_recv()

        def step_a(p, carry):
            fin_a[c, 2 * x + p] = (
                widen(keep[c, 2 * x + p, z, y])
                + widen(recv_za[c, 0, p])
                + widen(recv_za[c, 1, p])
                + widen(recv_za[c, 2, p])
            ).astype(jnp.bfloat16)
            return carry

        lax.fori_loop(0, 2, step_a, 0)
        copy_ag(c).start()
        copy_xb(c).wait_recv()

        for p in range(4):
            write(c, 4 + p, widen(fin_b[c, 0, p]) + widen(fin_b[c, 1, p]))

    def after_last(c):
        copy_ag(c).wait_recv()

        for p in range(4):
            write(c, p, widen(fin_a[c, p]))

    begin(left_loads(0, 0))
    begin(right_loads(0, 0))
    small_sum[0] = small_ref[...]
    small_copy(0, at_core).start()
    for c in range(chunks + 5):
        if c < chunks:
            produce(c)
        if 0 <= c - 1 < chunks:
            after_core(c - 1)
        if 0 <= c - 2 < chunks:
            after_first(c - 2)
        if 0 <= c - 3 < chunks:
            after_second(c - 3)
        if 0 <= c - 4 < chunks:
            after_third(c - 4)
        if 0 <= c - 5 < chunks:
            after_last(c - 5)
        if c == 1:
            small_copy(0, at_core).wait_recv()
            small_sum[1] = small_sum[0] + small_recv[0]
            small_copy(1, at_x).start()
        if c == 2:
            small_copy(1, at_x).wait_recv()
            small_sum[2] = small_sum[1] + small_recv[1]
            small_copy(2, at_y).start()
        if c == 3:
            small_copy(2, at_y).wait_recv()
            small_sum[3] = small_sum[2] + small_recv[2]
            for d in range(3):
                remote(small_sum.at[3], small_recv.at[3 + d], small_ss.at[3 + d], small_rs.at[3 + d], at_z[d]).start()
        if c == 4:
            for d in range(3):
                remote(small_sum.at[3], small_recv.at[3 + d], small_ss.at[3 + d], small_rs.at[3 + d], at_z[d]).wait_recv()
            result = jnp.zeros_like(small_ref)
            for iz in range(4):
                back = (z - iz + 4) % 4
                value = jnp.where(back == 0, small_sum[3], 0.0)
                for d in range(3):
                    value = jnp.where(back == d + 1, small_recv[3 + d], value)
                result = result + value
            small_out[...] = result

    copy_core(chunks - 2).wait_send()
    copy_core(chunks - 1).wait_send()

    def drain(c, carry):
        copy_xa(c).wait_send()
        copy_ya(c).wait_send()
        copy_ag(c).wait_send()
        copy_yb(c).wait_send()
        copy_xb(c).wait_send()
        for d in range(3):
            copy_za(c, d).wait_send()
            copy_zb(c, d).wait_send()
        return carry

    lax.fori_loop(0, chunks, drain, 0)
    small_copy(0, at_core).wait_send()
    small_copy(1, at_x).wait_send()
    small_copy(2, at_y).wait_send()
    for d in range(3):
        remote(small_sum.at[3], small_recv.at[3 + d], small_ss.at[3 + d], small_rs.at[3 + d], at_z[d]).wait_send()


def reduce_by_kernel(operands, small):
    tokens = (operands[-2].shape[0], operands[-1].shape[0])
    most = max(tokens)
    chunks = 2 * encoder_chunks
    tile = (panel_rows, lane)
    low = jnp.bfloat16
    dma = pltpu.SemaphoreType.DMA
    one, three = dma((chunks,)), dma((chunks, 3))
    shape = jax.ShapeDtypeStruct
    return pl.pallas_call(
        partial(reduce_kernel, tokens),
        out_shape=[
            shape((2, 48, 2304), jnp.float32),
            shape((2, 48, 768), jnp.float32),
            shape((2, 48, 3072), jnp.float32),
            shape((2, 192, 768), jnp.float32),
            shape(small.shape, jnp.float32),
        ],
        in_specs=[pl.BlockSpec(memory_space=pl.ANY)] * 9 + [pl.BlockSpec(memory_space=pltpu.VMEM)],
        out_specs=[pl.BlockSpec(memory_space=pltpu.VMEM)] * 5,
        scratch_shapes=[
            pltpu.VMEM((chunks, chunk_panels, 4, 2) + tile, low),
            pltpu.VMEM((2, chunk_panels, 4, 2) + tile, low),
            pltpu.VMEM((3, chunk_panels, 4, 2) + tile, low),
            pltpu.VMEM((chunks, 2, 4, 2) + tile, low),
            pltpu.VMEM((chunks, 2, 4) + tile, low),
            pltpu.VMEM((chunks, 3, 2) + tile, low),
            pltpu.VMEM((chunks, 4, 4) + tile, low),
            pltpu.VMEM((chunks, 3, 4) + tile, low),
            pltpu.VMEM((chunks, 4) + tile, low),
            pltpu.VMEM((chunks, 2, 4) + tile, low),
            pltpu.VMEM((most, 3072), low),
            pltpu.VMEM((3072, most), low),
            pltpu.VMEM((2, most, 1024), low),
            pltpu.VMEM((768, 256), jnp.float32),
            pltpu.VMEM((6,) + small.shape, jnp.float32),
            pltpu.VMEM((4,) + small.shape, jnp.float32),
            dma((5,)),
            one, one, one, one, one, one, three, three, one, one,
            one, one, three, three, one, one, dma((6,)), dma((6,)),
            pltpu.SemaphoreType.REGULAR,
        ],
        compiler_params=pltpu.CompilerParams(
            collective_id=1, has_side_effects=True, vmem_limit_bytes=63 * 1024 * 1024
        ),
        cost_estimate=pl.CostEstimate(flops=22 * 10**9, bytes_accessed=60 * 10**6, transcendentals=0),
    )(*operands, small)


def share_gradients(operands, small):
    size_pa, size_pb = lax.axis_size("pa"), lax.axis_size("pb")
    active, second, first, hidden, packed, context, branch, q_rows, p_rows = operands
    features = q_rows.shape[1]
    if size_pa == 16 and size_pb == 2:
        projection, mixing, expand, shrink, small = reduce_by_kernel(
            operands, small.reshape(-1, features)
        )
        small = small.reshape(2, -1, features)
    else:
        products = []
        cut = q_rows.shape[0]
        for rows, part in ((q_rows, slice(None, cut)), (p_rows, slice(cut, None))):
            pairs = ((rows, packed[part]), (context[part], branch[part]), (first[part], hidden[part]), (active[part], second[part]))
            products.append([contract_rows(*pair) for pair in pairs])
        projection, mixing, expand, shrink = (
            lax.psum(
                jnp.stack(
                    [
                        lax.psum_scatter(products[e][i], "pa", scatter_dimension=0, tiled=True)
                        for e in range(2)
                    ]
                ),
                "pb",
            )
            for i in range(4)
        )
        small = lax.psum(small, ("pb", "pa"))
    mine = lax.axis_index("pa")
    share = features // size_pa
    columns = lax.dynamic_slice_in_dim(small[:, :8], mine * share, share, 2)
    widening = small[:, 8:].reshape(2, -1)
    wide = widening.shape[1] // size_pa
    widening = lax.dynamic_slice_in_dim(widening, mine * wide, wide, 1)
    return (projection, mixing, expand, shrink, columns[:, :6], columns[:, 6:], widening)


def body(
    question_rows,
    passage_rows,
    segment_lengths,
    positives,
    negatives,
    question_cotangent,
    passage_cotangent,
    loss_weight,
    projection,
    mixing,
    expand,
    shrink,
    biases,
    gains,
    widening,
):
    stacked = (projection, mixing, expand, shrink, biases, gains, widening)
    question_count, _, features = question_rows.shape
    q_rows = question_rows.reshape(-1, features)
    p_rows = passage_rows.reshape(-1, features)
    q_states, p_states, cls, *saved = encode_all(segment_lengths, q_rows, p_rows, stacked)
    cls_grad, question_loss = contrast(cls, question_count, positives, loss_weight, negatives)
    q_grad, p_grad, second, hidden, branch, packed_grad, small = encode_all_back(
        segment_lengths,
        question_cotangent.reshape(-1, features),
        passage_cotangent.reshape(-1, features),
        cls_grad,
        saved,
        stacked,
    )
    chances, stats, packed, context, first, n1, n2, active, slope = saved
    totals = share_gradients(
        (active, second, first, hidden, packed_grad, context, branch, q_rows, p_rows), small
    )
    return (
        q_states.reshape(question_rows.shape),
        p_states.reshape(passage_rows.shape),
        question_loss,
        q_grad.reshape(question_rows.shape),
        p_grad.reshape(passage_rows.shape),
    ) + totals


def solution(mesh):
    return jax.shard_map(
        body,
        mesh=mesh,
        in_specs=(
            P(("pb", "pa"), None, None),
            P(("pb", "pa"), None, None),
            P(("pb", "pa"), None),
            P("pb"),
            P("pa", None),
            P(("pb", "pa"), None, None),
            P(("pb", "pa"), None, None),
            P("pb"),
            P(),
            P(),
            P(),
            P(),
            P(),
            P(),
            P(),
        ),
        out_specs=(
            P(("pb", "pa"), None, None),
            P(("pb", "pa"), None, None),
            P("pb"),
            P(("pb", "pa"), None, None),
            P(("pb", "pa"), None, None),
            P(None, "pa", None),
            P(None, "pa", None),
            P(None, "pa", None),
            P(None, "pa", None),
            P(None, None, "pa"),
            P(None, None, "pa"),
            P(None, "pa"),
        ),
        check_vma=False,
    )
```

```python
from functools import partial
import math

import jax
import jax.numpy as jnp
from jax import lax
from jax.experimental import pallas as pl
from jax.experimental.pallas import tpu as pltpu
from jax.sharding import PartitionSpec as P

HEADS = 12
HEAD_DIM = 64


eps_norm = 1e-12
masked_score = -1000000000.0


def matmul(left_side, right_side):
    return jnp.dot(left_side, right_side, preferred_element_type=jnp.float32)


def contract_rows(left_side, right_side):
    return lax.dot_general(
        left_side, right_side, (((0,), (0,)), ((), ())), preferred_element_type=jnp.float32
    )


def contract_cols(left_side, right_side):
    return lax.dot_general(
        left_side, right_side, (((1,), (1,)), ((), ())), preferred_element_type=jnp.float32
    )


MESH = pl.DeviceIdType.MESH
lane = 128
block_tokens = 256
cls_slots = 4
stat_first, stat_final = 0, 1
vmem_bytes = 63 * 1024 * 1024


def dot_nn(left_side, right_side):
    return jnp.dot(left_side, right_side, preferred_element_type=jnp.float32)


def dot_nt(left_side, right_side):
    return lax.dot_general(
        left_side, right_side, (((1,), (1,)), ((), ())), preferred_element_type=jnp.float32
    )


def dot_tn(left_side, right_side):
    return lax.dot_general(
        left_side, right_side, (((0,), (0,)), ((), ())), preferred_element_type=jnp.float32
    )


def gelu_and_slope(hidden):
    size = jnp.abs(hidden)
    t = pl.reciprocal(1.0 + (0.3275911 * math.sqrt(0.5)) * size, approx=True)
    bell = jnp.exp2((hidden * hidden) * (-0.5 * math.log2(math.e)))
    tail = (0.5 * 1.061405429) * t - (0.5 * 1.453152027)
    tail = tail * t + (0.5 * 1.421413741)
    tail = tail * t - (0.5 * 0.284496736)
    tail = (tail * t + (0.5 * 0.254829592)) * (t * bell)
    below = jnp.where(hidden < 0.0, tail, 1.0 - tail)
    return hidden * below, below + (hidden * bell) * (1.0 / math.sqrt(2.0 * math.pi))


def normalize(values):
    centre = values - jnp.mean(values, axis=-1, keepdims=True)
    inverse = lax.rsqrt(jnp.mean(centre * centre, axis=-1, keepdims=True) + eps_norm)
    return centre * inverse, inverse


def normalize_back(gradient, normal, inverse, gain_row):
    scaled = gradient * gain_row
    inner_mean = jnp.mean(scaled, axis=-1, keepdims=True)
    projected = jnp.mean(scaled * normal, axis=-1, keepdims=True)
    return inverse * (scaled - inner_mean - normal * projected)


def head_pair(packed_ref, pair, features):
    return [packed_ref[:, pl.ds(j * features + pair * lane, lane)] for j in range(3)]


def side_mask(side, scale):
    at = lax.broadcasted_iota(jnp.int32, (1, lane), 1) // HEAD_DIM
    return jnp.where(at == side, scale, 0.0).astype(jnp.bfloat16)


def start_of(lengths, i, first_passage, k):
    row = jnp.maximum(i - first_passage, 0)
    at = 0
    for j in range(k):
        at = at + lengths[row, j]
    return jnp.where(i < first_passage, k * (block_tokens // cls_slots), at)


class Weights:
    def __init__(self, sources, buffers, sems, step, first_passage, order, passages=True):
        self.sources, self.buffers, self.sems, self.order = sources, buffers, sems, order
        self.step, self.first_passage = step, first_passage
        self.encoder = (step >= first_passage).astype(jnp.int32)
        self.parts = ((0, 0), (1, first_passage))[: 1 + passages]
        self.seen = set()

    def copy(self, which, e):
        return pltpu.make_async_copy(
            self.sources[which].at[e], self.buffers[which].at[e], self.sems.at[which, e]
        )

    def begin(self):
        for e, at in self.parts:

            @pl.when(self.step == max(at - 1, 0))
            def _():
                for which in self.order:
                    self.copy(which, e).start()

    def get(self, which):
        if which not in self.seen:
            self.seen.add(which)
            for e, at in self.parts:

                @pl.when(self.step == at)
                def _():
                    self.copy(which, e).wait()

        return self.buffers[which].at[self.encoder]


def forward_kernel(
    first_passage,
    lengths,
    q_rows, p_rows, projection, mixing, expand, shrink, biases, gains, widening,
    q_states, p_states, cls, chances, stats, packed_ref, context_ref, first_ref, n1_ref, n2_ref,
    active_ref, slope_ref,
    w0, w1, w2, w3, sems, final_buf, x_buf,
):
    i = pl.program_id(0)
    weights = Weights((projection, mixing, expand, shrink), (w0, w1, w2, w3), sems, i, first_passage, (0, 1, 2, 3))
    weights.begin()
    e = weights.encoder
    features = q_rows.shape[1]
    shifts = biases[e].astype(jnp.float32)
    gain_rows = gains[e].astype(jnp.float32)
    both = widening[...].astype(jnp.float32)
    wide_shift = jnp.where(e == 0, both[0:1], both[1:2])
    x_buf[...] = jnp.where(i < first_passage, q_rows[...], p_rows[...])

    weight = weights.get(0)
    x_low = x_buf[...]
    for part in range(3):
        columns = pl.ds(part * features, features)
        value = dot_nn(x_low, weight[:, columns])
        if part != 1:
            value = value + shifts[part // 2 : part // 2 + 1]
        packed_ref[:, columns] = value.astype(jnp.bfloat16)

    tokens = q_rows.shape[0]
    row_at = lax.broadcasted_iota(jnp.int32, (tokens, tokens), 0)
    col_at = lax.broadcasted_iota(jnp.int32, (tokens, tokens), 1)
    starts = [start_of(lengths, i, first_passage, k) for k in range(cls_slots)]
    row_segment = jnp.zeros_like(row_at)
    col_segment = jnp.zeros_like(col_at)
    for k in range(1, cls_slots):
        row_segment = row_segment + (row_at >= starts[k]).astype(jnp.int32)
        col_segment = col_segment + (col_at >= starts[k]).astype(jnp.int32)
    penalty = jnp.where(row_segment == col_segment, 0.0, masked_score)
    def scores_of(pair):
        queries, keys, _ = head_pair(packed_ref, pair, features)
        both = [keys * side_mask(side, HEAD_DIM ** (-0.5)) for side in range(2)]
        return dot_nt(jnp.concatenate(both), queries)

    def chances_of(pair, scores):
        result = []
        for side in range(2):
            part = scores[side * tokens : (side + 1) * tokens] + penalty
            chance = jnp.exp(part - jnp.max(part, axis=0, keepdims=True))
            inverse = 1.0 / jnp.sum(chance, axis=0, keepdims=True)
            result.append((chance * inverse).astype(jnp.bfloat16))
            chances[0, 2 * pair + side] = result[side]
        return result

    def mix(pair, both):
        values_t = head_pair(packed_ref, pair, features)[2].T
        mixed = [
            dot_nn(values_t[side * HEAD_DIM : (side + 1) * HEAD_DIM], both[side])
            for side in range(2)
        ]
        context_ref[:, pl.ds(pair * lane, lane)] = jnp.concatenate(mixed).astype(jnp.bfloat16).T

    pairs = HEADS // 2
    scores, both = {}, {}
    for step in range(pairs + 2):
        if step < pairs:
            scores[step] = scores_of(step)
        if step >= 2:
            mix(step - 2, both.pop(step - 2))
        if 1 <= step <= pairs:
            both[step - 1] = chances_of(step - 1, scores.pop(step - 1))
    lanes = lax.broadcasted_iota(jnp.int32, stats.shape, 1)

    weight = weights.get(1)
    branch = dot_nn(context_ref[...], weight[...]) + shifts[2:3]
    normal, inverse = normalize(x_buf[...].astype(jnp.float32) + branch)
    n1_ref[...] = normal.astype(jnp.bfloat16)
    first_inverse = inverse
    first = normal * gain_rows[0:1] + shifts[3:4]
    first_low = first.astype(jnp.bfloat16)
    first_ref[...] = first_low
    final_buf[...] = first

    up, down = weights.get(2), weights.get(3)
    second = jnp.broadcast_to(shifts[4:5], (tokens, features))
    tile = 512

    def raised(j):
        columns = pl.ds(j * tile, tile)
        return dot_nn(first_low, up[:, columns]) + wide_shift[:, j * tile : (j + 1) * tile]

    ahead = raised(0)
    for j in range(up.shape[1] // tile):
        columns = pl.ds(j * tile, tile)
        hidden = ahead
        if (j + 1) * tile < up.shape[1]:
            ahead = raised(j + 1)
        active, slope = gelu_and_slope(hidden)
        active_low = active.astype(jnp.bfloat16)
        active_ref[:, columns] = active_low
        slope_ref[:, columns] = slope.astype(jnp.bfloat16)
        second = second + dot_nn(active_low, down[columns, :])

    normal, inverse = normalize(final_buf[...] + second)
    n2_ref[...] = normal.astype(jnp.bfloat16)
    stats[...] = jnp.where(lanes == stat_final, inverse, first_inverse)
    final = normal * gain_rows[1:2] + shifts[5:6]
    final_buf[...] = final

    @pl.when(i < first_passage)
    def _():
        q_states[...] = final.astype(jnp.bfloat16)

    @pl.when(i >= first_passage)
    def _():
        p_states[...] = final.astype(jnp.bfloat16)

    for k in range(cls_slots):
        at = jnp.minimum(starts[k], tokens - 1)
        cls[pl.ds(i * cls_slots + k, 1), :] = final_buf[pl.ds(at, 1), :]


class Back:
    def __init__(self, **refs):
        self.__dict__.update(refs)

    def add_small(self, row, value):
        self.small[pl.ds(row, 1), :] += jnp.sum(value, axis=0, keepdims=True)

    def part_a(self):
        gradient = self.gradient()
        normal = self.n2[...].astype(jnp.float32)
        self.add_small(5, gradient)
        self.add_small(7, gradient * normal)
        total_grad = normalize_back(
            gradient, normal, self.stats[:, stat_final : stat_final + 1], self.gain_rows[1:2]
        )
        second_low = total_grad.astype(jnp.bfloat16)
        self.second[...] = second_low
        self.add_small(4, second_low.astype(jnp.float32))
        self.total[...] = total_grad
        self.feed_forward(0, 2)

    def feed_forward(self, begin, end):
        down, up = self.weight(3), self.weight(2)
        features = self.total.shape[1]
        second_low = self.second[...]
        first_grad = self.total[...]
        for j in range(begin, end):
            columns = pl.ds(j * features, features)
            hidden_grad = dot_nt(second_low, down[columns, :]) * self.slope[:, columns].astype(jnp.float32)
            hidden_low = hidden_grad.astype(jnp.bfloat16)
            self.hidden[:, columns] = hidden_low
            self.add_small(8 + j, hidden_low.astype(jnp.float32))
            first_grad = first_grad + dot_nt(hidden_low, up[:, columns])
        self.total[...] = first_grad

    def part_b(self):
        features = self.total.shape[1]
        self.feed_forward(2, self.hidden.shape[1] // features)
        first_grad = self.total[...]
        normal = self.n1[...].astype(jnp.float32)
        self.add_small(3, first_grad)
        self.add_small(6, first_grad * normal)
        branch_grad = normalize_back(
            first_grad, normal, self.stats[:, stat_first : stat_first + 1], self.gain_rows[0:1]
        )
        self.total[...] = branch_grad
        branch_low = branch_grad.astype(jnp.bfloat16)
        self.branch[...] = branch_low
        self.add_small(2, branch_low.astype(jnp.float32))
        mixed_grad = dot_nt(branch_low, self.weight(1)[...])
        self.mixed[...] = mixed_grad.astype(jnp.bfloat16)
        heads = lax.broadcasted_iota(jnp.int32, (16, features), 0)
        of_head = lax.broadcasted_iota(jnp.int32, (16, features), 1) // HEAD_DIM == heads
        of_head = jnp.where(of_head, 1.0, 0.0).astype(jnp.bfloat16)
        inner = mixed_grad * self.context[...].astype(jnp.float32)
        inner_high = inner.astype(jnp.bfloat16)
        inner_low = (inner - inner_high.astype(jnp.float32)).astype(jnp.bfloat16)
        self.inner[...] = dot_nt(of_head, inner_high) + dot_nt(of_head, inner_low)

    def part_c(self):
        packed_ref, mixed, chances = self.packed, self.mixed, self.chances
        tokens, features = mixed.shape
        inner = self.inner[...]
        left_side = lax.broadcasted_iota(jnp.int32, (tokens, lane), 1) < HEAD_DIM

        def weight_grads(pair):
            values = head_pair(packed_ref, pair, features)[2]
            both = [values * side_mask(side, 1.0) for side in range(2)]
            return dot_nt(jnp.concatenate(both), mixed[:, pl.ds(pair * lane, lane)])

        def score_grads(pair, weight_grad):
            result = []
            for side in range(2):
                h = 2 * pair + side
                part = weight_grad[side * tokens : (side + 1) * tokens] - inner[h : h + 1]
                result.append((chances[h].astype(jnp.float32) * part).astype(jnp.bfloat16))
            return result

        def head_grads(pair, score_low):
            queries, keys, _ = head_pair(packed_ref, pair, features)
            mixed_low = mixed[:, pl.ds(pair * lane, lane)]
            keys_t = keys.T
            query_grad = [
                dot_nn(keys_t[side * HEAD_DIM : (side + 1) * HEAD_DIM], score_low[side])
                for side in range(2)
            ]
            key_grad = dot_nn(jnp.concatenate(score_low), queries)
            both = chances[2 * pair : 2 * pair + 2].reshape(2 * tokens, tokens)
            value_grad = dot_nn(both, mixed_low)
            scale = HEAD_DIM ** (-0.5)
            for j, value in enumerate(
                (
                    (jnp.concatenate(query_grad) * scale).astype(jnp.bfloat16).T,
                    (jnp.where(left_side, key_grad[:tokens], key_grad[tokens:]) * scale).astype(jnp.bfloat16),
                    jnp.where(left_side, value_grad[:tokens], value_grad[tokens:]).astype(jnp.bfloat16),
                )
            ):
                self.packed_grad[:, pl.ds(j * features + pair * lane, lane)] = value

        pairs = HEADS // 2
        raw, low_grads = {}, {}
        for step in range(pairs + 2):
            if step < pairs:
                raw[step] = weight_grads(step)
            if step >= 2:
                head_grads(step - 2, low_grads.pop(step - 2))
            if 1 <= step <= pairs:
                low_grads[step - 1] = score_grads(step - 1, raw.pop(step - 1))

    def part_d(self):
        features = self.total.shape[1]
        self.add_small(0, self.packed_grad[:, :features].astype(jnp.float32))
        self.add_small(1, self.packed_grad[:, 2 * features :].astype(jnp.float32))
        return self.total[...] + dot_nt(self.packed_grad[...], self.weight(0)[...])


def with_cls(gradient, starts, cls_grad, first_row):
    row_at = lax.broadcasted_iota(jnp.int32, (gradient.shape[0], 1), 0)
    for k, start in enumerate(starts):
        gradient = gradient + jnp.where(row_at == start, cls_grad[pl.ds(first_row + k, 1), :], 0.0)
    return gradient


def backward_kernel(
    first_passage, passages,
    lengths,
    *refs,
):
    refs = list(refs)
    q_cot = refs.pop(0)
    p_cot = refs.pop(0) if passages else q_cot
    cls_grad, chances, stats, packed_ref, context_ref, n1_ref, n2_ref, slope_ref = refs[:8]
    projection, mixing, expand, shrink, gains = refs[8:13]
    refs = refs[13:]
    q_grad = refs.pop(0)
    p_grad = refs.pop(0) if passages else q_grad
    second_ref, hidden_ref, branch_ref, packed_grad, small = refs[:5]
    w0, w1, w2, w3, sems, total_buf, context_grad, inner_buf = refs[5:]
    i = pl.program_id(0)
    weights = Weights((projection, mixing, expand, shrink), (w0, w1, w2, w3), sems, i, first_passage, (3, 2, 1, 0), passages)
    weights.begin()

    @pl.when((i == 0) | (i == first_passage))
    def _():
        small[...] = jnp.zeros_like(small)

    def gradient():
        value = jnp.where(i < first_passage, q_cot[...], p_cot[...]).astype(jnp.float32)
        starts = [start_of(lengths, i, first_passage, k) for k in range(cls_slots)]
        return with_cls(value, starts, cls_grad, i * cls_slots)

    block = Back(
        gradient=gradient, chances=chances.at[0], stats=stats, packed=packed_ref, context=context_ref,
        n1=n1_ref, n2=n2_ref, slope=slope_ref, second=second_ref, hidden=hidden_ref, branch=branch_ref,
        packed_grad=packed_grad, small=small.at[0], total=total_buf, mixed=context_grad, inner=inner_buf,
        weight=weights.get, gain_rows=gains[weights.encoder].astype(jnp.float32),
    )
    block.part_a()
    block.part_b()
    block.part_c()
    input_grad = block.part_d()

    @pl.when(i < first_passage)
    def _():
        q_grad[...] = input_grad

    if passages:

        @pl.when(i >= first_passage)
        def _():
            p_grad[...] = input_grad


def block_specs(first_passage):
    q_at = lambda i, lengths: (jnp.minimum(i, first_passage - 1), 0)
    p_at = lambda i, lengths: (jnp.maximum(i - first_passage, 0), 0)
    at = lambda i, lengths: (i, 0)

    def rows(width, index=at):
        return pl.BlockSpec((block_tokens, width), index)

    def lead(*shape):
        return pl.BlockSpec((1,) + shape, lambda i, lengths: (i,) + (0,) * len(shape))

    def whole(array):
        return pl.BlockSpec(array.shape, lambda i, lengths: (0,) * array.ndim)

    anywhere = pl.BlockSpec(memory_space=pl.ANY)
    return q_at, p_at, rows, lead, whole, anywhere


def weight_scratch(stacked, encoders=2):
    return [pltpu.VMEM((encoders,) + w.shape[1:], w.dtype) for w in stacked[:4]] + [pltpu.SemaphoreType.DMA((4, 2))]


def encode_all(lengths, q_rows, p_rows, stacked):
    projection, mixing, expand, shrink, biases, gains, widening = stacked
    features, wide = projection.shape[1], expand.shape[2]
    first_passage = q_rows.shape[0] // block_tokens
    blocks = first_passage + lengths.shape[0]
    q_at, p_at, rows, lead, whole, anywhere = block_specs(first_passage)
    low, tokens = jnp.bfloat16, blocks * block_tokens
    shape = jax.ShapeDtypeStruct
    return pl.pallas_call(
        partial(forward_kernel, first_passage),
        out_shape=[
            shape(q_rows.shape, low), shape(p_rows.shape, low),
            shape((blocks * cls_slots, features), jnp.float32),
            shape((blocks, HEADS, block_tokens, block_tokens), low),
            shape((tokens, lane), jnp.float32),
            shape((tokens, 3 * features), low),
            shape((tokens, features), low), shape((tokens, features), low),
            shape((tokens, features), low), shape((tokens, features), low),
            shape((tokens, wide), low), shape((tokens, wide), low),
        ],
        grid_spec=pltpu.PrefetchScalarGridSpec(
            num_scalar_prefetch=1,
            grid=(blocks,),
            in_specs=[
                rows(features, q_at), rows(features, p_at), anywhere, anywhere, anywhere, anywhere,
                whole(biases), whole(gains), whole(widening),
            ],
            out_specs=[
                rows(features, q_at), rows(features, p_at),
                pl.BlockSpec((blocks * cls_slots, features), lambda i, lengths: (0, 0)),
                lead(HEADS, block_tokens, block_tokens), rows(lane), rows(3 * features),
                rows(features), rows(features), rows(features), rows(features), rows(wide), rows(wide),
            ],
            scratch_shapes=weight_scratch(stacked) + [
                pltpu.VMEM((block_tokens, features), jnp.float32),
                pltpu.VMEM((block_tokens, features), low),
            ],
        ),
        compiler_params=pltpu.CompilerParams(
            dimension_semantics=("arbitrary",), vmem_limit_bytes=vmem_bytes
        ),
    )(lengths, q_rows, p_rows, projection, mixing, expand, shrink, biases, gains, widening)


def encode_all_back(lengths, q_cot, p_cot, cls_grad, saved, stacked, passages=True):
    projection, mixing, expand, shrink, biases, gains, widening = stacked
    chances, stats, packed, context, first, n1, n2, active, slope = saved
    features, wide = projection.shape[1], expand.shape[2]
    first_passage = q_cot.shape[0] // block_tokens
    blocks = first_passage + (lengths.shape[0] if passages else 0)
    q_at, p_at, rows, lead, whole, anywhere = block_specs(first_passage)
    low, tokens = jnp.bfloat16, blocks * block_tokens
    shape = jax.ShapeDtypeStruct
    small_rows = 8 + wide // features
    encoders = 1 + passages
    return pl.pallas_call(
        partial(backward_kernel, first_passage, passages),
        out_shape=[shape(q_cot.shape, jnp.float32)] + [shape(p_cot.shape, jnp.float32)] * passages + [
            shape((tokens, features), low), shape((tokens, wide), low),
            shape((tokens, features), low), shape((tokens, 3 * features), low),
            shape((encoders, small_rows, features), jnp.float32),
        ],
        grid_spec=pltpu.PrefetchScalarGridSpec(
            num_scalar_prefetch=1,
            grid=(blocks,),
            in_specs=[rows(features, q_at)] + [rows(features, p_at)] * passages + [
                whole(cls_grad),
                lead(HEADS, block_tokens, block_tokens), rows(lane), rows(3 * features),
                rows(features), rows(features), rows(features), rows(wide),
                anywhere, anywhere, anywhere, anywhere, whole(gains),
            ],
            out_specs=[rows(features, q_at)] + [rows(features, p_at)] * passages + [
                rows(features), rows(wide), rows(features), rows(3 * features),
                pl.BlockSpec(
                    (1, small_rows, features),
                    lambda i, lengths: ((i >= first_passage).astype(jnp.int32), 0, 0),
                ),
            ],
            scratch_shapes=weight_scratch(stacked, encoders) + [
                pltpu.VMEM((block_tokens, features), jnp.float32),
                pltpu.VMEM((block_tokens, features), low),
                pltpu.VMEM((16, block_tokens), jnp.float32),
            ],
        ),
        compiler_params=pltpu.CompilerParams(
            dimension_semantics=("arbitrary",), vmem_limit_bytes=vmem_bytes
        ),
    )(
        lengths, q_cot, *[p_cot] * passages, cls_grad, chances, stats, packed, context, n1, n2, slope,
        projection, mixing, expand, shrink, gains,
    )


def contrast_kernel(
    cls, positives, loss_weight, negatives,
    cls_grad, loss,
    q_all, p_all, stat_all, row_send, row_recv, col_send, col_recv, q_wide, q_low,
    q_ss, q_rs, p_ss, p_rs, stat_ss, stat_rs, row_ss, row_rs, col_ss, col_rs,
):
    size_pa, size_pb = lax.axis_size("pa"), lax.axis_size("pb")
    pa, pb = lax.axis_index("pa"), lax.axis_index("pb")
    features = cls.shape[1]
    half = features // 2
    own_q = q_all.shape[1] // 2
    own_p = p_all.shape[1]
    far_a = [(d, lax.rem(pa + d, size_pa)) for d in range(1, size_pa)]
    far_b = [(d, lax.rem(pb + d, size_pb)) for d in range(1, size_pb)]

    barrier = pltpu.get_barrier_semaphore()
    for _, a in far_a:
        pl.semaphore_signal(barrier, inc=1, device_id=(pb, a), device_id_type=MESH)
    for _, b in far_b:
        pl.semaphore_signal(barrier, inc=1, device_id=(b, pa), device_id_type=MESH)
    pl.semaphore_wait(barrier, size_pa + size_pb - 2)

    def to_a(src, dst, ss, rs, d, a):
        return pltpu.make_async_remote_copy(
            src_ref=src, dst_ref=dst, send_sem=ss.at[d], recv_sem=rs.at[d], device_id=(pb, a), device_id_type=MESH
        )

    def to_b(src, dst, ss, rs, d, b):
        return pltpu.make_async_remote_copy(
            src_ref=src, dst_ref=dst, send_sem=ss.at[d], recv_sem=rs.at[d], device_id=(b, pa), device_id_type=MESH
        )

    def fold(block):
        return jnp.concatenate([block[:, :half], block[:, half:]], axis=0).astype(jnp.bfloat16)

    q_all[pa] = fold(cls[:own_q, :])
    p_all[pb] = cls[own_q:, :].astype(jnp.bfloat16)
    copies = [to_a(q_all.at[pa], q_all.at[pa], q_ss, q_rs, d, a) for d, a in far_a]
    copies += [to_b(p_all.at[pb], p_all.at[pb], p_ss, p_rs, d, b) for d, b in far_b]
    for copy in copies:
        copy.start()
    for copy in copies:
        copy.wait()
    for a in range(size_pa):
        block = q_all[a].astype(jnp.float32)
        q_wide[pl.ds(a * own_q, own_q), :half] = block[:own_q]
        q_wide[pl.ds(a * own_q, own_q), half:] = block[own_q:]
    q_low[...] = q_wide[...].astype(jnp.bfloat16)

    tile_scale = 2.0 / math.sqrt(features)
    count = q_low.shape[0]
    p_rows = p_all[...].reshape(size_pb * own_p, features)
    row = lax.broadcasted_iota(jnp.int32, (size_pb * own_p, count), 0)
    slot = row % cls_slots
    valid = slot < cls_slots - 1
    place = row % own_p // cls_slots
    owner = row // own_p * size_pa + pa
    identity = (owner * (own_p // cls_slots) + place) * (cls_slots - 1) + slot
    chosen = jnp.where(valid & (identity == positives[...]), 1.0, 0.0)
    p_scores = dot_nt(p_rows, q_low[...]) * tile_scale
    p_scores = jnp.where(valid, p_scores, -1e30)
    n_scores = dot_nt(negatives[...], q_low[...]) * tile_scale
    top = jnp.maximum(
        jnp.max(p_scores, axis=0, keepdims=True), jnp.max(n_scores, axis=0, keepdims=True)
    )
    mass = jnp.sum(jnp.exp(p_scores - top), axis=0, keepdims=True)
    mass = mass + jnp.sum(jnp.exp(n_scores - top), axis=0, keepdims=True)
    picked = jnp.sum(jnp.where(chosen > 0.0, p_scores, 0.0), axis=0, keepdims=True)
    stat_all[pa] = jnp.concatenate([top, mass, picked] + [jnp.zeros_like(top)] * 5, axis=0)
    copies = [to_a(stat_all.at[pa], stat_all.at[pa], stat_ss, stat_rs, d, a) for d, a in far_a]
    for copy in copies:
        copy.start()
    for copy in copies:
        copy.wait()
    all_top = stat_all[0, 0:1]
    for a in range(1, size_pa):
        all_top = jnp.maximum(all_top, stat_all[a, 0:1])
    all_mass = jnp.zeros_like(all_top)
    all_picked = jnp.zeros_like(all_top)
    for a in range(size_pa):
        all_mass = all_mass + stat_all[a, 1:2] * jnp.exp(stat_all[a, 0:1] - all_top)
        all_picked = all_picked + stat_all[a, 2:3]
    logsum = all_top + jnp.log(all_mass)
    loss[...] = logsum - all_picked

    p_tile = (loss_weight[...] * (jnp.exp(p_scores - logsum) - chosen)).astype(jnp.bfloat16)
    n_tile = (loss_weight[...] * jnp.exp(n_scores - logsum)).astype(jnp.bfloat16)
    q_wide[...] = (dot_tn(p_tile, p_rows) + dot_tn(n_tile, negatives[...])) * tile_scale
    col_send[...] = (dot_nn(p_tile, q_low[...]) * tile_scale).reshape(col_send.shape)
    for a in range(size_pa):
        row_send[a] = fold(q_wide[pl.ds(a * own_q, own_q), :])
    copies = [to_a(row_send.at[a], row_recv.at[pa], row_ss, row_rs, d, a) for d, a in far_a]
    copies += [to_b(col_send.at[b], col_recv.at[pb], col_ss, col_rs, d, b) for d, b in far_b]
    for copy in copies:
        copy.start()
    for copy in copies:
        copy.wait()
    row_recv[pa] = row_send[pa]
    col_recv[pb] = col_send[pb]
    total = row_recv[0].astype(jnp.float32)
    for a in range(1, size_pa):
        total = total + row_recv[a].astype(jnp.float32)
    cls_grad[:own_q, :half] = total[:own_q]
    cls_grad[:own_q, half:] = total[own_q:]
    total = col_recv[0]
    for b in range(1, size_pb):
        total = total + col_recv[b]
    cls_grad[own_q:, :] = total


def contrast(cls, own_q, positives, loss_weight, negatives):
    size_pa, size_pb = lax.axis_size("pa"), lax.axis_size("pb")
    slots, features = cls.shape
    own_p, count = slots - own_q, positives.shape[0]
    low, dma = jnp.bfloat16, pltpu.SemaphoreType.DMA
    folded = (size_pa, 2 * own_q, features // 2)
    sems = [dma((size_pa,))] * 2 + [dma((size_pb,))] * 2 + [dma((size_pa,))] * 4 + [dma((size_pb,))] * 2
    cls_grad, loss = pl.pallas_call(
        contrast_kernel,
        out_shape=[
            jax.ShapeDtypeStruct(cls.shape, jnp.float32),
            jax.ShapeDtypeStruct((1, count), jnp.float32),
        ],
        in_specs=[pl.BlockSpec(memory_space=pltpu.VMEM)] * 4,
        out_specs=[pl.BlockSpec(memory_space=pltpu.VMEM)] * 2,
        scratch_shapes=[
            pltpu.VMEM(folded, low),
            pltpu.VMEM((size_pb, own_p, features), low),
            pltpu.VMEM((size_pa, 8, count), jnp.float32),
            pltpu.VMEM(folded, low),
            pltpu.VMEM(folded, low),
            pltpu.VMEM((size_pb, own_p, features), jnp.float32),
            pltpu.VMEM((size_pb, own_p, features), jnp.float32),
            pltpu.VMEM((count, features), jnp.float32),
            pltpu.VMEM((count, features), low),
        ] + sems,
        compiler_params=pltpu.CompilerParams(
            collective_id=2, has_side_effects=True, vmem_limit_bytes=vmem_bytes
        ),
    )(cls, positives[None, :], loss_weight[None, :], negatives)
    return cls_grad, loss[0]


panel_rows = 48
chunk_panels = 8
encoder_chunks = 9


ring = 6


def reduce_kernel(
    tokens,
    active, first, context, q_rows, p_rows, q_second, q_hidden, q_branch, q_packed,
    p_cot, chances, stats, packed, n1, n2, slope, projection, mixing, expand, shrink,
    lengths, cls_grad, gains, small_ref,
    p_second, p_hidden, p_branch, p_packed, p_grad,
    projection_out, mixing_out, expand_out, shrink_out, small_out,
    keep, core_send, core_recv, recv_x, recv_ya, recv_za, recv_yb, recv_zb, fin_a, fin_b,
    left_buf, left_t, right_buf, product, small_recv, small_sum,
    load_sem, core_ss, core_rs, xa_ss, xa_rs, ya_ss, ya_rs, za_ss, za_rs, ag_ss, ag_rs,
    yb_ss, yb_rs, zb_ss, zb_rs, xb_ss, xb_rs, small_ss, small_rs, credit,
    w0, w1, w2, w3, weight_sem, in_sem, out_sem,
    b_cot, b_chances, b_stats, b_packed, b_context, b_n1, b_n2, b_slope,
    b_second, b_hidden, b_branch, b_packed_grad, b_grad, b_total, b_mixed, b_inner, p_small,
):
    chunks = 2 * encoder_chunks
    pb, pa = lax.axis_index("pb"), lax.axis_index("pa")
    core, y, z, x = pa % 2, pa // 2 % 2, pa // 4, pb
    at_core = (pb, pa + 1 - 2 * core)
    at_y = (pb, pa + 2 - 4 * y)
    at_x = (1 - pb, pa)
    far_z = [(z + d) % 4 for d in (1, 2, 3)]
    at_z = [(pb, t * 4 + y * 2 + core) for t in far_z]

    barrier = pltpu.get_barrier_semaphore()
    for device in [at_core, at_y, at_x] + at_z:
        pl.semaphore_signal(barrier, inc=1, device_id=device, device_id_type=MESH)
    pl.semaphore_wait(barrier, 6)

    def remote(src, dst, ss, rs, device):
        return pltpu.make_async_remote_copy(
            src_ref=src, dst_ref=dst, send_sem=ss, recv_sem=rs, device_id=device, device_id_type=MESH
        )

    def copy_core(c):
        return remote(core_send.at[c % 2], core_recv.at[c % 3], core_ss.at[c], core_rs.at[c], at_core)

    def copy_xa(c):
        return remote(keep.at[c % ring, pl.ds(2 * (1 - x), 2)], recv_x.at[c % ring], xa_ss.at[c], xa_rs.at[c], at_x)

    def copy_ya(c):
        return remote(
            keep.at[c % ring, pl.ds(2 * x, 2), :, 1 - y], recv_ya.at[c % ring], ya_ss.at[c], ya_rs.at[c], at_y
        )

    def copy_za(c, d):
        return remote(
            keep.at[c % ring, pl.ds(2 * x, 2), far_z[d], y], recv_za.at[c % ring, d], za_ss.at[c, d], za_rs.at[c, d], at_z[d]
        )

    def copy_ag(c):
        half = fin_a.at[c % ring, pl.ds(2 * x, 2)]
        return remote(half, half, ag_ss.at[c], ag_rs.at[c], at_x)

    def copy_yb(c):
        return remote(keep.at[c % ring, pl.ds(4, 4), :, 1 - y], recv_yb.at[c % ring], yb_ss.at[c], yb_rs.at[c], at_y)

    def copy_zb(c, d):
        return remote(
            keep.at[c % ring, pl.ds(4, 4), far_z[d], y], recv_zb.at[c % ring, d], zb_ss.at[c, d], zb_rs.at[c, d], at_z[d]
        )

    def copy_xb(c):
        return remote(fin_b.at[c % ring, x], fin_b.at[c % ring, x], xb_ss.at[c], xb_rs.at[c], at_x)

    def small_copy(stage, device):
        source = small_sum.at[max(stage - 3, 0) if stage >= 3 else stage]
        return remote(source, small_recv.at[stage], small_ss.at[stage], small_rs.at[stage], device)

    def own(e, ref):
        return ref.at[pl.ds(0 if e == 0 else tokens[0], tokens[e])]

    grads = ((q_second, q_hidden, q_branch, q_packed), (p_second, p_hidden, p_branch, p_packed))

    def left_loads(e, part):
        count = tokens[e]
        features = q_rows.shape[1]
        if part == 0:
            pairs = [(own(e, active), 0)]
        elif part == 1:
            pairs = [(own(e, first), 0)]
        else:
            pairs = [((q_rows, p_rows)[e], 0), (own(e, context), features)]
        return [
            pltpu.make_async_copy(
                ref,
                left_buf.at[pl.ds(0, count), pl.ds(at, ref.shape[1])],
                load_sem.at[2 + i],
            )
            for i, (ref, at) in enumerate(pairs)
        ]

    def right_loads(e, k):
        count = tokens[e]
        slot = (e * encoder_chunks + k) % 2
        second, hidden, branch, packed_grad = grads[e]
        if k < 3:
            pairs = [(second, 256 * k, 256, 0)]
        elif k < 6:
            pairs = [(hidden, 1024 * (k - 3), 1024, 0)]
        elif k < 8:
            pairs = [(packed_grad, 1024 * (k - 6), 1024, 0)]
        else:
            pairs = [(packed_grad, 2048, 256, 0), (branch, 0, 768, 256)]
        return [
            pltpu.make_async_copy(
                ref.at[:, pl.ds(start, width)],
                right_buf.at[slot, pl.ds(0, count), pl.ds(at, width)],
                load_sem.at[slot] if i == 0 else load_sem.at[4],
            )
            for i, (ref, start, width, at) in enumerate(pairs)
        ]

    def begin(copies):
        for copy in copies:
            copy.start()

    def finish(copies):
        for copy in copies:
            copy.wait()

    def transpose_left(e, part):
        count = tokens[e]
        width = (3072, 768, 1536)[part]

        def step(i, carry):
            at = pl.multiple_of(i * 256, 256)
            left_t[pl.ds(at, 256), pl.ds(0, count)] = left_buf[pl.ds(0, count), pl.ds(at, 256)].T
            return carry

        lax.fori_loop(0, width // 256, step, 0)

    def compute(e, k):
        count = tokens[e]
        c = e * encoder_chunks + k
        slot = c % 2

        def step(q, carry):
            if k < 3:
                rows_at, columns_at = q * 768, 0
            elif k < 8:
                rows_at, columns_at = 0, q * 256
            else:
                rows_at, columns_at = jnp.where(q > 0, 768, 0), q * 256
            rows_at = pl.multiple_of(rows_at, 256)
            columns_at = pl.multiple_of(columns_at, 256)
            product[...] = jnp.dot(
                left_t[pl.ds(rows_at, 768), pl.ds(0, count)],
                right_buf[slot, pl.ds(0, count), pl.ds(columns_at, 256)],
                preferred_element_type=jnp.float32,
            )
            if k < 3:
                for iy in range(2):
                    for sub in range(4):
                        for which, target in ((core, keep.at[c % ring]), (1 - core, core_send.at[slot])):
                            at = pl.multiple_of((2 * iy + which) * 192 + sub * 48, 16)
                            block = product[pl.ds(at, 48), :].astype(jnp.bfloat16)
                            target[sub * 2, q, iy] = block[:, :lane]
                            target[sub * 2 + 1, q, iy] = block[:, lane:]
            else:
                for iz in range(4):
                    for iy in range(2):
                        for which, target in ((core, keep.at[c % ring]), (1 - core, core_send.at[slot])):
                            at = pl.multiple_of((4 * iz + 2 * iy + which) * 48, 16)
                            block = product[pl.ds(at, 48), :].astype(jnp.bfloat16)
                            target[2 * q, iz, iy] = block[:, :lane]
                            target[2 * q + 1, iz, iy] = block[:, lane:]
            return carry

        lax.fori_loop(0, 4, step, 0)

    order = [(e, k) for e in range(2) for k in range(encoder_chunks)]
    part_of = lambda k: 0 if k < 3 else 1 if k < 6 else 2

    def produce(c):
        e, k = order[c]
        if c >= 2:
            copy_core(c - 2).wait_send()
        if k % 3 == 0:
            finish(left_loads(e, part_of(k)))
            transpose_left(e, part_of(k))
            if c + 3 < chunks:
                e2, k2 = order[c + 3]
                begin(left_loads(e2, part_of(k2)))
        finish(right_loads(e, k))
        if c + 1 < chunks and c + 1 != encoder_chunks:
            begin(right_loads(*order[c + 1]))
        compute(e, k)
        if c >= 3:
            pl.semaphore_wait(credit, 1)
        copy_core(c).start()

    def write(c, panel, value):
        e, k = order[c]
        if k < 3:
            rows = pl.ds(panel // 2 * panel_rows, panel_rows)
            shrink_out[e, rows, pl.ds(256 * k + panel % 2 * lane, lane)] = value
        elif k < 6:
            expand_out[e, :, pl.ds(1024 * (k - 3) + panel * lane, lane)] = value
        else:
            at = 1024 * (k - 6) + panel * lane
            width = projection_out.shape[2]
            if at < width:
                projection_out[e, :, pl.ds(at, lane)] = value
            else:
                mixing_out[e, :, pl.ds(at - width, lane)] = value

    def after_core(c):
        copy_core(c).wait_recv()

        def step(p, carry):
            keep[c % ring, p] = keep[c % ring, p] + core_recv[c % 3, p]
            return carry

        lax.fori_loop(0, chunk_panels, step, 0)
        copy_xa(c).start()
        copy_yb(c).start()

        @pl.when(c < chunks - 3)
        def _():
            pl.semaphore_signal(credit, inc=1, device_id=at_core, device_id_type=MESH)

    def after_first(c):
        copy_yb(c).wait_recv()

        def step_b(p, carry):
            for iz in range(4):
                keep[c % ring, 4 + p, iz, y] = keep[c % ring, 4 + p, iz, y] + recv_yb[c % ring, p, iz]
            return carry

        lax.fori_loop(0, 4, step_b, 0)
        for d in range(3):
            copy_zb(c, d).start()
        copy_xa(c).wait_recv()

        def step_a(p, carry):
            keep[c % ring, 2 * x + p] = keep[c % ring, 2 * x + p] + recv_x[c % ring, p]
            return carry

        lax.fori_loop(0, 2, step_a, 0)
        copy_ya(c).start()

    def widen(value):
        return value.astype(jnp.float32)

    def after_second(c):
        copy_ya(c).wait_recv()

        def step_a(p, carry):
            for iz in range(4):
                keep[c % ring, 2 * x + p, iz, y] = keep[c % ring, 2 * x + p, iz, y] + recv_ya[c % ring, p, iz]
            return carry

        lax.fori_loop(0, 2, step_a, 0)
        for d in range(3):
            copy_za(c, d).start()
        for d in range(3):
            copy_zb(c, d).wait_recv()

        def step_b(p, carry):
            fin_b[c % ring, x, p] = (
                widen(keep[c % ring, 4 + p, z, y])
                + widen(recv_zb[c % ring, 0, p])
                + widen(recv_zb[c % ring, 1, p])
                + widen(recv_zb[c % ring, 2, p])
            ).astype(jnp.bfloat16)
            return carry

        lax.fori_loop(0, 4, step_b, 0)
        copy_xb(c).start()

    def after_third(c):
        for d in range(3):
            copy_za(c, d).wait_recv()

        def step_a(p, carry):
            fin_a[c % ring, 2 * x + p] = (
                widen(keep[c % ring, 2 * x + p, z, y])
                + widen(recv_za[c % ring, 0, p])
                + widen(recv_za[c % ring, 1, p])
                + widen(recv_za[c % ring, 2, p])
            ).astype(jnp.bfloat16)
            return carry

        lax.fori_loop(0, 2, step_a, 0)
        copy_ag(c).start()
        copy_xb(c).wait_recv()

        for p in range(4):
            write(c, 4 + p, widen(fin_b[c % ring, 0, p]) + widen(fin_b[c % ring, 1, p]))

    def after_last(c):
        copy_ag(c).wait_recv()
        copy_xa(c).wait_send()
        copy_ya(c).wait_send()
        copy_ag(c).wait_send()
        copy_yb(c).wait_send()
        copy_xb(c).wait_send()
        for d in range(3):
            copy_za(c, d).wait_send()
            copy_zb(c, d).wait_send()

        for p in range(4):
            write(c, p, widen(fin_a[c % ring, p]))

    passage_blocks = tokens[1] // block_tokens
    weight_copies = [
        pltpu.make_async_copy(source.at[1], buffer, weight_sem.at[i])
        for i, (source, buffer) in enumerate(zip((projection, mixing, expand, shrink), (w0, w1, w2, w3)))
    ]

    def block_loads(b):
        at = pl.ds(tokens[0] + b * block_tokens, block_tokens)
        first_block = tokens[0] // block_tokens
        pairs = [(p_cot.at[pl.ds(b * block_tokens, block_tokens)], b_cot), (chances.at[first_block + b], b_chances)]
        pairs += [
            (ref.at[at], buffer)
            for ref, buffer in (
                (stats, b_stats), (packed, b_packed), (context, b_context), (n1, b_n1), (n2, b_n2), (slope, b_slope)
            )
        ]
        return [pltpu.make_async_copy(src, dst, in_sem.at[i]) for i, (src, dst) in enumerate(pairs)]

    def block_stores(b):
        at = pl.ds(b * block_tokens, block_tokens)
        pairs = (
            (b_second, p_second), (b_hidden, p_hidden), (b_branch, p_branch), (b_packed_grad, p_packed), (b_grad, p_grad)
        )
        return [
            pltpu.make_async_copy(src, dst.at[at], out_sem.at[i]) for i, (src, dst) in enumerate(pairs)
        ]

    waited = set()

    def weight(which):
        if which not in waited:
            waited.add(which)
            weight_copies[which].wait()
        return (w0, w1, w2, w3)[which]

    def part(index):
        b, which = divmod(index, 4)

        def gradient():
            starts, at = [], jnp.zeros((1, 1), jnp.int32)
            for k in range(cls_slots):
                starts.append(at)
                if k < cls_slots - 1:
                    at = at + lengths[pl.ds(b, 1), pl.ds(k, 1)]
            first_row = (tokens[0] // block_tokens + b) * cls_slots
            return with_cls(b_cot[...].astype(jnp.float32), starts, cls_grad, first_row)

        block = Back(
            gradient=gradient, chances=b_chances, stats=b_stats, packed=b_packed, context=b_context,
            n1=b_n1, n2=b_n2, slope=b_slope, second=b_second, hidden=b_hidden, branch=b_branch,
            packed_grad=b_packed_grad, small=p_small, total=b_total, mixed=b_mixed, inner=b_inner,
            weight=weight, gain_rows=gains[1].astype(jnp.float32),
        )
        if which == 0:
            finish(block_loads(b))
            if b > 0:
                finish(block_stores(b - 1))
            block.part_a()
        elif which == 1:
            block.part_b()
        elif which == 2:
            block.part_c()
        else:
            b_grad[...] = block.part_d()
            if b + 1 < passage_blocks:
                begin(block_loads(b + 1))
            begin(block_stores(b))
            if b + 1 == passage_blocks:
                finish(block_stores(b))
                begin(right_loads(1, 0))

    begin(left_loads(0, 0))
    begin(right_loads(0, 0))
    begin(block_loads(0))
    begin([weight_copies[i] for i in (3, 2, 1, 0)])
    p_small[...] = jnp.zeros_like(p_small)
    todo = list(range(4 * passage_blocks))
    per_step = -(-len(todo) // (encoder_chunks - 1))

    def parts(count):
        for _ in range(count):
            if todo:
                part(todo.pop(0))

    for c in range(chunks + 5):
        if c < chunks:
            produce(c)
        if 0 <= c - 1 < chunks:
            after_core(c - 1)
        if c > 0:
            parts(per_step // 2)
        if 0 <= c - 2 < chunks:
            after_first(c - 2)
        if 0 <= c - 3 < chunks:
            after_second(c - 3)
        if c > 0:
            parts(per_step - per_step // 2)
        if 0 <= c - 4 < chunks:
            after_third(c - 4)
        if 0 <= c - 5 < chunks:
            after_last(c - 5)
        if c == encoder_chunks:
            half = small_ref.shape[0]
            small_sum[0, :half] = small_ref[...]
            small_sum[0, half:] = p_small[...]
            small_copy(0, at_core).start()
        if c == encoder_chunks + 1:
            small_copy(0, at_core).wait_recv()
            small_sum[1] = small_sum[0] + small_recv[0]
            small_copy(1, at_x).start()
        if c == encoder_chunks + 2:
            small_copy(1, at_x).wait_recv()
            small_sum[2] = small_sum[1] + small_recv[1]
            small_copy(2, at_y).start()
        if c == encoder_chunks + 3:
            small_copy(2, at_y).wait_recv()
            small_sum[3] = small_sum[2] + small_recv[2]
            for d in range(3):
                remote(small_sum.at[3], small_recv.at[3 + d], small_ss.at[3 + d], small_rs.at[3 + d], at_z[d]).start()
        if c == encoder_chunks + 4:
            for d in range(3):
                remote(small_sum.at[3], small_recv.at[3 + d], small_ss.at[3 + d], small_rs.at[3 + d], at_z[d]).wait_recv()
            result = jnp.zeros(small_out.shape, jnp.float32)
            for iz in range(4):
                back = (z - iz + 4) % 4
                value = jnp.where(back == 0, small_sum[3], 0.0)
                for d in range(3):
                    value = jnp.where(back == d + 1, small_recv[3 + d], value)
                result = result + value
            small_out[...] = result

    copy_core(chunks - 2).wait_send()
    copy_core(chunks - 1).wait_send()

    small_copy(0, at_core).wait_send()
    small_copy(1, at_x).wait_send()
    small_copy(2, at_y).wait_send()
    for d in range(3):
        remote(small_sum.at[3], small_recv.at[3 + d], small_ss.at[3 + d], small_rs.at[3 + d], at_z[d]).wait_send()


def reduce_by_kernel(lengths, q_rows, p_rows, p_cot, cls_grad, saved, question_side, stacked):
    projection, mixing, expand, shrink, biases, gains, widening = stacked
    chances, stats, packed, context, first, n1, n2, active, slope = saved
    q_second, q_hidden, q_branch, q_packed, small = question_side
    features, wide = projection.shape[1], expand.shape[2]
    tokens = (q_rows.shape[0], p_rows.shape[0])
    small = small[0]
    most = max(tokens)
    chunks = 2 * encoder_chunks
    tile = (panel_rows, lane)
    low = jnp.bfloat16
    dma = pltpu.SemaphoreType.DMA
    one, three = dma((chunks,)), dma((chunks, 3))
    block = lambda width, kind=low: pltpu.VMEM((block_tokens, width), kind)
    shape = jax.ShapeDtypeStruct
    return pl.pallas_call(
        partial(reduce_kernel, tokens),
        out_shape=[
            shape((tokens[1], features), low), shape((tokens[1], wide), low),
            shape((tokens[1], features), low), shape((tokens[1], 3 * features), low),
            shape((tokens[1], features), jnp.float32),
            shape((2, 48, 2304), jnp.float32),
            shape((2, 48, 768), jnp.float32),
            shape((2, 48, 3072), jnp.float32),
            shape((2, 192, 768), jnp.float32),
            shape((2 * small.shape[0],) + small.shape[1:], jnp.float32),
        ],
        in_specs=[pl.BlockSpec(memory_space=pl.ANY)] * 20 + [pl.BlockSpec(memory_space=pltpu.VMEM)] * 4,
        out_specs=[pl.BlockSpec(memory_space=pl.ANY)] * 5 + [pl.BlockSpec(memory_space=pltpu.VMEM)] * 5,
        scratch_shapes=[
            pltpu.VMEM((ring, chunk_panels, 4, 2) + tile, low),
            pltpu.VMEM((2, chunk_panels, 4, 2) + tile, low),
            pltpu.VMEM((3, chunk_panels, 4, 2) + tile, low),
            pltpu.VMEM((ring, 2, 4, 2) + tile, low),
            pltpu.VMEM((ring, 2, 4) + tile, low),
            pltpu.VMEM((ring, 3, 2) + tile, low),
            pltpu.VMEM((ring, 4, 4) + tile, low),
            pltpu.VMEM((ring, 3, 4) + tile, low),
            pltpu.VMEM((ring, 4) + tile, low),
            pltpu.VMEM((ring, 2, 4) + tile, low),
            pltpu.VMEM((most, 3072), low),
            pltpu.VMEM((3072, most), low),
            pltpu.VMEM((2, most, 1024), low),
            pltpu.VMEM((768, 256), jnp.float32),
            pltpu.VMEM((6, 2 * small.shape[0], features), jnp.float32),
            pltpu.VMEM((4, 2 * small.shape[0], features), jnp.float32),
            dma((5,)),
            one, one, one, one, one, one, three, three, one, one,
            one, one, three, three, one, one, dma((6,)), dma((6,)),
            pltpu.SemaphoreType.REGULAR,
        ] + [pltpu.VMEM(w.shape[1:], low) for w in (projection, mixing, expand, shrink)] + [
            dma((4,)), dma((8,)), dma((5,)),
            block(features), pltpu.VMEM((HEADS, block_tokens, block_tokens), low), block(lane, jnp.float32),
            block(3 * features), block(features), block(features), block(features), block(wide),
            block(features), block(wide), block(features), block(3 * features), block(features, jnp.float32),
            block(features, jnp.float32), block(features), pltpu.VMEM((16, block_tokens), jnp.float32),
            pltpu.VMEM(small.shape, jnp.float32),
        ],
        compiler_params=pltpu.CompilerParams(
            collective_id=1, has_side_effects=True, vmem_limit_bytes=vmem_bytes
        ),
        cost_estimate=pl.CostEstimate(flops=40 * 10**9, bytes_accessed=150 * 10**6, transcendentals=0),
    )(
        active, first, context, q_rows, p_rows, q_second, q_hidden, q_branch, q_packed,
        p_cot, chances, stats, packed, n1, n2, slope, projection, mixing, expand, shrink,
        lengths, cls_grad, gains, small,
    )


def backward_all(lengths, q_rows, p_rows, q_cot, p_cot, cls_grad, saved, stacked):
    size_pa, size_pb = lax.axis_size("pa"), lax.axis_size("pb")
    chances, stats, packed, context, first, n1, n2, active, slope = saved
    features = q_rows.shape[1]
    if size_pa == 16 and size_pb == 2:
        q_grad, *question_side = encode_all_back(
            lengths, q_cot, p_cot, cls_grad, saved, stacked, passages=False
        )
        reduced = reduce_by_kernel(
            lengths, q_rows, p_rows, p_cot, cls_grad, saved, question_side, stacked
        )
        p_grad, projection, mixing, expand, shrink, small = reduced[4:]
        small = small.reshape(2, -1, features)
    else:
        q_grad, p_grad, second, hidden, branch, packed_grad, small = encode_all_back(
            lengths, q_cot, p_cot, cls_grad, saved, stacked
        )
        products = []
        cut = q_rows.shape[0]
        for rows, part in ((q_rows, slice(None, cut)), (p_rows, slice(cut, None))):
            pairs = ((rows, packed_grad[part]), (context[part], branch[part]), (first[part], hidden[part]), (active[part], second[part]))
            products.append([contract_rows(*pair) for pair in pairs])
        projection, mixing, expand, shrink = (
            lax.psum(
                jnp.stack(
                    [
                        lax.psum_scatter(products[e][i], "pa", scatter_dimension=0, tiled=True)
                        for e in range(2)
                    ]
                ),
                "pb",
            )
            for i in range(4)
        )
        small = lax.psum(small, ("pb", "pa"))
    mine = lax.axis_index("pa")
    share = features // size_pa
    columns = lax.dynamic_slice_in_dim(small[:, :8], mine * share, share, 2)
    widening = small[:, 8:].reshape(2, -1)
    wide = widening.shape[1] // size_pa
    widening = lax.dynamic_slice_in_dim(widening, mine * wide, wide, 1)
    return q_grad, p_grad, (projection, mixing, expand, shrink, columns[:, :6], columns[:, 6:], widening)


def body(
    question_rows,
    passage_rows,
    segment_lengths,
    positives,
    negatives,
    question_cotangent,
    passage_cotangent,
    loss_weight,
    projection,
    mixing,
    expand,
    shrink,
    biases,
    gains,
    widening,
):
    stacked = (projection, mixing, expand, shrink, biases, gains, widening)
    question_count, _, features = question_rows.shape
    q_rows = question_rows.reshape(-1, features)
    p_rows = passage_rows.reshape(-1, features)
    q_states, p_states, cls, *saved = encode_all(segment_lengths, q_rows, p_rows, stacked)
    cls_grad, question_loss = contrast(cls, question_count, positives, loss_weight, negatives)
    q_grad, p_grad, totals = backward_all(
        segment_lengths,
        q_rows,
        p_rows,
        question_cotangent.reshape(-1, features),
        passage_cotangent.reshape(-1, features),
        cls_grad,
        saved,
        stacked,
    )
    return (
        q_states.reshape(question_rows.shape),
        p_states.reshape(passage_rows.shape),
        question_loss,
        q_grad.reshape(question_rows.shape),
        p_grad.reshape(passage_rows.shape),
    ) + totals


def solution(mesh):
    return jax.shard_map(
        body,
        mesh=mesh,
        in_specs=(
            P(("pb", "pa"), None, None),
            P(("pb", "pa"), None, None),
            P(("pb", "pa"), None),
            P("pb"),
            P("pa", None),
            P(("pb", "pa"), None, None),
            P(("pb", "pa"), None, None),
            P("pb"),
            P(),
            P(),
            P(),
            P(),
            P(),
            P(),
            P(),
        ),
        out_specs=(
            P(("pb", "pa"), None, None),
            P(("pb", "pa"), None, None),
            P("pb"),
            P(("pb", "pa"), None, None),
            P(("pb", "pa"), None, None),
            P(None, "pa", None),
            P(None, "pa", None),
            P(None, "pa", None),
            P(None, "pa", None),
            P(None, None, "pa"),
            P(None, None, "pa"),
            P(None, "pa"),
        ),
        check_vma=False,
    )
```

```python
from functools import partial
import math

import jax
import jax.numpy as jnp
from jax import lax
from jax.experimental import pallas as pl
from jax.experimental.pallas import tpu as pltpu
from jax.sharding import PartitionSpec as P

HEADS = 12
HEAD_DIM = 64


eps_norm = 1e-12
masked_score = -1000000000.0


def matmul(left_side, right_side):
    return jnp.dot(left_side, right_side, preferred_element_type=jnp.float32)


def contract_rows(left_side, right_side):
    return lax.dot_general(
        left_side, right_side, (((0,), (0,)), ((), ())), preferred_element_type=jnp.float32
    )


def contract_cols(left_side, right_side):
    return lax.dot_general(
        left_side, right_side, (((1,), (1,)), ((), ())), preferred_element_type=jnp.float32
    )


MESH = pl.DeviceIdType.MESH
lane = 128
block_tokens = 256
cls_slots = 4
stat_first, stat_final = 0, 1
vmem_bytes = 63 * 1024 * 1024


def dot_nn(left_side, right_side):
    return jnp.dot(left_side, right_side, preferred_element_type=jnp.float32)


def dot_nt(left_side, right_side):
    return lax.dot_general(
        left_side, right_side, (((1,), (1,)), ((), ())), preferred_element_type=jnp.float32
    )


def dot_tn(left_side, right_side):
    return lax.dot_general(
        left_side, right_side, (((0,), (0,)), ((), ())), preferred_element_type=jnp.float32
    )


def gelu_and_slope(hidden):
    size = jnp.abs(hidden)
    t = pl.reciprocal(1.0 + (0.3275911 * math.sqrt(0.5)) * size, approx=True)
    bell = jnp.exp2((hidden * hidden) * (-0.5 * math.log2(math.e)))
    tail = (0.5 * 1.061405429) * t - (0.5 * 1.453152027)
    tail = tail * t + (0.5 * 1.421413741)
    tail = tail * t - (0.5 * 0.284496736)
    tail = (tail * t + (0.5 * 0.254829592)) * (t * bell)
    below = jnp.where(hidden < 0.0, tail, 1.0 - tail)
    return hidden * below, below + (hidden * bell) * (1.0 / math.sqrt(2.0 * math.pi))


def normalize(values):
    centre = values - jnp.mean(values, axis=-1, keepdims=True)
    inverse = lax.rsqrt(jnp.mean(centre * centre, axis=-1, keepdims=True) + eps_norm)
    return centre * inverse, inverse


def normalize_back(gradient, normal, inverse, gain_row):
    scaled = gradient * gain_row
    inner_mean = jnp.mean(scaled, axis=-1, keepdims=True)
    projected = jnp.mean(scaled * normal, axis=-1, keepdims=True)
    return inverse * (scaled - inner_mean - normal * projected)


def head_pair(packed_ref, pair, features):
    return [packed_ref[:, pl.ds(j * features + pair * lane, lane)] for j in range(3)]


def side_mask(side, scale):
    at = lax.broadcasted_iota(jnp.int32, (1, lane), 1) // HEAD_DIM
    return jnp.where(at == side, scale, 0.0).astype(jnp.bfloat16)


def start_of(lengths, i, first_passage, k):
    row = jnp.maximum(i - first_passage, 0)
    at = 0
    for j in range(k):
        at = at + lengths[row, j]
    return jnp.where(i < first_passage, k * (block_tokens // cls_slots), at)


class Weights:
    def __init__(self, sources, buffers, sems, step, first_passage, order, passages=True):
        self.sources, self.buffers, self.sems, self.order = sources, buffers, sems, order
        self.step, self.first_passage = step, first_passage
        self.encoder = (step >= first_passage).astype(jnp.int32)
        self.parts = ((0, 0), (1, first_passage))[: 1 + passages]
        self.seen = set()

    def copy(self, which, e):
        return pltpu.make_async_copy(
            self.sources[which].at[e], self.buffers[which].at[e], self.sems.at[which, e]
        )

    def begin(self):
        for e, at in self.parts:

            @pl.when(self.step == max(at - 1, 0))
            def _():
                for which in self.order:
                    self.copy(which, e).start()

    def get(self, which):
        if which not in self.seen:
            self.seen.add(which)
            for e, at in self.parts:

                @pl.when(self.step == at)
                def _():
                    self.copy(which, e).wait()

        return self.buffers[which].at[self.encoder]


def feed_forward(first_low, first, up, down, wide_shift, shifts, gain_rows, keep):
    tile = 512

    def raised(j):
        return dot_nn(first_low, up[:, pl.ds(j * tile, tile)]) + wide_shift[:, j * tile : (j + 1) * tile]

    second = jnp.broadcast_to(shifts[4:5], first.shape)
    ahead = raised(0)
    for j in range(up.shape[1] // tile):
        columns = pl.ds(j * tile, tile)
        hidden = ahead
        if (j + 1) * tile < up.shape[1]:
            ahead = raised(j + 1)
        active, slope = gelu_and_slope(hidden)
        active_low = active.astype(jnp.bfloat16)
        if keep is not None:
            keep(columns, active_low, slope.astype(jnp.bfloat16))
        second = second + dot_nn(active_low, down[columns, :])
    normal, inverse = normalize(first[...] + second)
    return normal, inverse, normal * gain_rows[1:2] + shifts[5:6]


def forward_kernel(
    first_passage,
    lengths,
    q_rows, p_rows, projection, mixing, expand, shrink, biases, gains, widening,
    q_states, cls, chances, stats, packed_ref, context_ref, first_ref, n1_ref, wide_first,
    n2_ref, active_ref, slope_ref,
    w0, w1, w2, w3, sems, final_buf, x_buf, cls_first,
):
    i = pl.program_id(0)
    weights = Weights((projection, mixing, expand, shrink), (w0, w1, w2, w3), sems, i, first_passage, (0, 1, 2, 3))
    weights.begin()
    e = weights.encoder
    features = q_rows.shape[1]
    shifts = biases[e].astype(jnp.float32)
    gain_rows = gains[e].astype(jnp.float32)
    both = widening[...].astype(jnp.float32)
    wide_shift = jnp.where(e == 0, both[0:1], both[1:2])
    x_buf[...] = jnp.where(i < first_passage, q_rows[...], p_rows[...])

    weight = weights.get(0)
    x_low = x_buf[...]
    for part in range(3):
        columns = pl.ds(part * features, features)
        value = dot_nn(x_low, weight[:, columns])
        if part != 1:
            value = value + shifts[part // 2 : part // 2 + 1]
        packed_ref[:, columns] = value.astype(jnp.bfloat16)

    tokens = q_rows.shape[0]
    row_at = lax.broadcasted_iota(jnp.int32, (tokens, tokens), 0)
    col_at = lax.broadcasted_iota(jnp.int32, (tokens, tokens), 1)
    starts = [start_of(lengths, i, first_passage, k) for k in range(cls_slots)]
    row_segment = jnp.zeros_like(row_at)
    col_segment = jnp.zeros_like(col_at)
    for k in range(1, cls_slots):
        row_segment = row_segment + (row_at >= starts[k]).astype(jnp.int32)
        col_segment = col_segment + (col_at >= starts[k]).astype(jnp.int32)
    penalty = jnp.where(row_segment == col_segment, 0.0, masked_score)
    def scores_of(pair):
        queries, keys, _ = head_pair(packed_ref, pair, features)
        both = [keys * side_mask(side, HEAD_DIM ** (-0.5)) for side in range(2)]
        return dot_nt(jnp.concatenate(both), queries)

    def chances_of(pair, scores):
        result = []
        for side in range(2):
            part = scores[side * tokens : (side + 1) * tokens] + penalty
            chance = jnp.exp(part - jnp.max(part, axis=0, keepdims=True))
            inverse = 1.0 / jnp.sum(chance, axis=0, keepdims=True)
            result.append((chance * inverse).astype(jnp.bfloat16))
            chances[0, 2 * pair + side] = result[side]
        return result

    def mix(pair, both):
        values_t = head_pair(packed_ref, pair, features)[2].T
        mixed = [
            dot_nn(values_t[side * HEAD_DIM : (side + 1) * HEAD_DIM], both[side])
            for side in range(2)
        ]
        context_ref[:, pl.ds(pair * lane, lane)] = jnp.concatenate(mixed).astype(jnp.bfloat16).T

    pairs = HEADS // 2
    scores, both = {}, {}
    for step in range(pairs + 2):
        if step < pairs:
            scores[step] = scores_of(step)
        if step >= 2:
            mix(step - 2, both.pop(step - 2))
        if 1 <= step <= pairs:
            both[step - 1] = chances_of(step - 1, scores.pop(step - 1))
    lanes = lax.broadcasted_iota(jnp.int32, stats.shape, 1)

    weight = weights.get(1)
    branch = dot_nn(context_ref[...], weight[...]) + shifts[2:3]
    normal, inverse = normalize(x_buf[...].astype(jnp.float32) + branch)
    n1_ref[...] = normal.astype(jnp.bfloat16)
    first_inverse = inverse
    first = normal * gain_rows[0:1] + shifts[3:4]
    first_low = first.astype(jnp.bfloat16)
    first_ref[...] = first_low
    final_buf[...] = first

    up, down = weights.get(2), weights.get(3)
    last = pl.num_programs(0) - 1

    @pl.when(i < first_passage)
    def _():
        def keep(columns, active_low, slope_low):
            active_ref[:, columns] = active_low
            slope_ref[:, columns] = slope_low

        normal, inverse, final = feed_forward(
            first_ref[...], final_buf, up, down, wide_shift, shifts, gain_rows, keep
        )
        n2_ref[...] = normal.astype(jnp.bfloat16)
        stats[...] = jnp.where(lanes == stat_final, inverse, first_inverse)
        q_states[...] = final.astype(jnp.bfloat16)
        final_buf[...] = final
        for k in range(cls_slots):
            cls[pl.ds(i * cls_slots + k, 1), :] = final_buf[pl.ds(starts[k], 1), :]

    @pl.when(i >= first_passage)
    def _():
        stats[...] = jnp.broadcast_to(first_inverse, stats.shape)
        wide_first[...] = final_buf[...]
        for k in range(cls_slots):
            at = jnp.minimum(starts[k], tokens - 1)
            cls_first[pl.ds((i - first_passage) * cls_slots + k, 1), :] = final_buf[pl.ds(at, 1), :]

    @pl.when(i == last)
    def _():
        _, _, final = feed_forward(
            cls_first[...].astype(jnp.bfloat16), cls_first, up, down, wide_shift, shifts, gain_rows, None
        )
        cls[first_passage * cls_slots :, :] = final


class Back:
    def __init__(self, **refs):
        self.__dict__.update(refs)

    def add_small(self, row, value):
        self.small[pl.ds(row, 1), :] += jnp.sum(value, axis=0, keepdims=True)

    def part_a(self):
        gradient = self.gradient()
        normal = self.n2[...].astype(jnp.float32)
        self.add_small(5, gradient)
        self.add_small(7, gradient * normal)
        total_grad = normalize_back(
            gradient, normal, self.stats[:, stat_final : stat_final + 1], self.gain_rows[1:2]
        )
        second_low = total_grad.astype(jnp.bfloat16)
        self.second[...] = second_low
        self.add_small(4, second_low.astype(jnp.float32))
        self.total[...] = total_grad
        self.feed_forward(0, 2)

    def feed_forward(self, begin, end):
        down, up = self.weight(3), self.weight(2)
        features = self.total.shape[1]
        second_low = self.second[...]
        first_grad = self.total[...]
        for j in range(begin, end):
            columns = pl.ds(j * features, features)
            hidden_grad = dot_nt(second_low, down[columns, :]) * self.slope[:, columns].astype(jnp.float32)
            hidden_low = hidden_grad.astype(jnp.bfloat16)
            self.hidden[:, columns] = hidden_low
            self.add_small(8 + j, hidden_low.astype(jnp.float32))
            first_grad = first_grad + dot_nt(hidden_low, up[:, columns])
        self.total[...] = first_grad

    def part_b(self):
        features = self.total.shape[1]
        self.feed_forward(2, self.hidden.shape[1] // features)
        first_grad = self.total[...]
        normal = self.n1[...].astype(jnp.float32)
        self.add_small(3, first_grad)
        self.add_small(6, first_grad * normal)
        branch_grad = normalize_back(
            first_grad, normal, self.stats[:, stat_first : stat_first + 1], self.gain_rows[0:1]
        )
        self.total[...] = branch_grad
        branch_low = branch_grad.astype(jnp.bfloat16)
        self.branch[...] = branch_low
        self.add_small(2, branch_low.astype(jnp.float32))

    def part_c(self):
        packed_ref, mixed, chances = self.packed, self.mixed, self.chances
        tokens, features = mixed.shape
        mixed_grad = dot_nt(self.branch[...], self.weight(1)[...])
        self.mixed[...] = mixed_grad.astype(jnp.bfloat16)
        heads = lax.broadcasted_iota(jnp.int32, (16, features), 0)
        of_head = lax.broadcasted_iota(jnp.int32, (16, features), 1) // HEAD_DIM == heads
        of_head = jnp.where(of_head, 1.0, 0.0).astype(jnp.bfloat16)
        inner = mixed_grad * self.context[...].astype(jnp.float32)
        inner_high = inner.astype(jnp.bfloat16)
        inner_low = (inner - inner_high.astype(jnp.float32)).astype(jnp.bfloat16)
        inner = dot_nt(of_head, inner_high) + dot_nt(of_head, inner_low)
        left_side = lax.broadcasted_iota(jnp.int32, (tokens, lane), 1) < HEAD_DIM

        def weight_grads(pair):
            values = head_pair(packed_ref, pair, features)[2]
            both = [values * side_mask(side, 1.0) for side in range(2)]
            return dot_nt(jnp.concatenate(both), mixed[:, pl.ds(pair * lane, lane)])

        def score_grads(pair, weight_grad):
            result = []
            for side in range(2):
                h = 2 * pair + side
                part = weight_grad[side * tokens : (side + 1) * tokens] - inner[h : h + 1]
                result.append((chances[h].astype(jnp.float32) * part).astype(jnp.bfloat16))
            return result

        def head_grads(pair, score_low):
            queries, keys, _ = head_pair(packed_ref, pair, features)
            mixed_low = mixed[:, pl.ds(pair * lane, lane)]
            keys_t = keys.T
            query_grad = [
                dot_nn(keys_t[side * HEAD_DIM : (side + 1) * HEAD_DIM], score_low[side])
                for side in range(2)
            ]
            key_grad = dot_nn(jnp.concatenate(score_low), queries)
            both = chances[2 * pair : 2 * pair + 2].reshape(2 * tokens, tokens)
            value_grad = dot_nn(both, mixed_low)
            scale = HEAD_DIM ** (-0.5)
            for j, value in enumerate(
                (
                    (jnp.concatenate(query_grad) * scale).astype(jnp.bfloat16).T,
                    (jnp.where(left_side, key_grad[:tokens], key_grad[tokens:]) * scale).astype(jnp.bfloat16),
                    jnp.where(left_side, value_grad[:tokens], value_grad[tokens:]).astype(jnp.bfloat16),
                )
            ):
                self.packed_grad[:, pl.ds(j * features + pair * lane, lane)] = value

        pairs = HEADS // 2
        raw, low_grads = {}, {}
        for step in range(pairs + 2):
            if step < pairs:
                raw[step] = weight_grads(step)
            if step >= 2:
                head_grads(step - 2, low_grads.pop(step - 2))
            if 1 <= step <= pairs:
                low_grads[step - 1] = score_grads(step - 1, raw.pop(step - 1))

    def part_d(self):
        features = self.total.shape[1]
        self.add_small(0, self.packed_grad[:, :features].astype(jnp.float32))
        self.add_small(1, self.packed_grad[:, 2 * features :].astype(jnp.float32))
        return self.total[...] + dot_nt(self.packed_grad[...], self.weight(0)[...])


def with_cls(gradient, starts, cls_grad, first_row):
    row_at = lax.broadcasted_iota(jnp.int32, (gradient.shape[0], 1), 0)
    for k, start in enumerate(starts):
        gradient = gradient + jnp.where(row_at == start, cls_grad[pl.ds(first_row + k, 1), :], 0.0)
    return gradient


def backward_kernel(
    first_passage, passages,
    lengths,
    *refs,
):
    refs = list(refs)
    q_cot = refs.pop(0)
    p_cot = refs.pop(0) if passages else q_cot
    cls_grad, chances, stats, packed_ref, context_ref, n1_ref, n2_ref, slope_ref = refs[:8]
    projection, mixing, expand, shrink, gains = refs[8:13]
    refs = refs[13:]
    q_grad = refs.pop(0)
    p_grad = refs.pop(0) if passages else q_grad
    second_ref, hidden_ref, branch_ref, packed_grad, small = refs[:5]
    w0, w1, w2, w3, sems, total_buf, context_grad = refs[5:]
    i = pl.program_id(0)
    weights = Weights((projection, mixing, expand, shrink), (w0, w1, w2, w3), sems, i, first_passage, (3, 2, 1, 0), passages)
    weights.begin()

    @pl.when((i == 0) | (i == first_passage))
    def _():
        small[...] = jnp.zeros_like(small)

    def gradient():
        value = jnp.where(i < first_passage, q_cot[...], p_cot[...]).astype(jnp.float32)
        starts = [start_of(lengths, i, first_passage, k) for k in range(cls_slots)]
        return with_cls(value, starts, cls_grad, i * cls_slots)

    block = Back(
        gradient=gradient, chances=chances.at[0], stats=stats, packed=packed_ref, context=context_ref,
        n1=n1_ref, n2=n2_ref, slope=slope_ref, second=second_ref, hidden=hidden_ref, branch=branch_ref,
        packed_grad=packed_grad, small=small.at[0], total=total_buf, mixed=context_grad,
        weight=weights.get, gain_rows=gains[weights.encoder].astype(jnp.float32),
    )
    block.part_a()
    block.part_b()
    block.part_c()
    input_grad = block.part_d()

    @pl.when(i < first_passage)
    def _():
        q_grad[...] = input_grad

    if passages:

        @pl.when(i >= first_passage)
        def _():
            p_grad[...] = input_grad


def block_specs(first_passage):
    q_at = lambda i, lengths: (jnp.minimum(i, first_passage - 1), 0)
    p_at = lambda i, lengths: (jnp.maximum(i - first_passage, 0), 0)
    at = lambda i, lengths: (i, 0)

    def rows(width, index=at):
        return pl.BlockSpec((block_tokens, width), index)

    def lead(*shape):
        return pl.BlockSpec((1,) + shape, lambda i, lengths: (i,) + (0,) * len(shape))

    def whole(array):
        return pl.BlockSpec(array.shape, lambda i, lengths: (0,) * array.ndim)

    anywhere = pl.BlockSpec(memory_space=pl.ANY)
    return q_at, p_at, rows, lead, whole, anywhere


def weight_scratch(stacked, encoders=2):
    return [pltpu.VMEM((encoders,) + w.shape[1:], w.dtype) for w in stacked[:4]] + [pltpu.SemaphoreType.DMA((4, 2))]


def encode_all(lengths, q_rows, p_rows, stacked):
    projection, mixing, expand, shrink, biases, gains, widening = stacked
    features, wide = projection.shape[1], expand.shape[2]
    first_passage = q_rows.shape[0] // block_tokens
    blocks = first_passage + lengths.shape[0]
    q_at, p_at, rows, lead, whole, anywhere = block_specs(first_passage)
    low, tokens = jnp.bfloat16, blocks * block_tokens
    shape = jax.ShapeDtypeStruct
    return pl.pallas_call(
        partial(forward_kernel, first_passage),
        out_shape=[
            shape(q_rows.shape, low),
            shape((blocks * cls_slots, features), jnp.float32),
            shape((blocks, HEADS, block_tokens, block_tokens), low),
            shape((tokens, lane), jnp.float32),
            shape((tokens, 3 * features), low),
            shape((tokens, features), low), shape((tokens, features), low), shape((tokens, features), low),
            shape(p_rows.shape, jnp.float32), shape(q_rows.shape, low),
            shape((q_rows.shape[0], wide), low), shape((q_rows.shape[0], wide), low),
        ],
        grid_spec=pltpu.PrefetchScalarGridSpec(
            num_scalar_prefetch=1,
            grid=(blocks,),
            in_specs=[
                rows(features, q_at), rows(features, p_at), anywhere, anywhere, anywhere, anywhere,
                whole(biases), whole(gains), whole(widening),
            ],
            out_specs=[
                rows(features, q_at),
                pl.BlockSpec((blocks * cls_slots, features), lambda i, lengths: (0, 0)),
                lead(HEADS, block_tokens, block_tokens), rows(lane), rows(3 * features),
                rows(features), rows(features), rows(features), rows(features, p_at),
                rows(features, q_at), rows(wide, q_at), rows(wide, q_at),
            ],
            scratch_shapes=weight_scratch(stacked) + [
                pltpu.VMEM((block_tokens, features), jnp.float32),
                pltpu.VMEM((block_tokens, features), low),
                pltpu.VMEM((p_rows.shape[0] // block_tokens * cls_slots, features), jnp.float32),
            ],
        ),
        compiler_params=pltpu.CompilerParams(
            dimension_semantics=("arbitrary",), vmem_limit_bytes=vmem_bytes
        ),
    )(lengths, q_rows, p_rows, projection, mixing, expand, shrink, biases, gains, widening)


def encode_all_back(lengths, q_cot, p_cot, cls_grad, saved, stacked):
    passages = True
    projection, mixing, expand, shrink, biases, gains, widening = stacked
    chances, stats, packed, context, n1, n2, slope = saved
    features, wide = projection.shape[1], expand.shape[2]
    first_passage = q_cot.shape[0] // block_tokens
    blocks = first_passage + (lengths.shape[0] if passages else 0)
    q_at, p_at, rows, lead, whole, anywhere = block_specs(first_passage)
    low, tokens = jnp.bfloat16, blocks * block_tokens
    shape = jax.ShapeDtypeStruct
    small_rows = 8 + wide // features
    encoders = 1 + passages
    return pl.pallas_call(
        partial(backward_kernel, first_passage, passages),
        out_shape=[shape(q_cot.shape, jnp.float32)] + [shape(p_cot.shape, jnp.float32)] * passages + [
            shape((tokens, features), low), shape((tokens, wide), low),
            shape((tokens, features), low), shape((tokens, 3 * features), low),
            shape((encoders, small_rows, features), jnp.float32),
        ],
        grid_spec=pltpu.PrefetchScalarGridSpec(
            num_scalar_prefetch=1,
            grid=(blocks,),
            in_specs=[rows(features, q_at)] + [rows(features, p_at)] * passages + [
                whole(cls_grad),
                lead(HEADS, block_tokens, block_tokens), rows(lane), rows(3 * features),
                rows(features), rows(features), rows(features), rows(wide),
                anywhere, anywhere, anywhere, anywhere, whole(gains),
            ],
            out_specs=[rows(features, q_at)] + [rows(features, p_at)] * passages + [
                rows(features), rows(wide), rows(features), rows(3 * features),
                pl.BlockSpec(
                    (1, small_rows, features),
                    lambda i, lengths: ((i >= first_passage).astype(jnp.int32), 0, 0),
                ),
            ],
            scratch_shapes=weight_scratch(stacked, encoders) + [
                pltpu.VMEM((block_tokens, features), jnp.float32),
                pltpu.VMEM((block_tokens, features), low),
            ],
        ),
        compiler_params=pltpu.CompilerParams(
            dimension_semantics=("arbitrary",), vmem_limit_bytes=vmem_bytes
        ),
    )(
        lengths, q_cot, *[p_cot] * passages, cls_grad, chances, stats, packed, context, n1, n2, slope,
        projection, mixing, expand, shrink, gains,
    )


def contrast_kernel(
    first_passage,
    cls, positives, loss_weight, negatives, biases, gains, widening, first, wide_first, stats, expand, shrink,
    cls_grad, loss, p_states, p_stats, p_n2, p_active, p_slope,
    q_all, p_all, stat_all, row_send, row_recv, col_send, col_recv, q_wide, q_low,
    q_ss, q_rs, p_ss, p_rs, stat_ss, stat_rs, row_ss, row_rs, col_ss, col_rs,
    up, down, f_first, f_wide, f_stats, f_states, f_stats_out, f_n2, f_active, f_slope, weight_sem, in_sem, out_sem,
):
    size_pa, size_pb = lax.axis_size("pa"), lax.axis_size("pb")
    pa, pb = lax.axis_index("pa"), lax.axis_index("pb")
    features = cls.shape[1]
    half = features // 2
    own_q = q_all.shape[1] // 2
    own_p = p_all.shape[1]
    far_a = [(d, lax.rem(pa + d, size_pa)) for d in range(1, size_pa)]
    far_b = [(d, lax.rem(pb + d, size_pb)) for d in range(1, size_pb)]

    blocks = wide_first.shape[0] // block_tokens
    weight_copies = [
        pltpu.make_async_copy(source.at[1], buffer, weight_sem.at[i])
        for i, (source, buffer) in enumerate(((expand, up), (shrink, down)))
    ]
    shifts = biases[1].astype(jnp.float32)
    gain_rows = gains[1].astype(jnp.float32)
    wide_shift = widening[...].astype(jnp.float32)[1:2]

    def loads(b):
        own, every = pl.ds(b * block_tokens, block_tokens), pl.ds((first_passage + b) * block_tokens, block_tokens)
        pairs = ((first.at[every], f_first), (wide_first.at[own], f_wide), (stats.at[every], f_stats))
        return [
            pltpu.make_async_copy(src, dst.at[b % 2], in_sem.at[b % 2, i]) for i, (src, dst) in enumerate(pairs)
        ]

    def stores(b):
        own = pl.ds(b * block_tokens, block_tokens)
        pairs = (
            (f_states, p_states), (f_stats_out, p_stats), (f_n2, p_n2), (f_active, p_active), (f_slope, p_slope)
        )
        return [
            pltpu.make_async_copy(src.at[b % 2], dst.at[own], out_sem.at[b % 2, i]) for i, (src, dst) in enumerate(pairs)
        ]

    def encode_block(b):
        if b >= blocks:
            return
        slot = b % 2
        if b == 0:
            for copy in weight_copies:
                copy.wait()
        for copy in loads(b):
            copy.wait()
        if b >= 2:
            for copy in stores(b - 2):
                copy.wait()

        def keep(columns, active_low, slope_low):
            f_active[slot, :, columns] = active_low
            f_slope[slot, :, columns] = slope_low

        normal, inverse, final = feed_forward(
            f_first[slot], f_wide.at[slot], up, down, wide_shift, shifts, gain_rows, keep
        )
        lanes = lax.broadcasted_iota(jnp.int32, f_stats.shape[1:], 1)
        f_n2[slot] = normal.astype(jnp.bfloat16)
        f_states[slot] = final.astype(jnp.bfloat16)
        f_stats_out[slot] = jnp.where(lanes == stat_final, inverse, f_stats[slot])
        for copy in stores(b) + (loads(b + 2) if b + 2 < blocks else []):
            copy.start()

    for copy in weight_copies + loads(0) + (loads(1) if blocks > 1 else []):
        copy.start()

    barrier = pltpu.get_barrier_semaphore()
    for _, a in far_a:
        pl.semaphore_signal(barrier, inc=1, device_id=(pb, a), device_id_type=MESH)
    for _, b in far_b:
        pl.semaphore_signal(barrier, inc=1, device_id=(b, pa), device_id_type=MESH)
    pl.semaphore_wait(barrier, size_pa + size_pb - 2)

    def to_a(src, dst, ss, rs, d, a):
        return pltpu.make_async_remote_copy(
            src_ref=src, dst_ref=dst, send_sem=ss.at[d], recv_sem=rs.at[d], device_id=(pb, a), device_id_type=MESH
        )

    def to_b(src, dst, ss, rs, d, b):
        return pltpu.make_async_remote_copy(
            src_ref=src, dst_ref=dst, send_sem=ss.at[d], recv_sem=rs.at[d], device_id=(b, pa), device_id_type=MESH
        )

    def fold(block):
        return jnp.concatenate([block[:, :half], block[:, half:]], axis=0).astype(jnp.bfloat16)

    q_all[pa] = fold(cls[:own_q, :])
    p_all[pb] = cls[own_q:, :].astype(jnp.bfloat16)
    copies = [to_a(q_all.at[pa], q_all.at[pa], q_ss, q_rs, d, a) for d, a in far_a]
    copies += [to_b(p_all.at[pb], p_all.at[pb], p_ss, p_rs, d, b) for d, b in far_b]
    for copy in copies:
        copy.start()
    encode_block(0)
    for copy in copies:
        copy.wait()
    for a in range(size_pa):
        block = q_all[a].astype(jnp.float32)
        q_wide[pl.ds(a * own_q, own_q), :half] = block[:own_q]
        q_wide[pl.ds(a * own_q, own_q), half:] = block[own_q:]
    q_low[...] = q_wide[...].astype(jnp.bfloat16)

    tile_scale = 2.0 / math.sqrt(features)
    count = q_low.shape[0]
    p_rows = p_all[...].reshape(size_pb * own_p, features)
    row = lax.broadcasted_iota(jnp.int32, (size_pb * own_p, count), 0)
    slot = row % cls_slots
    valid = slot < cls_slots - 1
    place = row % own_p // cls_slots
    owner = row // own_p * size_pa + pa
    identity = (owner * (own_p // cls_slots) + place) * (cls_slots - 1) + slot
    chosen = jnp.where(valid & (identity == positives[...]), 1.0, 0.0)
    p_scores = dot_nt(p_rows, q_low[...]) * tile_scale
    p_scores = jnp.where(valid, p_scores, -1e30)
    n_scores = dot_nt(negatives[...], q_low[...]) * tile_scale
    top = jnp.maximum(
        jnp.max(p_scores, axis=0, keepdims=True), jnp.max(n_scores, axis=0, keepdims=True)
    )
    mass = jnp.sum(jnp.exp(p_scores - top), axis=0, keepdims=True)
    mass = mass + jnp.sum(jnp.exp(n_scores - top), axis=0, keepdims=True)
    picked = jnp.sum(jnp.where(chosen > 0.0, p_scores, 0.0), axis=0, keepdims=True)
    stat_all[pa] = jnp.concatenate([top, mass, picked] + [jnp.zeros_like(top)] * 5, axis=0)
    copies = [to_a(stat_all.at[pa], stat_all.at[pa], stat_ss, stat_rs, d, a) for d, a in far_a]
    for copy in copies:
        copy.start()
    encode_block(1)
    for copy in copies:
        copy.wait()
    all_top = stat_all[0, 0:1]
    for a in range(1, size_pa):
        all_top = jnp.maximum(all_top, stat_all[a, 0:1])
    all_mass = jnp.zeros_like(all_top)
    all_picked = jnp.zeros_like(all_top)
    for a in range(size_pa):
        all_mass = all_mass + stat_all[a, 1:2] * jnp.exp(stat_all[a, 0:1] - all_top)
        all_picked = all_picked + stat_all[a, 2:3]
    logsum = all_top + jnp.log(all_mass)
    loss[...] = logsum - all_picked

    p_tile = (loss_weight[...] * (jnp.exp(p_scores - logsum) - chosen)).astype(jnp.bfloat16)
    n_tile = (loss_weight[...] * jnp.exp(n_scores - logsum)).astype(jnp.bfloat16)
    q_wide[...] = (dot_tn(p_tile, p_rows) + dot_tn(n_tile, negatives[...])) * tile_scale
    col_send[...] = (dot_nn(p_tile, q_low[...]) * tile_scale).reshape(col_send.shape)
    for a in range(size_pa):
        row_send[a] = fold(q_wide[pl.ds(a * own_q, own_q), :])
    copies = [to_a(row_send.at[a], row_recv.at[pa], row_ss, row_rs, d, a) for d, a in far_a]
    copies += [to_b(col_send.at[b], col_recv.at[pb], col_ss, col_rs, d, b) for d, b in far_b]
    for copy in copies:
        copy.start()
    for b in range(2, blocks):
        encode_block(b)
    for copy in copies:
        copy.wait()
    row_recv[pa] = row_send[pa]
    col_recv[pb] = col_send[pb]
    total = row_recv[0].astype(jnp.float32)
    for a in range(1, size_pa):
        total = total + row_recv[a].astype(jnp.float32)
    cls_grad[:own_q, :half] = total[:own_q]
    cls_grad[:own_q, half:] = total[own_q:]
    total = col_recv[0]
    for b in range(1, size_pb):
        total = total + col_recv[b]
    cls_grad[own_q:, :] = total
    for b in range(max(blocks - 2, 0), blocks):
        for copy in stores(b):
            copy.wait()


def contrast(cls, own_q, positives, loss_weight, negatives, first, wide_first, stats, stacked):
    projection, mixing, expand, shrink, biases, gains, widening = stacked
    size_pa, size_pb = lax.axis_size("pa"), lax.axis_size("pb")
    slots, features = cls.shape
    own_p, count = slots - own_q, positives.shape[0]
    low, wide, dma = jnp.bfloat16, jnp.float32, pltpu.SemaphoreType.DMA
    folded = (size_pa, 2 * own_q, features // 2)
    sems = [dma((size_pa,))] * 2 + [dma((size_pb,))] * 2 + [dma((size_pa,))] * 4 + [dma((size_pb,))] * 2
    tokens, units = wide_first.shape[0], expand.shape[2]
    shape = jax.ShapeDtypeStruct
    vmem, anywhere = pl.BlockSpec(memory_space=pltpu.VMEM), pl.BlockSpec(memory_space=pl.ANY)
    two = lambda width, kind: pltpu.VMEM((2, block_tokens, width), kind)
    cls_grad, loss, p_states, *p_side = pl.pallas_call(
        partial(contrast_kernel, (first.shape[0] - tokens) // block_tokens),
        out_shape=[
            shape(cls.shape, wide), shape((1, count), wide),
            shape((tokens, features), low), shape((tokens, lane), wide), shape((tokens, features), low),
            shape((tokens, units), low), shape((tokens, units), low),
        ],
        in_specs=[vmem] * 7 + [anywhere] * 5,
        out_specs=[vmem] * 2 + [anywhere] * 5,
        scratch_shapes=[
            pltpu.VMEM(folded, low),
            pltpu.VMEM((size_pb, own_p, features), low),
            pltpu.VMEM((size_pa, 8, count), wide),
            pltpu.VMEM(folded, low),
            pltpu.VMEM(folded, low),
            pltpu.VMEM((size_pb, own_p, features), wide),
            pltpu.VMEM((size_pb, own_p, features), wide),
            pltpu.VMEM((count, features), wide),
            pltpu.VMEM((count, features), low),
        ] + sems + [
            pltpu.VMEM(expand.shape[1:], low), pltpu.VMEM(shrink.shape[1:], low),
            two(features, low), two(features, wide), two(lane, wide),
            two(features, low), two(lane, wide), two(features, low), two(units, low), two(units, low),
            dma((2,)), dma((2, 3)), dma((2, 5)),
        ],
        compiler_params=pltpu.CompilerParams(
            collective_id=2, has_side_effects=True, vmem_limit_bytes=vmem_bytes
        ),
    )(
        cls, positives[None, :], loss_weight[None, :], negatives, biases, gains, widening,
        first, wide_first, stats, expand, shrink,
    )
    return cls_grad, loss[0], p_states, p_side


panel_rows = 48
chunk_panels = 8
encoder_chunks = 9


ring = 6


def reduce_kernel(
    tokens,
    q_active, p_active, first, context, q_rows, p_rows,
    q_cot, p_cot, chances, q_stats, p_stats, packed, n1, q_n2, p_n2, q_slope, p_slope,
    projection, mixing, expand, shrink,
    lengths, cls_grad, gains,
    second, hidden, branch, packed_grad, q_grad, p_grad,
    projection_out, mixing_out, expand_out, shrink_out, small_out,
    keep, core_send, core_recv, recv_x, recv_ya, recv_za, recv_yb, recv_zb, fin_a, fin_b,
    left_buf, left_t, right_buf, product, small_recv, small_sum,
    load_sem, core_ss, core_rs, xa_ss, xa_rs, ya_ss, ya_rs, za_ss, za_rs, ag_ss, ag_rs,
    yb_ss, yb_rs, zb_ss, zb_rs, xb_ss, xb_rs, small_ss, small_rs, credit,
    w0, w1, w2, w3, weight_sem, in_sem, out_sem,
    b_cot, b_stats, b_n1, b_n2, b_slope, b_second, b_hidden, b_branch, b_total,
    b_chances, b_packed, b_context, b_branch_in, b_total_in, b_packed_grad, b_grad, b_mixed,
):
    chunks = 2 * encoder_chunks
    pb, pa = lax.axis_index("pb"), lax.axis_index("pa")
    core, y, z, x = pa % 2, pa // 2 % 2, pa // 4, pb
    at_core = (pb, pa + 1 - 2 * core)
    at_y = (pb, pa + 2 - 4 * y)
    at_x = (1 - pb, pa)
    far_z = [(z + d) % 4 for d in (1, 2, 3)]
    at_z = [(pb, t * 4 + y * 2 + core) for t in far_z]

    def remote(src, dst, ss, rs, device):
        return pltpu.make_async_remote_copy(
            src_ref=src, dst_ref=dst, send_sem=ss, recv_sem=rs, device_id=device, device_id_type=MESH
        )

    def copy_core(c):
        return remote(core_send.at[c % 2], core_recv.at[c % 2], core_ss.at[c], core_rs.at[c], at_core)

    def copy_xa(c):
        return remote(keep.at[c % ring, pl.ds(2 * (1 - x), 2)], recv_x.at[c % ring], xa_ss.at[c], xa_rs.at[c], at_x)

    def copy_ya(c):
        return remote(
            keep.at[c % ring, pl.ds(2 * x, 2), :, 1 - y], recv_ya.at[c % ring], ya_ss.at[c], ya_rs.at[c], at_y
        )

    def copy_za(c, d):
        return remote(
            keep.at[c % ring, pl.ds(2 * x, 2), far_z[d], y], recv_za.at[c % ring, d], za_ss.at[c, d], za_rs.at[c, d], at_z[d]
        )

    def copy_ag(c):
        half = fin_a.at[c % ring, pl.ds(2 * x, 2)]
        return remote(half, half, ag_ss.at[c], ag_rs.at[c], at_x)

    def copy_yb(c):
        return remote(keep.at[c % ring, pl.ds(4, 4), :, 1 - y], recv_yb.at[c % ring], yb_ss.at[c], yb_rs.at[c], at_y)

    def copy_zb(c, d):
        return remote(
            keep.at[c % ring, pl.ds(4, 4), far_z[d], y], recv_zb.at[c % ring, d], zb_ss.at[c, d], zb_rs.at[c, d], at_z[d]
        )

    def copy_xb(c):
        return remote(fin_b.at[c % ring, x], fin_b.at[c % ring, x], xb_ss.at[c], xb_rs.at[c], at_x)

    def small_copy(stage, device):
        source = small_sum.at[max(stage - 3, 0) if stage >= 3 else stage]
        return remote(source, small_recv.at[stage], small_ss.at[stage], small_rs.at[stage], device)

    order = [(e, k) for e in range(2) for k in (3, 4, 5, 0, 1, 2, 6, 7, 8)]
    place = {what: c for c, what in enumerate(order)}

    def own(e, ref):
        return ref.at[pl.ds(0 if e == 0 else tokens[0], tokens[e])]

    def left_loads(e, part):
        count = tokens[e]
        features = q_rows.shape[1]
        if part == 0:
            pairs = [((q_active, p_active)[e], 0)]
        elif part == 1:
            pairs = [(own(e, first), 0)]
        else:
            pairs = [((q_rows, p_rows)[e], 0), (own(e, context), features)]
        return [
            pltpu.make_async_copy(
                ref,
                left_buf.at[pl.ds(0, count), pl.ds(at, ref.shape[1])],
                load_sem.at[2 + i],
            )
            for i, (ref, at) in enumerate(pairs)
        ]

    def right_loads(e, k):
        count = tokens[e]
        slot = place[e, k] % 2
        if k < 3:
            pairs = [(second, 256 * k, 256, 0)]
        elif k < 6:
            pairs = [(hidden, 1024 * (k - 3), 1024, 0)]
        elif k < 8:
            pairs = [(packed_grad, 1024 * (k - 6), 1024, 0)]
        else:
            pairs = [(packed_grad, 2048, 256, 0), (branch, 0, 768, 256)]
        return [
            pltpu.make_async_copy(
                own(e, ref).at[:, pl.ds(start, width)],
                right_buf.at[slot, pl.ds(0, count), pl.ds(at, width)],
                load_sem.at[slot] if i == 0 else load_sem.at[4],
            )
            for i, (ref, start, width, at) in enumerate(pairs)
        ]

    def begin(copies):
        for copy in copies:
            copy.start()

    def finish(copies):
        for copy in copies:
            copy.wait()

    def transpose_left(e, part):
        count = tokens[e]
        width = (3072, 768, 1536)[part]

        def step(i, carry):
            at = pl.multiple_of(i * 256, 256)
            left_t[pl.ds(at, 256), pl.ds(0, count)] = left_buf[pl.ds(0, count), pl.ds(at, 256)].T
            return carry

        lax.fori_loop(0, width // 256, step, 0)

    def compute(e, k):
        count = tokens[e]
        c = place[e, k]
        slot = c % 2

        def step(q, carry):
            if k < 3:
                rows_at, columns_at = q * 768, 0
            elif k < 8:
                rows_at, columns_at = 0, q * 256
            else:
                rows_at, columns_at = jnp.where(q > 0, 768, 0), q * 256
            rows_at = pl.multiple_of(rows_at, 256)
            columns_at = pl.multiple_of(columns_at, 256)
            product[...] = jnp.dot(
                left_t[pl.ds(rows_at, 768), pl.ds(0, count)],
                right_buf[slot, pl.ds(0, count), pl.ds(columns_at, 256)],
                preferred_element_type=jnp.float32,
            )
            if k < 3:
                for iy in range(2):
                    for sub in range(4):
                        for which, target in ((core, keep.at[c % ring]), (1 - core, core_send.at[slot])):
                            at = pl.multiple_of((2 * iy + which) * 192 + sub * 48, 16)
                            block = product[pl.ds(at, 48), :].astype(jnp.bfloat16)
                            target[sub * 2, q, iy] = block[:, :lane]
                            target[sub * 2 + 1, q, iy] = block[:, lane:]
            else:
                for iz in range(4):
                    for iy in range(2):
                        for which, target in ((core, keep.at[c % ring]), (1 - core, core_send.at[slot])):
                            at = pl.multiple_of((4 * iz + 2 * iy + which) * 48, 16)
                            block = product[pl.ds(at, 48), :].astype(jnp.bfloat16)
                            target[2 * q, iz, iy] = block[:, :lane]
                            target[2 * q + 1, iz, iy] = block[:, lane:]
            return carry

        lax.fori_loop(0, 4, step, 0)

    part_of = lambda k: 0 if k < 3 else 1 if k < 6 else 2

    def produce(c):
        e, k = order[c]
        if c >= 2:
            copy_core(c - 2).wait_send()
        if k % 3 == 0:
            finish(left_loads(e, part_of(k)))
            transpose_left(e, part_of(k))
            if c + 3 < chunks:
                e2, k2 = order[c + 3]
                begin(left_loads(e2, part_of(k2)))
        try_right(c)
        finish(right_loads(e, k))
        compute(e, k)
        if c >= 2:
            pl.semaphore_wait(credit, 1)
        copy_core(c).start()

    def write(c, panel, value):
        e, k = order[c]
        if k < 3:
            rows = pl.ds(panel // 2 * panel_rows, panel_rows)
            shrink_out[e, rows, pl.ds(256 * k + panel % 2 * lane, lane)] = value
        elif k < 6:
            expand_out[e, :, pl.ds(1024 * (k - 3) + panel * lane, lane)] = value
        else:
            at = 1024 * (k - 6) + panel * lane
            width = projection_out.shape[2]
            if at < width:
                projection_out[e, :, pl.ds(at, lane)] = value
            else:
                mixing_out[e, :, pl.ds(at - width, lane)] = value

    def after_core(c):
        copy_core(c).wait_recv()

        def step(p, carry):
            keep[c % ring, p] = keep[c % ring, p] + core_recv[c % 2, p]
            return carry

        lax.fori_loop(0, chunk_panels, step, 0)
        copy_xa(c).start()
        copy_yb(c).start()

        if c < chunks - 2:
            pl.semaphore_signal(credit, inc=1, device_id=at_core, device_id_type=MESH)

    def after_first(c):
        copy_yb(c).wait_recv()

        def step_b(p, carry):
            for iz in range(4):
                keep[c % ring, 4 + p, iz, y] = keep[c % ring, 4 + p, iz, y] + recv_yb[c % ring, p, iz]
            return carry

        lax.fori_loop(0, 4, step_b, 0)
        for d in range(3):
            copy_zb(c, d).start()
        copy_xa(c).wait_recv()

        def step_a(p, carry):
            keep[c % ring, 2 * x + p] = keep[c % ring, 2 * x + p] + recv_x[c % ring, p]
            return carry

        lax.fori_loop(0, 2, step_a, 0)
        copy_ya(c).start()

    def widen(value):
        return value.astype(jnp.float32)

    def after_second(c):
        copy_ya(c).wait_recv()

        def step_a(p, carry):
            for iz in range(4):
                keep[c % ring, 2 * x + p, iz, y] = keep[c % ring, 2 * x + p, iz, y] + recv_ya[c % ring, p, iz]
            return carry

        lax.fori_loop(0, 2, step_a, 0)
        for d in range(3):
            copy_za(c, d).start()
        for d in range(3):
            copy_zb(c, d).wait_recv()

        def step_b(p, carry):
            fin_b[c % ring, x, p] = (
                widen(keep[c % ring, 4 + p, z, y])
                + widen(recv_zb[c % ring, 0, p])
                + widen(recv_zb[c % ring, 1, p])
                + widen(recv_zb[c % ring, 2, p])
            ).astype(jnp.bfloat16)
            return carry

        lax.fori_loop(0, 4, step_b, 0)
        copy_xb(c).start()

    def after_third(c):
        for d in range(3):
            copy_za(c, d).wait_recv()

        def step_a(p, carry):
            fin_a[c % ring, 2 * x + p] = (
                widen(keep[c % ring, 2 * x + p, z, y])
                + widen(recv_za[c % ring, 0, p])
                + widen(recv_za[c % ring, 1, p])
                + widen(recv_za[c % ring, 2, p])
            ).astype(jnp.bfloat16)
            return carry

        lax.fori_loop(0, 2, step_a, 0)
        copy_ag(c).start()
        copy_xb(c).wait_recv()

        for p in range(4):
            write(c, 4 + p, widen(fin_b[c % ring, 0, p]) + widen(fin_b[c % ring, 1, p]))

    def after_last(c):
        copy_ag(c).wait_recv()
        copy_xa(c).wait_send()
        copy_ya(c).wait_send()
        copy_ag(c).wait_send()
        copy_yb(c).wait_send()
        copy_xb(c).wait_send()
        for d in range(3):
            copy_za(c, d).wait_send()
            copy_zb(c, d).wait_send()

        for p in range(4):
            write(c, p, widen(fin_a[c % ring, p]))

    q_blocks = tokens[0] // block_tokens
    blocks = (tokens[0] + tokens[1]) // block_tokens
    buffers = (w0, w1, w2, w3)

    def weight_copy(which, e):
        source = (projection, mixing, expand, shrink)[which]
        return pltpu.make_async_copy(source.at[e], buffers[which], weight_sem.at[which])

    def rows_of(b):
        return pl.ds(b * block_tokens, block_tokens)

    def input_rows(b, q_ref, p_ref):
        return q_ref.at[rows_of(b)] if b < q_blocks else p_ref.at[rows_of(b - q_blocks)]

    def copies(pairs, sem):
        return [pltpu.make_async_copy(src, dst, sem) for (src, dst), sem in pairs]

    def loads(half, b):
        at = rows_of(b)
        if half == 0:
            pairs = [
                (input_rows(b, *refs), buffer)
                for refs, buffer in (
                    ((q_cot, p_cot), b_cot), ((q_n2, p_n2), b_n2), ((q_stats, p_stats), b_stats), ((q_slope, p_slope), b_slope)
                )
            ] + [(n1.at[at], b_n1)]
        else:
            pairs = [(input_rows(b, q_grad, p_grad), b_total_in), (chances.at[b], b_chances)]
            pairs += [(ref.at[at], buffer) for ref, buffer in ((branch, b_branch_in), (packed, b_packed), (context, b_context))]
        return [pltpu.make_async_copy(src, dst, in_sem.at[half, i]) for i, (src, dst) in enumerate(pairs)]

    def stores(half, b):
        at = rows_of(b)
        if half == 0:
            pairs = [(b_second, second.at[at]), (b_hidden, hidden.at[at]), (b_branch, branch.at[at]), (b_total, input_rows(b, q_grad, p_grad))]
        else:
            pairs = [(b_packed_grad, packed_grad.at[at]), (b_grad, input_rows(b, q_grad, p_grad))]
        return [pltpu.make_async_copy(src, dst, out_sem.at[half, i]) for i, (src, dst) in enumerate(pairs)]

    stored, done, started, waited = set(), set(), set(), set()

    def settle(half, b):
        if (half, b) in done and (half, b) not in stored:
            stored.add((half, b))
            finish(stores(half, b))

    def start_loads(half, b, which):
        if b < blocks and (half == 0 or (0, b) in done):
            if half == 1:
                settle(0, b)
            for i in which:
                if (half, b, i) not in started:
                    started.add((half, b, i))
                    loads(half, b)[i].start()

    def weight_of(e):
        def get(which):
            if (which, e) not in waited:
                waited.add((which, e))
                weight_copy(which, e).wait()
            return buffers[which]

        return get

    def part(b, which):
        e = int(b >= q_blocks)
        half = which // 2

        def gradient():
            at = jnp.zeros((1, 1), jnp.int32)
            starts = []
            for k in range(cls_slots):
                if e == 0:
                    starts.append(k * (block_tokens // cls_slots))
                else:
                    starts.append(at)
                    if k < cls_slots - 1:
                        at = at + lengths[pl.ds(b - q_blocks, 1), pl.ds(k, 1)]
            return with_cls(b_cot[...].astype(jnp.float32), starts, cls_grad, b * cls_slots)

        rows = small_sum.shape[1] // 2
        block = Back(
            gradient=gradient, chances=b_chances, stats=b_stats, packed=b_packed, context=b_context,
            n1=b_n1, n2=b_n2, slope=b_slope, second=b_second, hidden=b_hidden,
            branch=b_branch if half == 0 else b_branch_in, packed_grad=b_packed_grad,
            small=small_sum.at[0, pl.ds(e * rows, rows)], total=b_total if half == 0 else b_total_in,
            mixed=b_mixed, weight=weight_of(e), gain_rows=gains[e].astype(jnp.float32),
        )
        if which % 2 == 0:
            start_loads(half, b, range(5))
            finish(loads(half, b)[:4] if half == 0 else loads(half, b)[1:])
            if b > 0:
                settle(half, b - 1)
        else:
            finish(loads(half, b)[4:] if half == 0 else loads(half, b)[:1])
        if which == 0:
            block.part_a()
        elif which == 1:
            block.part_b()
        elif which == 2:
            block.part_c()
        else:
            b_grad[...] = block.part_d()
        if which == 0:
            start_loads(0, b + 1, range(2))
        elif which == 2:
            start_loads(1, b + 1, range(1, 5))
        if which % 2 == 1:
            begin(stores(half, b))
            done.add((half, b))
            start_loads(half, b + 1, range(5))
            if half == 0:
                start_loads(1, b, range(1, 5) if b == 0 else ())
            if b + 1 == q_blocks:
                for again in ((3, 2), (1, 0))[half]:
                    weight_copy(again, 1).start()

    right_begun = set()

    def try_right(c):
        if c >= chunks or c in right_begun:
            return
        e, k = order[c]
        half = int(k >= 6)
        mine = range(q_blocks) if e == 0 else range(q_blocks, blocks)
        if all((half, b) in done for b in mine):
            for b in mine:
                settle(half, b)
            right_begun.add(c)
            begin(right_loads(e, k))

    start_loads(0, 0, range(5))
    begin([weight_copy(which, 0) for which in (3, 2)])
    barrier = pltpu.get_barrier_semaphore()
    for device in [at_core, at_y, at_x] + at_z:
        pl.semaphore_signal(barrier, inc=1, device_id=device, device_id_type=MESH)
    pl.semaphore_wait(barrier, 6)
    small_sum[0] = jnp.zeros(small_out.shape, jnp.float32)
    begin(left_loads(order[0][0], part_of(order[0][1])))
    part(0, 0)
    begin([weight_copy(which, 0) for which in (1, 0)])
    part(0, 1)
    for b in range(1, q_blocks):
        part(b, 0)
        part(b, 1)

    first_ones = [(b, which) for b in range(q_blocks) for which in (2, 3)]
    then = [(b, which) for b in range(q_blocks, blocks) for which in (0, 1)]
    early = [item for both in zip(first_ones, then) for item in both] + then[len(first_ones):]
    late = [(b, which) for b in range(q_blocks, blocks) for which in (2, 3)]
    points = {}
    for todo, begin_at, end_at in ((early, 1, encoder_chunks - 1), (late, encoder_chunks, encoder_chunks + 5)):
        spots = [(c, i) for c in range(begin_at, end_at + 1) for i in range(2)][: 2 * (end_at - begin_at) + 1]
        for i, item in enumerate(todo):
            points.setdefault(spots[i * len(spots) // len(todo)], []).append(item)

    def parts(c, i):
        for item in points.get((c, i), []):
            part(*item)

    for c in range(chunks + 5):
        if c < chunks:
            produce(c)
        if 0 <= c - 1 < chunks:
            after_core(c - 1)
        parts(c, 0)
        try_right(c + 1)
        if 0 <= c - 2 < chunks:
            after_first(c - 2)
        if 0 <= c - 3 < chunks:
            after_second(c - 3)
        parts(c, 1)
        if 0 <= c - 4 < chunks:
            after_third(c - 4)
        if 0 <= c - 5 < chunks:
            after_last(c - 5)
        if c == encoder_chunks + 6:
            for b in range(blocks):
                for half in range(2):
                    settle(half, b)
            small_copy(0, at_core).start()
        if c == encoder_chunks + 7:
            small_copy(0, at_core).wait_recv()
            small_sum[1] = small_sum[0] + small_recv[0]
            small_copy(1, at_x).start()
        if c == encoder_chunks + 8:
            small_copy(1, at_x).wait_recv()
            small_sum[2] = small_sum[1] + small_recv[1]
            small_copy(2, at_y).start()
        if c == encoder_chunks + 9:
            small_copy(2, at_y).wait_recv()
            small_sum[3] = small_sum[2] + small_recv[2]
            for d in range(3):
                remote(small_sum.at[3], small_recv.at[3 + d], small_ss.at[3 + d], small_rs.at[3 + d], at_z[d]).start()
        if c == encoder_chunks + 10:
            for d in range(3):
                remote(small_sum.at[3], small_recv.at[3 + d], small_ss.at[3 + d], small_rs.at[3 + d], at_z[d]).wait_recv()
            result = jnp.zeros(small_out.shape, jnp.float32)
            for iz in range(4):
                back = (z - iz + 4) % 4
                value = jnp.where(back == 0, small_sum[3], 0.0)
                for d in range(3):
                    value = jnp.where(back == d + 1, small_recv[3 + d], value)
                result = result + value
            small_out[...] = result

    copy_core(chunks - 2).wait_send()
    copy_core(chunks - 1).wait_send()

    small_copy(0, at_core).wait_send()
    small_copy(1, at_x).wait_send()
    small_copy(2, at_y).wait_send()
    for d in range(3):
        remote(small_sum.at[3], small_recv.at[3 + d], small_ss.at[3 + d], small_rs.at[3 + d], at_z[d]).wait_send()


def reduce_by_kernel(lengths, q_rows, p_rows, q_cot, p_cot, cls_grad, saved, stacked):
    projection, mixing, expand, shrink, biases, gains, widening = stacked
    chances, packed, context, first, n1, q_side, p_side = saved
    (q_stats, q_n2, q_active, q_slope), (p_stats, p_n2, p_active, p_slope) = q_side, p_side
    features, wide = projection.shape[1], expand.shape[2]
    tokens = (q_rows.shape[0], p_rows.shape[0])
    all_tokens = sum(tokens)
    small = jax.ShapeDtypeStruct((2 * (-(-(8 + wide // features) // 8) * 8), features), jnp.float32)
    most = max(tokens)
    chunks = 2 * encoder_chunks
    tile = (panel_rows, lane)
    low = jnp.bfloat16
    dma = pltpu.SemaphoreType.DMA
    one, three = dma((chunks,)), dma((chunks, 3))
    block = lambda width, kind=low: pltpu.VMEM((block_tokens, width), kind)
    shape = jax.ShapeDtypeStruct
    return pl.pallas_call(
        partial(reduce_kernel, tokens),
        out_shape=[
            shape((all_tokens, features), low), shape((all_tokens, wide), low),
            shape((all_tokens, features), low), shape((all_tokens, 3 * features), low),
            shape(q_cot.shape, jnp.float32), shape(p_cot.shape, jnp.float32),
            shape((2, 48, 2304), jnp.float32),
            shape((2, 48, 768), jnp.float32),
            shape((2, 48, 3072), jnp.float32),
            shape((2, 192, 768), jnp.float32),
            small,
        ],
        in_specs=[pl.BlockSpec(memory_space=pl.ANY)] * 21 + [pl.BlockSpec(memory_space=pltpu.VMEM)] * 3,
        out_specs=[pl.BlockSpec(memory_space=pl.ANY)] * 6 + [pl.BlockSpec(memory_space=pltpu.VMEM)] * 5,
        scratch_shapes=[
            pltpu.VMEM((ring, chunk_panels, 4, 2) + tile, low),
            pltpu.VMEM((2, chunk_panels, 4, 2) + tile, low),
            pltpu.VMEM((2, chunk_panels, 4, 2) + tile, low),
            pltpu.VMEM((ring, 2, 4, 2) + tile, low),
            pltpu.VMEM((ring, 2, 4) + tile, low),
            pltpu.VMEM((ring, 3, 2) + tile, low),
            pltpu.VMEM((ring, 4, 4) + tile, low),
            pltpu.VMEM((ring, 3, 4) + tile, low),
            pltpu.VMEM((ring, 4) + tile, low),
            pltpu.VMEM((ring, 2, 4) + tile, low),
            pltpu.VMEM((most, 3072), low),
            pltpu.VMEM((3072, most), low),
            pltpu.VMEM((2, most, 1024), low),
            pltpu.VMEM((768, 256), jnp.float32),
            pltpu.VMEM((6,) + small.shape, jnp.float32),
            pltpu.VMEM((4,) + small.shape, jnp.float32),
            dma((5,)),
            one, one, one, one, one, one, three, three, one, one,
            one, one, three, three, one, one, dma((6,)), dma((6,)),
            pltpu.SemaphoreType.REGULAR,
        ] + [pltpu.VMEM(w.shape[1:], low) for w in (projection, mixing, expand, shrink)] + [
            dma((4,)), dma((2, 5)), dma((2, 4)),
            block(features), block(lane, jnp.float32), block(features), block(features), block(wide),
            block(features), block(wide), block(features), block(features, jnp.float32),
            pltpu.VMEM((HEADS, block_tokens, block_tokens), low), block(3 * features), block(features),
            block(features), block(features, jnp.float32), block(3 * features), block(features, jnp.float32),
            block(features),
        ],
        compiler_params=pltpu.CompilerParams(
            collective_id=1, has_side_effects=True, vmem_limit_bytes=vmem_bytes
        ),
        cost_estimate=pl.CostEstimate(flops=50 * 10**9, bytes_accessed=200 * 10**6, transcendentals=0),
    )(
        q_active, p_active, first, context, q_rows, p_rows, q_cot, p_cot, chances, q_stats, p_stats, packed, n1,
        q_n2, p_n2, q_slope, p_slope, projection, mixing, expand, shrink, lengths, cls_grad, gains,
    )


def finish_kernel(*refs):
    count = len(refs) // 2 - 2
    small, outs = refs[count], refs[count + 1 :]
    biases, gains, widening = outs[count:]
    for src, dst in zip(refs[:count], outs[:count]):
        dst[...] = src[...]
    mine = lax.axis_index("pa")
    rows, features = small.shape[0] // 2, small.shape[1]
    share, wide = biases.shape[2], widening.shape[1]
    per_row = features // wide
    turned = pltpu.roll(small[...], features - mine * share, 1)[:, :share]
    for e in range(2):
        biases[e] = turned[e * rows : e * rows + 6]
        gains[e] = turned[e * rows + 6 : e * rows + 8]
        row = small[pl.ds(e * rows + 8 + mine // per_row, 1), :]
        widening[pl.ds(e, 1), :] = pltpu.roll(row, features - mine % per_row * wide, 1)[:, :wide]


def finish_all(arrays, small, wide):
    shape = jax.ShapeDtypeStruct
    size_pa = lax.axis_size("pa")
    features = small.shape[1]
    share, wide = features // size_pa, wide // size_pa
    steps = 4

    def cut(array):
        block = array.shape[:-2] + (array.shape[-2] // steps, array.shape[-1])
        axis = len(block) - 2
        return pl.BlockSpec(block, lambda i: tuple(i if d == axis else 0 for d in range(len(block))))

    def whole(dims):
        return pl.BlockSpec(dims, lambda i: (0,) * len(dims))

    cuts = [cut(a) if a.shape[-2] % (16 * steps) == 0 else whole(a.shape) for a in arrays]
    own = [(2, 6, share), (2, 2, share), (2, wide)]
    return pl.pallas_call(
        finish_kernel,
        out_shape=[shape(a.shape, a.dtype) for a in arrays] + [shape(dims, jnp.float32) for dims in own],
        grid=(steps,),
        in_specs=cuts + [whole(small.shape)],
        out_specs=cuts + [whole(dims) for dims in own],
        compiler_params=pltpu.CompilerParams(vmem_limit_bytes=vmem_bytes),
    )(*arrays, small)


def backward_all(lengths, q_rows, p_rows, q_cot, p_cot, cls_grad, saved, stacked, p_states):
    size_pa, size_pb = lax.axis_size("pa"), lax.axis_size("pb")
    features = q_rows.shape[1]
    if size_pa == 16 and size_pb == 2:
        reduced = reduce_by_kernel(lengths, q_rows, p_rows, q_cot, p_cot, cls_grad, saved, stacked)
        p_states, q_grad, p_grad, *totals = finish_all(
            (p_states, *reduced[4:10]), reduced[10], stacked[6].shape[1]
        )
        return p_states, q_grad, p_grad, tuple(totals)
    chances, packed, context, first, n1, q_side, p_side = saved
    cut = q_rows.shape[0]
    stats, n2, active, slope = (jnp.concatenate([q_part[:cut], p_part]) for q_part, p_part in zip(q_side, p_side))
    q_grad, p_grad, second, hidden, branch, packed_grad, small = encode_all_back(
        lengths, q_cot, p_cot, cls_grad, (chances, stats, packed, context, n1, n2, slope), stacked
    )
    products = []
    cut = q_rows.shape[0]
    for rows, part in ((q_rows, slice(None, cut)), (p_rows, slice(cut, None))):
        pairs = ((rows, packed_grad[part]), (context[part], branch[part]), (first[part], hidden[part]), (active[part], second[part]))
        products.append([contract_rows(*pair) for pair in pairs])
    projection, mixing, expand, shrink = (
        lax.psum(
            jnp.stack(
                [
                    lax.psum_scatter(products[e][i], "pa", scatter_dimension=0, tiled=True)
                    for e in range(2)
                ]
            ),
            "pb",
        )
        for i in range(4)
    )
    small = lax.psum(small, ("pb", "pa"))
    mine = lax.axis_index("pa")
    share = features // size_pa
    columns = lax.dynamic_slice_in_dim(small[:, :8], mine * share, share, 2)
    widening = small[:, 8:].reshape(2, -1)
    wide = widening.shape[1] // size_pa
    widening = lax.dynamic_slice_in_dim(widening, mine * wide, wide, 1)
    return p_states, q_grad, p_grad, (projection, mixing, expand, shrink, columns[:, :6], columns[:, 6:], widening)


def body(
    question_rows,
    passage_rows,
    segment_lengths,
    positives,
    negatives,
    question_cotangent,
    passage_cotangent,
    loss_weight,
    projection,
    mixing,
    expand,
    shrink,
    biases,
    gains,
    widening,
):
    stacked = (projection, mixing, expand, shrink, biases, gains, widening)
    question_count, _, features = question_rows.shape
    q_rows = question_rows.reshape(-1, features)
    p_rows = passage_rows.reshape(-1, features)
    (
        q_states, cls, chances, stats, packed, context, first, n1, wide_first, q_n2, q_active, q_slope,
    ) = encode_all(segment_lengths, q_rows, p_rows, stacked)
    cls_grad, question_loss, p_states, p_side = contrast(
        cls, question_count, positives, loss_weight, negatives, first, wide_first, stats, stacked
    )
    q_side = (stats, q_n2, q_active, q_slope)
    saved = (chances, packed, context, first, n1, q_side, p_side)
    p_states, q_grad, p_grad, totals = backward_all(
        segment_lengths,
        q_rows,
        p_rows,
        question_cotangent.reshape(-1, features),
        passage_cotangent.reshape(-1, features),
        cls_grad,
        saved,
        stacked,
        p_states,
    )
    return (
        q_states.reshape(question_rows.shape),
        p_states.reshape(passage_rows.shape),
        question_loss,
        q_grad.reshape(question_rows.shape),
        p_grad.reshape(passage_rows.shape),
    ) + totals


def solution(mesh):
    return jax.shard_map(
        body,
        mesh=mesh,
        in_specs=(
            P(("pb", "pa"), None, None),
            P(("pb", "pa"), None, None),
            P(("pb", "pa"), None),
            P("pb"),
            P("pa", None),
            P(("pb", "pa"), None, None),
            P(("pb", "pa"), None, None),
            P("pb"),
            P(),
            P(),
            P(),
            P(),
            P(),
            P(),
            P(),
        ),
        out_specs=(
            P(("pb", "pa"), None, None),
            P(("pb", "pa"), None, None),
            P("pb"),
            P(("pb", "pa"), None, None),
            P(("pb", "pa"), None, None),
            P(None, "pa", None),
            P(None, "pa", None),
            P(None, "pa", None),
            P(None, "pa", None),
            P(None, None, "pa"),
            P(None, None, "pa"),
            P(None, "pa"),
        ),
        check_vma=False,
    )
```

```python
from functools import partial
import math

import jax
import jax.numpy as jnp
from jax import lax
from jax.experimental import pallas as pl
from jax.experimental.pallas import tpu as pltpu
from jax.sharding import PartitionSpec as P

HEADS = 12
HEAD_DIM = 64


eps_norm = 1e-12
masked_score = -1000000000.0


def matmul(left_side, right_side):
    return jnp.dot(left_side, right_side, preferred_element_type=jnp.float32)


def contract_rows(left_side, right_side):
    return lax.dot_general(
        left_side, right_side, (((0,), (0,)), ((), ())), preferred_element_type=jnp.float32
    )


def contract_cols(left_side, right_side):
    return lax.dot_general(
        left_side, right_side, (((1,), (1,)), ((), ())), preferred_element_type=jnp.float32
    )


MESH = pl.DeviceIdType.MESH
lane = 128
block_tokens = 256
cls_slots = 4
stat_first, stat_final = 0, 1
vmem_bytes = 63 * 1024 * 1024


def dot_nn(left_side, right_side):
    return jnp.dot(left_side, right_side, preferred_element_type=jnp.float32)


def dot_nt(left_side, right_side):
    return lax.dot_general(
        left_side, right_side, (((1,), (1,)), ((), ())), preferred_element_type=jnp.float32
    )


def dot_tn(left_side, right_side):
    return lax.dot_general(
        left_side, right_side, (((0,), (0,)), ((), ())), preferred_element_type=jnp.float32
    )


def gelu_and_slope(hidden):
    size = jnp.abs(hidden)
    t = pl.reciprocal(1.0 + (0.3275911 * math.sqrt(0.5)) * size, approx=True)
    bell = jnp.exp2((hidden * hidden) * (-0.5 * math.log2(math.e)))
    tail = (0.5 * 1.061405429) * t - (0.5 * 1.453152027)
    tail = tail * t + (0.5 * 1.421413741)
    tail = tail * t - (0.5 * 0.284496736)
    tail = (tail * t + (0.5 * 0.254829592)) * (t * bell)
    below = jnp.where(hidden < 0.0, tail, 1.0 - tail)
    return hidden * below, below + (hidden * bell) * (1.0 / math.sqrt(2.0 * math.pi))


def normalize(values):
    centre = values - jnp.mean(values, axis=-1, keepdims=True)
    inverse = lax.rsqrt(jnp.mean(centre * centre, axis=-1, keepdims=True) + eps_norm)
    return centre * inverse, inverse


def normalize_back(gradient, normal, inverse, gain_row):
    scaled = gradient * gain_row
    inner_mean = jnp.mean(scaled, axis=-1, keepdims=True)
    projected = jnp.mean(scaled * normal, axis=-1, keepdims=True)
    return inverse * (scaled - inner_mean - normal * projected)


def head_pair(packed_ref, pair, features):
    return [packed_ref[:, pl.ds(j * features + pair * lane, lane)] for j in range(3)]


def side_mask(side, scale):
    at = lax.broadcasted_iota(jnp.int32, (1, lane), 1) // HEAD_DIM
    return jnp.where(at == side, scale, 0.0).astype(jnp.bfloat16)


def start_of(lengths, i, first_passage, k):
    row = jnp.maximum(i - first_passage, 0)
    at = 0
    for j in range(k):
        at = at + lengths[row, j]
    return jnp.where(i < first_passage, k * (block_tokens // cls_slots), at)


class Weights:
    def __init__(self, sources, buffers, sems, step, first_passage, order, passage_order):
        self.sources, self.buffers, self.sems, self.order = sources, buffers, sems, order
        self.step, self.first_passage = step, first_passage
        self.encoder = (step >= first_passage).astype(jnp.int32)
        self.parts = ((0, 0, order), (1, first_passage, passage_order))
        self.seen = set()

    def copy(self, which, e):
        return pltpu.make_async_copy(
            self.sources[which].at[e], self.buffers[which].at[e], self.sems.at[which, e]
        )

    def begin(self):
        for e, at, order in self.parts:

            @pl.when(self.step == max(at - 1, 0))
            def _():
                for which in order if e > 0 else order[:1]:
                    self.copy(which, e).start()

    def get(self, which):
        if which not in self.seen:
            self.seen.add(which)
            for e, at, order in self.parts:
                if which not in order:
                    continue

                @pl.when(self.step == at)
                def _():
                    self.copy(which, e).wait()
                    if e == 0 and which == order[0]:
                        for later in order[1:]:
                            self.copy(later, e).start()

        return self.buffers[which].at[self.encoder if which in self.parts[1][2] else 0]


def feed_forward(first_low, first, up, down, wide_shift, shifts, gain_rows, keep):
    tile = 512

    def raised(j):
        return dot_nn(first_low, up[:, pl.ds(j * tile, tile)]) + wide_shift[:, j * tile : (j + 1) * tile]

    second = jnp.broadcast_to(shifts[4:5], first.shape)
    ahead = raised(0)
    for j in range(up.shape[1] // tile):
        columns = pl.ds(j * tile, tile)
        hidden = ahead
        if (j + 1) * tile < up.shape[1]:
            ahead = raised(j + 1)
        active, slope = gelu_and_slope(hidden)
        active_low = active.astype(jnp.bfloat16)
        if keep is not None:
            keep(columns, active_low, slope.astype(jnp.bfloat16))
        second = second + dot_nn(active_low, down[columns, :])
    normal, inverse = normalize(first[...] + second)
    return normal, inverse, normal * gain_rows[1:2] + shifts[5:6]


def forward_kernel(
    first_passage,
    lengths,
    q_rows, p_rows, projection, mixing, expand, shrink, biases, gains, widening,
    q_states, cls, chances, stats, packed_ref, context_ref, first_ref, n1_ref, wide_first,
    n2_ref, active_ref, slope_ref,
    w0, w1, w2, w3, sems, final_buf, x_buf,
):
    i = pl.program_id(0)
    weights = Weights((projection, mixing, expand, shrink), (w0, w1, w2, w3), sems, i, first_passage, (0, 1, 2, 3), (0, 1))
    weights.begin()
    e = weights.encoder
    features = q_rows.shape[1]
    shifts = biases[e].astype(jnp.float32)
    gain_rows = gains[e].astype(jnp.float32)
    both = widening[...].astype(jnp.float32)
    wide_shift = jnp.where(e == 0, both[0:1], both[1:2])
    x_buf[...] = jnp.where(i < first_passage, q_rows[...], p_rows[...])

    weight = weights.get(0)
    x_low = x_buf[...]
    for part in range(3):
        columns = pl.ds(part * features, features)
        value = dot_nn(x_low, weight[:, columns])
        if part != 1:
            value = value + shifts[part // 2 : part // 2 + 1]
        packed_ref[:, columns] = value.astype(jnp.bfloat16)

    tokens = q_rows.shape[0]
    row_at = lax.broadcasted_iota(jnp.int32, (tokens, tokens), 0)
    col_at = lax.broadcasted_iota(jnp.int32, (tokens, tokens), 1)
    starts = [start_of(lengths, i, first_passage, k) for k in range(cls_slots)]
    row_segment = jnp.zeros_like(row_at)
    col_segment = jnp.zeros_like(col_at)
    for k in range(1, cls_slots):
        row_segment = row_segment + (row_at >= starts[k]).astype(jnp.int32)
        col_segment = col_segment + (col_at >= starts[k]).astype(jnp.int32)
    penalty = jnp.where(row_segment == col_segment, 0.0, masked_score)
    def scores_of(pair):
        queries, keys, _ = head_pair(packed_ref, pair, features)
        both = [keys * side_mask(side, HEAD_DIM ** (-0.5)) for side in range(2)]
        return dot_nt(jnp.concatenate(both), queries)

    def chances_of(pair, scores):
        result = []
        for side in range(2):
            part = scores[side * tokens : (side + 1) * tokens] + penalty
            chance = jnp.exp(part - jnp.max(part, axis=0, keepdims=True))
            inverse = 1.0 / jnp.sum(chance, axis=0, keepdims=True)
            result.append((chance * inverse).astype(jnp.bfloat16))
            chances[0, 2 * pair + side] = result[side]
        return result

    def mix(pair, both):
        values_t = head_pair(packed_ref, pair, features)[2].T
        mixed = [
            dot_nn(values_t[side * HEAD_DIM : (side + 1) * HEAD_DIM], both[side])
            for side in range(2)
        ]
        context_ref[:, pl.ds(pair * lane, lane)] = jnp.concatenate(mixed).astype(jnp.bfloat16).T

    pairs = HEADS // 2
    scores, both = {}, {}
    for step in range(pairs + 2):
        if step < pairs:
            scores[step] = scores_of(step)
        if step >= 2:
            mix(step - 2, both.pop(step - 2))
        if 1 <= step <= pairs:
            both[step - 1] = chances_of(step - 1, scores.pop(step - 1))
    lanes = lax.broadcasted_iota(jnp.int32, stats.shape, 1)

    weight = weights.get(1)
    branch = dot_nn(context_ref[...], weight[...]) + shifts[2:3]
    normal, inverse = normalize(x_buf[...].astype(jnp.float32) + branch)
    n1_ref[...] = normal.astype(jnp.bfloat16)
    first_inverse = inverse
    first = normal * gain_rows[0:1] + shifts[3:4]
    first_low = first.astype(jnp.bfloat16)
    first_ref[...] = first_low
    final_buf[...] = first

    up, down = weights.get(2), weights.get(3)

    @pl.when(i < first_passage)
    def _():
        def keep(columns, active_low, slope_low):
            active_ref[:, columns] = active_low
            slope_ref[:, columns] = slope_low

        normal, inverse, final = feed_forward(
            first_ref[...], final_buf, up, down, wide_shift, shifts, gain_rows, keep
        )
        n2_ref[...] = normal.astype(jnp.bfloat16)
        stats[...] = jnp.where(lanes == stat_final, inverse, first_inverse)
        q_states[...] = final.astype(jnp.bfloat16)
        final_buf[...] = final
        for k in range(cls_slots):
            cls[pl.ds(i * cls_slots + k, 1), :] = final_buf[pl.ds(starts[k], 1), :]

    @pl.when(i >= first_passage)
    def _():
        stats[...] = jnp.broadcast_to(first_inverse, stats.shape)
        wide_first[...] = final_buf[...]
        for k in range(cls_slots):
            at = jnp.minimum(starts[k], tokens - 1)
            cls[pl.ds(i * cls_slots + k, 1), :] = final_buf[pl.ds(at, 1), :]


class Back:
    def __init__(self, **refs):
        self.__dict__.update(refs)

    def add_small(self, row, value):
        self.small[pl.ds(row, 1), :] += jnp.sum(value, axis=0, keepdims=True)

    def part_a(self):
        gradient = self.gradient()
        normal = self.n2[...].astype(jnp.float32)
        self.add_small(5, gradient)
        self.add_small(7, gradient * normal)
        total_grad = normalize_back(
            gradient, normal, self.stats[:, stat_final : stat_final + 1], self.gain_rows[1:2]
        )
        second_low = total_grad.astype(jnp.bfloat16)
        self.second[...] = second_low
        self.add_small(4, second_low.astype(jnp.float32))
        self.total[...] = total_grad
        self.feed_forward(0, 2)

    def feed_forward(self, begin, end):
        down, up = self.weight(3), self.weight(2)
        features = self.total.shape[1]
        second_low = self.second[...]
        first_grad = self.total[...]
        for j in range(begin, end):
            columns = pl.ds(j * features, features)
            hidden_grad = dot_nt(second_low, down[columns, :]) * self.slope[:, columns].astype(jnp.float32)
            hidden_low = hidden_grad.astype(jnp.bfloat16)
            self.hidden[:, columns] = hidden_low
            self.add_small(8 + j, hidden_low.astype(jnp.float32))
            first_grad = first_grad + dot_nt(hidden_low, up[:, columns])
        self.total[...] = first_grad

    def part_b(self):
        features = self.total.shape[1]
        self.feed_forward(2, self.hidden.shape[1] // features)
        first_grad = self.total[...]
        normal = self.n1[...].astype(jnp.float32)
        self.add_small(3, first_grad)
        self.add_small(6, first_grad * normal)
        branch_grad = normalize_back(
            first_grad, normal, self.stats[:, stat_first : stat_first + 1], self.gain_rows[0:1]
        )
        self.total[...] = branch_grad
        branch_low = branch_grad.astype(jnp.bfloat16)
        self.branch[...] = branch_low
        self.add_small(2, branch_low.astype(jnp.float32))

    def part_c(self):
        packed_ref, mixed, chances = self.packed, self.mixed, self.chances
        tokens, features = mixed.shape
        mixed_grad = dot_nt(self.branch[...], self.weight(1)[...])
        self.mixed[...] = mixed_grad.astype(jnp.bfloat16)
        heads = lax.broadcasted_iota(jnp.int32, (16, features), 0)
        of_head = lax.broadcasted_iota(jnp.int32, (16, features), 1) // HEAD_DIM == heads
        of_head = jnp.where(of_head, 1.0, 0.0).astype(jnp.bfloat16)
        inner = mixed_grad * self.context[...].astype(jnp.float32)
        inner_high = inner.astype(jnp.bfloat16)
        inner_low = (inner - inner_high.astype(jnp.float32)).astype(jnp.bfloat16)
        inner = dot_nt(of_head, inner_high) + dot_nt(of_head, inner_low)
        left_side = lax.broadcasted_iota(jnp.int32, (tokens, lane), 1) < HEAD_DIM

        def weight_grads(pair):
            values = head_pair(packed_ref, pair, features)[2]
            both = [values * side_mask(side, 1.0) for side in range(2)]
            return dot_nt(jnp.concatenate(both), mixed[:, pl.ds(pair * lane, lane)])

        def score_grads(pair, weight_grad):
            result = []
            for side in range(2):
                h = 2 * pair + side
                part = weight_grad[side * tokens : (side + 1) * tokens] - inner[h : h + 1]
                result.append((chances[h].astype(jnp.float32) * part).astype(jnp.bfloat16))
            return result

        def head_grads(pair, score_low):
            queries, keys, _ = head_pair(packed_ref, pair, features)
            mixed_low = mixed[:, pl.ds(pair * lane, lane)]
            keys_t = keys.T
            query_grad = [
                dot_nn(keys_t[side * HEAD_DIM : (side + 1) * HEAD_DIM], score_low[side])
                for side in range(2)
            ]
            key_grad = dot_nn(jnp.concatenate(score_low), queries)
            both = chances[2 * pair : 2 * pair + 2].reshape(2 * tokens, tokens)
            value_grad = dot_nn(both, mixed_low)
            scale = HEAD_DIM ** (-0.5)
            for j, value in enumerate(
                (
                    (jnp.concatenate(query_grad) * scale).astype(jnp.bfloat16).T,
                    (jnp.where(left_side, key_grad[:tokens], key_grad[tokens:]) * scale).astype(jnp.bfloat16),
                    jnp.where(left_side, value_grad[:tokens], value_grad[tokens:]).astype(jnp.bfloat16),
                )
            ):
                self.packed_grad[:, pl.ds(j * features + pair * lane, lane)] = value

        pairs = HEADS // 2
        raw, low_grads = {}, {}
        for step in range(pairs + 2):
            if step < pairs:
                raw[step] = weight_grads(step)
            if step >= 2:
                head_grads(step - 2, low_grads.pop(step - 2))
            if 1 <= step <= pairs:
                low_grads[step - 1] = score_grads(step - 1, raw.pop(step - 1))
        self.add_small(0, self.packed_grad[:, :features].astype(jnp.float32))
        self.add_small(1, self.packed_grad[:, 2 * features :].astype(jnp.float32))

    def part_d(self):
        return self.total[...] + dot_nt(self.packed_grad[...], self.weight(0)[...])


def with_cls(gradient, starts, cls_grad, first_row):
    row_at = lax.broadcasted_iota(jnp.int32, (gradient.shape[0], 1), 0)
    for k, start in enumerate(starts):
        gradient = gradient + jnp.where(row_at == start, cls_grad[pl.ds(first_row + k, 1), :], 0.0)
    return gradient


def backward_kernel(
    first_passage,
    lengths,
    *refs,
):
    refs = list(refs)
    q_cot = refs.pop(0)
    p_cot = refs.pop(0)
    cls_grad, chances, stats, packed_ref, context_ref, n1_ref, n2_ref, slope_ref = refs[:8]
    projection, mixing, expand, shrink, gains = refs[8:13]
    refs = refs[13:]
    q_grad = refs.pop(0)
    p_grad = refs.pop(0)
    second_ref, hidden_ref, branch_ref, packed_grad, small = refs[:5]
    w0, w1, w2, w3, sems, total_buf, context_grad = refs[5:]
    i = pl.program_id(0)
    weights = Weights((projection, mixing, expand, shrink), (w0, w1, w2, w3), sems, i, first_passage, (3, 2, 1, 0), (3, 2, 1, 0))
    weights.begin()

    @pl.when((i == 0) | (i == first_passage))
    def _():
        small[...] = jnp.zeros_like(small)

    def gradient():
        value = jnp.where(i < first_passage, q_cot[...], p_cot[...]).astype(jnp.float32)
        starts = [start_of(lengths, i, first_passage, k) for k in range(cls_slots)]
        return with_cls(value, starts, cls_grad, i * cls_slots)

    block = Back(
        gradient=gradient, chances=chances.at[0], stats=stats, packed=packed_ref, context=context_ref,
        n1=n1_ref, n2=n2_ref, slope=slope_ref, second=second_ref, hidden=hidden_ref, branch=branch_ref,
        packed_grad=packed_grad, small=small.at[0], total=total_buf, mixed=context_grad,
        weight=weights.get, gain_rows=gains[weights.encoder].astype(jnp.float32),
    )
    block.part_a()
    block.part_b()
    block.part_c()
    input_grad = block.part_d()

    @pl.when(i < first_passage)
    def _():
        q_grad[...] = input_grad

    @pl.when(i >= first_passage)
    def _():
        p_grad[...] = input_grad


def block_specs(first_passage):
    q_at = lambda i, lengths: (jnp.minimum(i, first_passage - 1), 0)
    p_at = lambda i, lengths: (jnp.maximum(i - first_passage, 0), 0)
    at = lambda i, lengths: (i, 0)

    def rows(width, index=at):
        return pl.BlockSpec((block_tokens, width), index)

    def lead(*shape):
        return pl.BlockSpec((1,) + shape, lambda i, lengths: (i,) + (0,) * len(shape))

    def whole(array):
        return pl.BlockSpec(array.shape, lambda i, lengths: (0,) * array.ndim)

    anywhere = pl.BlockSpec(memory_space=pl.ANY)
    return q_at, p_at, rows, lead, whole, anywhere


def weight_scratch(stacked, encoders):
    sizes = zip(stacked[:4], encoders)
    return [pltpu.VMEM((n,) + w.shape[1:], w.dtype) for w, n in sizes] + [pltpu.SemaphoreType.DMA((4, 2))]


def encode_all(lengths, q_rows, p_rows, stacked):
    projection, mixing, expand, shrink, biases, gains, widening = stacked
    features, wide = projection.shape[1], expand.shape[2]
    first_passage = q_rows.shape[0] // block_tokens
    blocks = first_passage + lengths.shape[0]
    q_at, p_at, rows, lead, whole, anywhere = block_specs(first_passage)
    low, tokens = jnp.bfloat16, blocks * block_tokens
    shape = jax.ShapeDtypeStruct
    return pl.pallas_call(
        partial(forward_kernel, first_passage),
        out_shape=[
            shape(q_rows.shape, low),
            shape((blocks * cls_slots, features), jnp.float32),
            shape((blocks, HEADS, block_tokens, block_tokens), low),
            shape((tokens, lane), jnp.float32),
            shape((tokens, 3 * features), low),
            shape((tokens, features), low), shape((tokens, features), low), shape((tokens, features), low),
            shape(p_rows.shape, jnp.float32), shape(q_rows.shape, low),
            shape((q_rows.shape[0], wide), low), shape((q_rows.shape[0], wide), low),
        ],
        grid_spec=pltpu.PrefetchScalarGridSpec(
            num_scalar_prefetch=1,
            grid=(blocks,),
            in_specs=[
                rows(features, q_at), rows(features, p_at), anywhere, anywhere, anywhere, anywhere,
                whole(biases), whole(gains), whole(widening),
            ],
            out_specs=[
                rows(features, q_at),
                pl.BlockSpec((blocks * cls_slots, features), lambda i, lengths: (0, 0)),
                lead(HEADS, block_tokens, block_tokens), rows(lane), rows(3 * features),
                rows(features), rows(features), rows(features), rows(features, p_at),
                rows(features, q_at), rows(wide, q_at), rows(wide, q_at),
            ],
            scratch_shapes=weight_scratch(stacked, (2, 2, 1, 1)) + [
                pltpu.VMEM((block_tokens, features), jnp.float32),
                pltpu.VMEM((block_tokens, features), low),
            ],
        ),
        compiler_params=pltpu.CompilerParams(
            dimension_semantics=("arbitrary",), vmem_limit_bytes=vmem_bytes
        ),
    )(lengths, q_rows, p_rows, projection, mixing, expand, shrink, biases, gains, widening)


def encode_all_back(lengths, q_cot, p_cot, cls_grad, saved, stacked):
    projection, mixing, expand, shrink, biases, gains, widening = stacked
    chances, stats, packed, context, n1, n2, slope = saved
    features, wide = projection.shape[1], expand.shape[2]
    first_passage = q_cot.shape[0] // block_tokens
    blocks = first_passage + lengths.shape[0]
    q_at, p_at, rows, lead, whole, anywhere = block_specs(first_passage)
    low, tokens = jnp.bfloat16, blocks * block_tokens
    shape = jax.ShapeDtypeStruct
    small_rows = 8 + wide // features
    return pl.pallas_call(
        partial(backward_kernel, first_passage),
        out_shape=[shape(q_cot.shape, jnp.float32)] + [shape(p_cot.shape, jnp.float32)] + [
            shape((tokens, features), low), shape((tokens, wide), low),
            shape((tokens, features), low), shape((tokens, 3 * features), low),
            shape((2, small_rows, features), jnp.float32),
        ],
        grid_spec=pltpu.PrefetchScalarGridSpec(
            num_scalar_prefetch=1,
            grid=(blocks,),
            in_specs=[rows(features, q_at)] + [rows(features, p_at)] + [
                whole(cls_grad),
                lead(HEADS, block_tokens, block_tokens), rows(lane), rows(3 * features),
                rows(features), rows(features), rows(features), rows(wide),
                anywhere, anywhere, anywhere, anywhere, whole(gains),
            ],
            out_specs=[rows(features, q_at)] + [rows(features, p_at)] + [
                rows(features), rows(wide), rows(features), rows(3 * features),
                pl.BlockSpec(
                    (1, small_rows, features),
                    lambda i, lengths: ((i >= first_passage).astype(jnp.int32), 0, 0),
                ),
            ],
            scratch_shapes=weight_scratch(stacked, (2, 2, 2, 2)) + [
                pltpu.VMEM((block_tokens, features), jnp.float32),
                pltpu.VMEM((block_tokens, features), low),
            ],
        ),
        compiler_params=pltpu.CompilerParams(
            dimension_semantics=("arbitrary",), vmem_limit_bytes=vmem_bytes
        ),
    )(
        lengths, q_cot, p_cot, cls_grad, chances, stats, packed, context, n1, n2, slope,
        projection, mixing, expand, shrink, gains,
    )


def contrast_kernel(
    first_passage,
    cls, positives, loss_weight, negatives, biases, gains, widening, first, wide_first, stats, expand, shrink,
    cls_grad, loss, p_states, p_stats, p_n2, p_active, p_slope,
    q_all, p_all, stat_all, row_send, row_recv, col_send, col_recv, q_wide, q_low,
    q_ss, q_rs, p_ss, p_rs, stat_ss, stat_rs, row_ss, row_rs, col_ss, col_rs,
    up, down, f_first, f_wide, f_stats, f_states, f_stats_out, f_n2, f_active, f_slope, weight_sem, in_sem, out_sem,
):
    size_pa, size_pb = lax.axis_size("pa"), lax.axis_size("pb")
    pa, pb = lax.axis_index("pa"), lax.axis_index("pb")
    features = cls.shape[1]
    half = features // 2
    own_q = q_all.shape[1] // 2
    own_p = p_all.shape[1]
    far_a = [(d, lax.rem(pa + d, size_pa)) for d in range(1, size_pa)]
    far_b = [(d, lax.rem(pb + d, size_pb)) for d in range(1, size_pb)]

    blocks = wide_first.shape[0] // block_tokens
    weight_copies = [
        pltpu.make_async_copy(source.at[1], buffer, weight_sem.at[i])
        for i, (source, buffer) in enumerate(((expand, up), (shrink, down)))
    ]
    shifts = biases[1].astype(jnp.float32)
    gain_rows = gains[1].astype(jnp.float32)
    wide_shift = widening[...].astype(jnp.float32)[1:2]

    def loads(b):
        own, every = pl.ds(b * block_tokens, block_tokens), pl.ds((first_passage + b) * block_tokens, block_tokens)
        pairs = ((first.at[every], f_first), (wide_first.at[own], f_wide), (stats.at[every], f_stats))
        return [
            pltpu.make_async_copy(src, dst.at[b % 2], in_sem.at[b % 2, i]) for i, (src, dst) in enumerate(pairs)
        ]

    def stores(b):
        own = pl.ds(b * block_tokens, block_tokens)
        pairs = (
            (f_states, p_states), (f_stats_out, p_stats), (f_n2, p_n2), (f_active, p_active), (f_slope, p_slope)
        )
        return [
            pltpu.make_async_copy(src.at[b % 2], dst.at[own], out_sem.at[b % 2, i]) for i, (src, dst) in enumerate(pairs)
        ]

    def encode_block(b):
        if b >= blocks:
            return
        slot = b % 2
        for copy in loads(b):
            copy.wait()
        if b >= 2:
            for copy in stores(b - 2):
                copy.wait()

        def keep(columns, active_low, slope_low):
            f_active[slot, :, columns] = active_low
            f_slope[slot, :, columns] = slope_low

        normal, inverse, final = feed_forward(
            f_first[slot], f_wide.at[slot], up, down, wide_shift, shifts, gain_rows, keep
        )
        lanes = lax.broadcasted_iota(jnp.int32, f_stats.shape[1:], 1)
        f_n2[slot] = normal.astype(jnp.bfloat16)
        f_states[slot] = final.astype(jnp.bfloat16)
        f_stats_out[slot] = jnp.where(lanes == stat_final, inverse, f_stats[slot])
        for copy in stores(b) + (loads(b + 2) if b + 2 < blocks else []):
            copy.start()

    for copy in weight_copies + loads(0) + (loads(1) if blocks > 1 else []):
        copy.start()

    barrier = pltpu.get_barrier_semaphore()
    for _, a in far_a:
        pl.semaphore_signal(barrier, inc=1, device_id=(pb, a), device_id_type=MESH)
    for _, b in far_b:
        pl.semaphore_signal(barrier, inc=1, device_id=(b, pa), device_id_type=MESH)
    pl.semaphore_wait(barrier, size_pa + size_pb - 2)

    def to_a(src, dst, ss, rs, d, a):
        return pltpu.make_async_remote_copy(
            src_ref=src, dst_ref=dst, send_sem=ss.at[d], recv_sem=rs.at[d], device_id=(pb, a), device_id_type=MESH
        )

    def to_b(src, dst, ss, rs, d, b):
        return pltpu.make_async_remote_copy(
            src_ref=src, dst_ref=dst, send_sem=ss.at[d], recv_sem=rs.at[d], device_id=(b, pa), device_id_type=MESH
        )

    def fold(block):
        return jnp.concatenate([block[:, :half], block[:, half:]], axis=0).astype(jnp.bfloat16)

    q_all[pa] = fold(cls[:own_q, :])
    copies = [to_a(q_all.at[pa], q_all.at[pa], q_ss, q_rs, d, a) for d, a in far_a]
    for copy in copies:
        copy.start()
    for copy in weight_copies:
        copy.wait()
    p_first = cls[own_q:, :]
    _, _, p_final = feed_forward(
        p_first.astype(jnp.bfloat16), p_first, up, down, wide_shift, shifts, gain_rows, None
    )
    p_all[pb] = p_final.astype(jnp.bfloat16)
    p_copies = [to_b(p_all.at[pb], p_all.at[pb], p_ss, p_rs, d, b) for d, b in far_b]
    for copy in p_copies:
        copy.start()
    copies += p_copies
    encode_block(0)
    for copy in copies:
        copy.wait()
    for a in range(size_pa):
        block = q_all[a].astype(jnp.float32)
        q_wide[pl.ds(a * own_q, own_q), :half] = block[:own_q]
        q_wide[pl.ds(a * own_q, own_q), half:] = block[own_q:]
    q_low[...] = q_wide[...].astype(jnp.bfloat16)

    tile_scale = 2.0 / math.sqrt(features)
    count = q_low.shape[0]
    p_rows = p_all[...].reshape(size_pb * own_p, features)
    row = lax.broadcasted_iota(jnp.int32, (size_pb * own_p, count), 0)
    slot = row % cls_slots
    valid = slot < cls_slots - 1
    place = row % own_p // cls_slots
    owner = row // own_p * size_pa + pa
    identity = (owner * (own_p // cls_slots) + place) * (cls_slots - 1) + slot
    chosen = jnp.where(valid & (identity == positives[...]), 1.0, 0.0)
    p_scores = dot_nt(p_rows, q_low[...]) * tile_scale
    p_scores = jnp.where(valid, p_scores, -1e30)
    n_scores = dot_nt(negatives[...], q_low[...]) * tile_scale
    top = jnp.maximum(
        jnp.max(p_scores, axis=0, keepdims=True), jnp.max(n_scores, axis=0, keepdims=True)
    )
    mass = jnp.sum(jnp.exp(p_scores - top), axis=0, keepdims=True)
    mass = mass + jnp.sum(jnp.exp(n_scores - top), axis=0, keepdims=True)
    picked = jnp.sum(jnp.where(chosen > 0.0, p_scores, 0.0), axis=0, keepdims=True)
    stat_all[pa] = jnp.concatenate([top, mass, picked] + [jnp.zeros_like(top)] * 5, axis=0)
    copies = [to_a(stat_all.at[pa], stat_all.at[pa], stat_ss, stat_rs, d, a) for d, a in far_a]
    for copy in copies:
        copy.start()
    encode_block(1)
    for copy in copies:
        copy.wait()
    all_top = stat_all[0, 0:1]
    for a in range(1, size_pa):
        all_top = jnp.maximum(all_top, stat_all[a, 0:1])
    all_mass = jnp.zeros_like(all_top)
    all_picked = jnp.zeros_like(all_top)
    for a in range(size_pa):
        all_mass = all_mass + stat_all[a, 1:2] * jnp.exp(stat_all[a, 0:1] - all_top)
        all_picked = all_picked + stat_all[a, 2:3]
    logsum = all_top + jnp.log(all_mass)
    loss[...] = logsum - all_picked

    p_tile = (loss_weight[...] * (jnp.exp(p_scores - logsum) - chosen)).astype(jnp.bfloat16)
    n_tile = (loss_weight[...] * jnp.exp(n_scores - logsum)).astype(jnp.bfloat16)
    q_wide[...] = (dot_tn(p_tile, p_rows) + dot_tn(n_tile, negatives[...])) * tile_scale
    col_send[...] = (dot_nn(p_tile, q_low[...]) * tile_scale).reshape(col_send.shape)
    for a in range(size_pa):
        row_send[a] = fold(q_wide[pl.ds(a * own_q, own_q), :])
    copies = [to_a(row_send.at[a], row_recv.at[pa], row_ss, row_rs, d, a) for d, a in far_a]
    copies += [to_b(col_send.at[b], col_recv.at[pb], col_ss, col_rs, d, b) for d, b in far_b]
    for copy in copies:
        copy.start()
    for b in range(2, blocks):
        encode_block(b)
    for copy in copies:
        copy.wait()
    row_recv[pa] = row_send[pa]
    col_recv[pb] = col_send[pb]
    total = row_recv[0].astype(jnp.float32)
    for a in range(1, size_pa):
        total = total + row_recv[a].astype(jnp.float32)
    cls_grad[:own_q, :half] = total[:own_q]
    cls_grad[:own_q, half:] = total[own_q:]
    total = col_recv[0]
    for b in range(1, size_pb):
        total = total + col_recv[b]
    cls_grad[own_q:, :] = total
    for b in range(max(blocks - 2, 0), blocks):
        for copy in stores(b):
            copy.wait()


def contrast(cls, own_q, positives, loss_weight, negatives, first, wide_first, stats, stacked):
    projection, mixing, expand, shrink, biases, gains, widening = stacked
    size_pa, size_pb = lax.axis_size("pa"), lax.axis_size("pb")
    slots, features = cls.shape
    own_p, count = slots - own_q, positives.shape[0]
    low, wide, dma = jnp.bfloat16, jnp.float32, pltpu.SemaphoreType.DMA
    folded = (size_pa, 2 * own_q, features // 2)
    sems = [dma((size_pa,))] * 2 + [dma((size_pb,))] * 2 + [dma((size_pa,))] * 4 + [dma((size_pb,))] * 2
    tokens, units = wide_first.shape[0], expand.shape[2]
    shape = jax.ShapeDtypeStruct
    vmem, anywhere = pl.BlockSpec(memory_space=pltpu.VMEM), pl.BlockSpec(memory_space=pl.ANY)
    two = lambda width, kind: pltpu.VMEM((2, block_tokens, width), kind)
    cls_grad, loss, p_states, *p_side = pl.pallas_call(
        partial(contrast_kernel, (first.shape[0] - tokens) // block_tokens),
        out_shape=[
            shape(cls.shape, wide), shape((1, count), wide),
            shape((tokens, features), low), shape((tokens, lane), wide), shape((tokens, features), low),
            shape((tokens, units), low), shape((tokens, units), low),
        ],
        in_specs=[vmem] * 7 + [anywhere] * 5,
        out_specs=[vmem] * 2 + [anywhere] * 5,
        scratch_shapes=[
            pltpu.VMEM(folded, low),
            pltpu.VMEM((size_pb, own_p, features), low),
            pltpu.VMEM((size_pa, 8, count), wide),
            pltpu.VMEM(folded, low),
            pltpu.VMEM(folded, low),
            pltpu.VMEM((size_pb, own_p, features), wide),
            pltpu.VMEM((size_pb, own_p, features), wide),
            pltpu.VMEM((count, features), wide),
            pltpu.VMEM((count, features), low),
        ] + sems + [
            pltpu.VMEM(expand.shape[1:], low), pltpu.VMEM(shrink.shape[1:], low),
            two(features, low), two(features, wide), two(lane, wide),
            two(features, low), two(lane, wide), two(features, low), two(units, low), two(units, low),
            dma((2,)), dma((2, 3)), dma((2, 5)),
        ],
        compiler_params=pltpu.CompilerParams(
            collective_id=2, has_side_effects=True, vmem_limit_bytes=vmem_bytes
        ),
    )(
        cls, positives[None, :], loss_weight[None, :], negatives, biases, gains, widening,
        first, wide_first, stats, expand, shrink,
    )
    return cls_grad, loss[0], p_states, p_side


panel_rows = 48
chunk_panels = 8
encoder_chunks = 9


ring = 6


def reduce_kernel(
    tokens,
    q_active, p_active, first, context, q_rows, p_rows,
    q_cot, p_cot, chances, q_stats, p_stats, packed, n1, q_n2, p_n2, q_slope, p_slope,
    projection, mixing, expand, shrink,
    lengths, cls_grad, gains,
    second, hidden, branch, packed_grad, q_grad, p_grad,
    projection_out, mixing_out, expand_out, shrink_out, small_out,
    keep, core_send, core_recv, recv_x, recv_ya, recv_za, recv_yb, recv_zb, fin_a, fin_b,
    left_buf, left_t, right_buf, product, small_recv, small_sum,
    load_sem, core_ss, core_rs, xa_ss, xa_rs, ya_ss, ya_rs, za_ss, za_rs, ag_ss, ag_rs,
    yb_ss, yb_rs, zb_ss, zb_rs, xb_ss, xb_rs, small_ss, small_rs, credit,
    w0, w1, w2, w3, weight_sem, in_sem, out_sem,
    b_cot, b_stats, b_n1, b_n2, b_slope, b_second, b_hidden, b_branch, b_total,
    b_chances, b_packed, b_context, b_branch_in, b_total_in, b_packed_grad, b_grad, b_mixed,
):
    chunks = 2 * encoder_chunks
    pb, pa = lax.axis_index("pb"), lax.axis_index("pa")
    core, y, z, x = pa % 2, pa // 2 % 2, pa // 4, pb
    at_core = (pb, pa + 1 - 2 * core)
    at_y = (pb, pa + 2 - 4 * y)
    at_x = (1 - pb, pa)
    far_z = [(z + d) % 4 for d in (1, 2, 3)]
    at_z = [(pb, t * 4 + y * 2 + core) for t in far_z]

    def remote(src, dst, ss, rs, device):
        return pltpu.make_async_remote_copy(
            src_ref=src, dst_ref=dst, send_sem=ss, recv_sem=rs, device_id=device, device_id_type=MESH
        )

    def by_x(c):
        return 6 if c < chunks - 4 and c % 3 == 0 else 4

    def copy_core(c):
        return remote(core_send.at[c % 2], core_recv.at[c % 2], core_ss.at[c], core_rs.at[c], at_core)

    def copy_xa(c):
        half = by_x(c) // 2
        return remote(
            keep.at[c % ring, pl.ds(half * (1 - x), half)], recv_x.at[c % ring, pl.ds(0, half)], xa_ss.at[c], xa_rs.at[c], at_x
        )

    def copy_ya(c):
        half = by_x(c) // 2
        return remote(
            keep.at[c % ring, pl.ds(half * x, half), :, 1 - y], recv_ya.at[c % ring, pl.ds(0, half)],
            ya_ss.at[c], ya_rs.at[c], at_y,
        )

    def copy_za(c, d):
        half = by_x(c) // 2
        return remote(
            keep.at[c % ring, pl.ds(half * x, half), far_z[d], y], recv_za.at[c % ring, d, pl.ds(0, half)],
            za_ss.at[c, d], za_rs.at[c, d], at_z[d],
        )

    def copy_ag(c):
        half = by_x(c) // 2
        part = fin_a.at[c % ring, pl.ds(half * x, half)]
        return remote(part, part, ag_ss.at[c], ag_rs.at[c], at_x)

    def copy_yb(c):
        rest = chunk_panels - by_x(c)
        return remote(
            keep.at[c % ring, pl.ds(by_x(c), rest), :, 1 - y], recv_yb.at[c % ring, pl.ds(0, rest)],
            yb_ss.at[c], yb_rs.at[c], at_y,
        )

    def copy_zb(c, d):
        rest = chunk_panels - by_x(c)
        return remote(
            keep.at[c % ring, pl.ds(by_x(c), rest), far_z[d], y], recv_zb.at[c % ring, d, pl.ds(0, rest)],
            zb_ss.at[c, d], zb_rs.at[c, d], at_z[d],
        )

    def copy_xb(c):
        part = fin_b.at[c % ring, x, pl.ds(0, chunk_panels - by_x(c))]
        return remote(part, part, xb_ss.at[c], xb_rs.at[c], at_x)

    def small_copy(stage, device):
        source = small_sum.at[max(stage - 3, 0) if stage >= 3 else stage]
        return remote(source, small_recv.at[stage], small_ss.at[stage], small_rs.at[stage], device)

    order = [(e, k) for e in range(2) for k in (3, 4, 5, 0, 1, 2, 6, 7, 8)]
    place = {what: c for c, what in enumerate(order)}

    def own(e, ref):
        return ref.at[pl.ds(0 if e == 0 else tokens[0], tokens[e])]

    def left_loads(e, part):
        count = tokens[e]
        features = q_rows.shape[1]
        if part == 0:
            pairs = [((q_active, p_active)[e], 0)]
        elif part == 1:
            pairs = [(own(e, first), 0)]
        else:
            pairs = [((q_rows, p_rows)[e], 0), (own(e, context), features)]
        return [
            pltpu.make_async_copy(
                ref,
                left_buf.at[pl.ds(0, count), pl.ds(at, ref.shape[1])],
                load_sem.at[2 + i],
            )
            for i, (ref, at) in enumerate(pairs)
        ]

    def right_loads(e, k):
        count = tokens[e]
        slot = place[e, k] % 2
        if k < 3:
            pairs = [(second, 256 * k, 256, 0)]
        elif k < 6:
            pairs = [(hidden, 1024 * (k - 3), 1024, 0)]
        elif k < 8:
            pairs = [(packed_grad, 1024 * (k - 6), 1024, 0)]
        else:
            pairs = [(packed_grad, 2048, 256, 0), (branch, 0, 768, 256)]
        return [
            pltpu.make_async_copy(
                own(e, ref).at[:, pl.ds(start, width)],
                right_buf.at[slot, pl.ds(0, count), pl.ds(at, width)],
                load_sem.at[slot] if i == 0 else load_sem.at[4],
            )
            for i, (ref, start, width, at) in enumerate(pairs)
        ]

    def begin(copies):
        for copy in copies:
            copy.start()

    def finish(copies):
        for copy in copies:
            copy.wait()

    def transpose_left(e, part):
        count = tokens[e]
        width = (3072, 768, 1536)[part]

        def step(i, carry):
            at = pl.multiple_of(i * 256, 256)
            left_t[pl.ds(at, 256), pl.ds(0, count)] = left_buf[pl.ds(0, count), pl.ds(at, 256)].T
            return carry

        lax.fori_loop(0, width // 256, step, 0)

    def compute(e, k):
        count = tokens[e]
        c = place[e, k]
        slot = c % 2

        def step(q, carry):
            if k < 3:
                rows_at, columns_at = q * 768, 0
            elif k < 8:
                rows_at, columns_at = 0, q * 256
            else:
                rows_at, columns_at = jnp.where(q > 0, 768, 0), q * 256
            rows_at = pl.multiple_of(rows_at, 256)
            columns_at = pl.multiple_of(columns_at, 256)
            product[...] = jnp.dot(
                left_t[pl.ds(rows_at, 768), pl.ds(0, count)],
                right_buf[slot, pl.ds(0, count), pl.ds(columns_at, 256)],
                preferred_element_type=jnp.float32,
            )
            if k < 3:
                for iy in range(2):
                    for sub in range(4):
                        for which, target in ((core, keep.at[c % ring]), (1 - core, core_send.at[slot])):
                            at = pl.multiple_of((2 * iy + which) * 192 + sub * 48, 16)
                            block = product[pl.ds(at, 48), :].astype(jnp.bfloat16)
                            target[sub * 2, q, iy] = block[:, :lane]
                            target[sub * 2 + 1, q, iy] = block[:, lane:]
            else:
                for iz in range(4):
                    for iy in range(2):
                        for which, target in ((core, keep.at[c % ring]), (1 - core, core_send.at[slot])):
                            at = pl.multiple_of((4 * iz + 2 * iy + which) * 48, 16)
                            block = product[pl.ds(at, 48), :].astype(jnp.bfloat16)
                            target[2 * q, iz, iy] = block[:, :lane]
                            target[2 * q + 1, iz, iy] = block[:, lane:]
            return carry

        lax.fori_loop(0, 4, step, 0)

    part_of = lambda k: 0 if k < 3 else 1 if k < 6 else 2

    def produce(c):
        e, k = order[c]
        if c >= 2:
            copy_core(c - 2).wait_send()
        if k % 3 == 0:
            finish(left_loads(e, part_of(k)))
            transpose_left(e, part_of(k))
            if c + 3 < chunks:
                e2, k2 = order[c + 3]
                begin(left_loads(e2, part_of(k2)))
        try_right(c)
        finish(right_loads(e, k))
        compute(e, k)
        if c >= 2:
            pl.semaphore_wait(credit, 1)
        copy_core(c).start()

    def write(c, panel, value):
        e, k = order[c]
        if k < 3:
            rows = pl.ds(panel // 2 * panel_rows, panel_rows)
            shrink_out[e, rows, pl.ds(256 * k + panel % 2 * lane, lane)] = value
        elif k < 6:
            expand_out[e, :, pl.ds(1024 * (k - 3) + panel * lane, lane)] = value
        else:
            at = 1024 * (k - 6) + panel * lane
            width = projection_out.shape[2]
            if at < width:
                projection_out[e, :, pl.ds(at, lane)] = value
            else:
                mixing_out[e, :, pl.ds(at - width, lane)] = value

    def after_core(c):
        copy_core(c).wait_recv()

        def step(p, carry):
            keep[c % ring, p] = keep[c % ring, p] + core_recv[c % 2, p]
            return carry

        lax.fori_loop(0, chunk_panels, step, 0)
        copy_xa(c).start()
        copy_yb(c).start()

        if c < chunks - 2:
            pl.semaphore_signal(credit, inc=1, device_id=at_core, device_id_type=MESH)

    def after_first(c):
        first, half = by_x(c), by_x(c) // 2
        copy_yb(c).wait_recv()

        def step_b(p, carry):
            for iz in range(4):
                keep[c % ring, first + p, iz, y] = keep[c % ring, first + p, iz, y] + recv_yb[c % ring, p, iz]
            return carry

        lax.fori_loop(0, chunk_panels - first, step_b, 0)
        for d in range(3):
            copy_zb(c, d).start()
        copy_xa(c).wait_recv()

        def step_a(p, carry):
            keep[c % ring, half * x + p] = keep[c % ring, half * x + p] + recv_x[c % ring, p]
            return carry

        lax.fori_loop(0, half, step_a, 0)
        copy_ya(c).start()

    def widen(value):
        return value.astype(jnp.float32)

    def after_second(c):
        first, half = by_x(c), by_x(c) // 2
        copy_ya(c).wait_recv()

        def step_a(p, carry):
            for iz in range(4):
                keep[c % ring, half * x + p, iz, y] = keep[c % ring, half * x + p, iz, y] + recv_ya[c % ring, p, iz]
            return carry

        lax.fori_loop(0, half, step_a, 0)
        for d in range(3):
            copy_za(c, d).start()
        for d in range(3):
            copy_zb(c, d).wait_recv()

        def step_b(p, carry):
            fin_b[c % ring, x, p] = (
                widen(keep[c % ring, first + p, z, y])
                + widen(recv_zb[c % ring, 0, p])
                + widen(recv_zb[c % ring, 1, p])
                + widen(recv_zb[c % ring, 2, p])
            ).astype(jnp.bfloat16)
            return carry

        lax.fori_loop(0, chunk_panels - first, step_b, 0)
        copy_xb(c).start()

    def after_third(c):
        first, half = by_x(c), by_x(c) // 2
        for d in range(3):
            copy_za(c, d).wait_recv()

        def step_a(p, carry):
            fin_a[c % ring, half * x + p] = (
                widen(keep[c % ring, half * x + p, z, y])
                + widen(recv_za[c % ring, 0, p])
                + widen(recv_za[c % ring, 1, p])
                + widen(recv_za[c % ring, 2, p])
            ).astype(jnp.bfloat16)
            return carry

        lax.fori_loop(0, half, step_a, 0)
        copy_ag(c).start()
        copy_xb(c).wait_recv()
        for p in range(chunk_panels - first):
            write(c, first + p, widen(fin_b[c % ring, 0, p]) + widen(fin_b[c % ring, 1, p]))

    def after_last(c):
        copy_ag(c).wait_recv()
        copy_xa(c).wait_send()
        copy_ya(c).wait_send()
        copy_ag(c).wait_send()
        copy_yb(c).wait_send()
        copy_xb(c).wait_send()
        for d in range(3):
            copy_za(c, d).wait_send()
            copy_zb(c, d).wait_send()

        for p in range(by_x(c)):
            write(c, p, widen(fin_a[c % ring, p]))

    q_blocks = tokens[0] // block_tokens
    blocks = (tokens[0] + tokens[1]) // block_tokens
    buffers = (w0, w1, w2, w3)

    def weight_copy(which, e):
        source = (projection, mixing, expand, shrink)[which]
        return pltpu.make_async_copy(source.at[e], buffers[which], weight_sem.at[which])

    def rows_of(b):
        return pl.ds(b * block_tokens, block_tokens)

    def input_rows(b, q_ref, p_ref):
        return q_ref.at[rows_of(b)] if b < q_blocks else p_ref.at[rows_of(b - q_blocks)]

    def copies(pairs, sem):
        return [pltpu.make_async_copy(src, dst, sem) for (src, dst), sem in pairs]

    def loads(half, b):
        at = rows_of(b)
        if half == 0:
            pairs = [
                (input_rows(b, *refs), buffer)
                for refs, buffer in (
                    ((q_cot, p_cot), b_cot), ((q_n2, p_n2), b_n2), ((q_stats, p_stats), b_stats), ((q_slope, p_slope), b_slope)
                )
            ] + [(n1.at[at], b_n1)]
        elif half == 1:
            pairs = [(input_rows(b, q_grad, p_grad), b_total_in), (chances.at[b], b_chances)]
            pairs += [(ref.at[at], buffer) for ref, buffer in ((branch, b_branch_in), (packed, b_packed), (context, b_context))]
        else:
            pairs = [(input_rows(b, q_grad, p_grad), b_total_in), (packed_grad.at[at], b_packed_grad)]
        return [pltpu.make_async_copy(src, dst, in_sem.at[half, i]) for i, (src, dst) in enumerate(pairs)]

    def stores(half, b):
        at = rows_of(b)
        if half == 0:
            pairs = [(b_second, second.at[at]), (b_hidden, hidden.at[at]), (b_branch, branch.at[at]), (b_total, input_rows(b, q_grad, p_grad))]
        elif half == 1:
            pairs = [(b_packed_grad, packed_grad.at[at])]
        else:
            pairs = [(b_grad, input_rows(b, q_grad, p_grad))]
        return [pltpu.make_async_copy(src, dst, out_sem.at[half, i]) for i, (src, dst) in enumerate(pairs)]

    stored, done, started, waited = set(), set(), set(), set()

    def settle(half, b):
        if (half, b) in done and (half, b) not in stored:
            stored.add((half, b))
            finish(stores(half, b))

    def start_loads(half, b, which):
        if b < blocks and (half == 0 or (half - 1, b) in done):
            if half > 0:
                settle(half - 1, b)
            for i in which:
                if (half, b, i) not in started:
                    started.add((half, b, i))
                    loads(half, b)[i].start()

    def weight_of(e):
        def get(which):
            if (which, e) not in waited:
                waited.add((which, e))
                weight_copy(which, e).wait()
            return buffers[which]

        return get

    def part(b, which):
        e = int(b >= q_blocks)
        half = which // 2

        def gradient():
            at = jnp.zeros((1, 1), jnp.int32)
            starts = []
            for k in range(cls_slots):
                if e == 0:
                    starts.append(k * (block_tokens // cls_slots))
                else:
                    starts.append(at)
                    if k < cls_slots - 1:
                        at = at + lengths[pl.ds(b - q_blocks, 1), pl.ds(k, 1)]
            return with_cls(b_cot[...].astype(jnp.float32), starts, cls_grad, b * cls_slots)

        rows = small_sum.shape[1] // 2
        block = Back(
            gradient=gradient, chances=b_chances, stats=b_stats, packed=b_packed, context=b_context,
            n1=b_n1, n2=b_n2, slope=b_slope, second=b_second, hidden=b_hidden,
            branch=b_branch if half == 0 else b_branch_in, packed_grad=b_packed_grad,
            small=small_sum.at[0, pl.ds(e * rows, rows)], total=b_total if half == 0 else b_total_in,
            mixed=b_mixed, weight=weight_of(e), gain_rows=gains[e].astype(jnp.float32),
        )
        if which == 0:
            start_loads(0, b, range(5))
            finish(loads(0, b)[:4])
            settle(0, b - 1)
            block.part_a()
            start_loads(0, b + 1, range(2))
        elif which == 1:
            finish(loads(0, b)[4:])
            block.part_b()
            begin(stores(0, b))
            done.add((0, b))
            start_loads(0, b + 1, range(5))
            if b == 0:
                start_loads(1, 0, range(1, 5))
        elif which == 2:
            start_loads(1, b, range(1, 5))
            finish(loads(1, b)[1:])
            settle(1, b - 1)
            block.part_c()
            begin(stores(1, b))
            done.add((1, b))
            start_loads(1, b + 1, range(1, 5))
            if e == 0:
                start_loads(1, b, range(1))
        else:
            if e == 0:
                finish(loads(1, b)[:1])
            else:
                start_loads(2, b, range(2))
                finish(loads(2, b))
            settle(2, b - 1)
            b_grad[...] = block.part_d()
            begin(stores(2, b))
            done.add((2, b))
            if e == 1:
                start_loads(2, b + 1, range(2))
        if b + 1 == q_blocks and which in (1, 3):
            for again in ((3, 2), (1, 0))[which // 2]:
                weight_copy(again, 1).start()

    right_begun = set()

    def try_right(c):
        if c >= chunks or c in right_begun:
            return
        e, k = order[c]
        half = int(k >= 6)
        mine = range(q_blocks) if e == 0 else range(q_blocks, blocks)
        if all((half, b) in done for b in mine):
            for b in mine:
                settle(half, b)
            right_begun.add(c)
            begin(right_loads(e, k))

    start_loads(0, 0, range(5))
    begin([weight_copy(which, 0) for which in (3, 2)])
    barrier = pltpu.get_barrier_semaphore()
    for device in [at_core, at_y, at_x] + at_z:
        pl.semaphore_signal(barrier, inc=1, device_id=device, device_id_type=MESH)
    pl.semaphore_wait(barrier, 6)
    small_sum[0] = jnp.zeros(small_out.shape, jnp.float32)
    begin(left_loads(order[0][0], part_of(order[0][1])))
    part(0, 0)
    begin([weight_copy(which, 0) for which in (1, 0)])
    part(0, 1)
    for b in range(1, q_blocks):
        part(b, 0)
        part(b, 1)

    first_ones = [(b, which) for b in range(q_blocks) for which in (2, 3)]
    then = [(b, which) for b in range(q_blocks, blocks) for which in (0, 1)]
    early = [item for both in zip(first_ones, then) for item in both] + then[len(first_ones):]
    late = [(b, 2) for b in range(q_blocks, blocks)]
    rest = [(b, 3) for b in range(q_blocks, blocks)]
    points = {}
    for todo, begin_at, end_at in (
        (early, 1, encoder_chunks - 1), (late, encoder_chunks, encoder_chunks + 5), (rest, chunks, chunks + 3)
    ):
        spots = [(c, i) for c in range(begin_at, end_at + 1) for i in range(2)][: 2 * (end_at - begin_at) + 1]
        for i, item in enumerate(todo):
            points.setdefault(spots[i * len(spots) // len(todo)], []).append(item)

    def parts(c, i):
        for item in points.get((c, i), []):
            part(*item)

    for c in range(chunks + 5):
        if c < chunks:
            produce(c)
        if 0 <= c - 1 < chunks:
            after_core(c - 1)
        parts(c, 0)
        try_right(c + 1)
        if 0 <= c - 2 < chunks:
            after_first(c - 2)
        if 0 <= c - 3 < chunks:
            after_second(c - 3)
        parts(c, 1)
        if 0 <= c - 4 < chunks:
            after_third(c - 4)
        if 0 <= c - 5 < chunks:
            after_last(c - 5)
        if c == encoder_chunks + 6:
            for b in range(blocks):
                settle(1, b)
            small_copy(0, at_core).start()
        if c == encoder_chunks + 7:
            small_copy(0, at_core).wait_recv()
            small_sum[1] = small_sum[0] + small_recv[0]
            small_copy(1, at_x).start()
        if c == encoder_chunks + 8:
            small_copy(1, at_x).wait_recv()
            small_sum[2] = small_sum[1] + small_recv[1]
            small_copy(2, at_y).start()
        if c == encoder_chunks + 9:
            small_copy(2, at_y).wait_recv()
            small_sum[3] = small_sum[2] + small_recv[2]
            for d in range(3):
                remote(small_sum.at[3], small_recv.at[3 + d], small_ss.at[3 + d], small_rs.at[3 + d], at_z[d]).start()
        if c == encoder_chunks + 10:
            for d in range(3):
                remote(small_sum.at[3], small_recv.at[3 + d], small_ss.at[3 + d], small_rs.at[3 + d], at_z[d]).wait_recv()
            result = jnp.zeros(small_out.shape, jnp.float32)
            for iz in range(4):
                back = (z - iz + 4) % 4
                value = jnp.where(back == 0, small_sum[3], 0.0)
                for d in range(3):
                    value = jnp.where(back == d + 1, small_recv[3 + d], value)
                result = result + value
            small_out[...] = result

    for b in range(blocks):
        for half in range(3):
            settle(half, b)

    copy_core(chunks - 2).wait_send()
    copy_core(chunks - 1).wait_send()

    small_copy(0, at_core).wait_send()
    small_copy(1, at_x).wait_send()
    small_copy(2, at_y).wait_send()
    for d in range(3):
        remote(small_sum.at[3], small_recv.at[3 + d], small_ss.at[3 + d], small_rs.at[3 + d], at_z[d]).wait_send()


def reduce_by_kernel(lengths, q_rows, p_rows, q_cot, p_cot, cls_grad, saved, stacked):
    projection, mixing, expand, shrink, biases, gains, widening = stacked
    chances, packed, context, first, n1, q_side, p_side = saved
    (q_stats, q_n2, q_active, q_slope), (p_stats, p_n2, p_active, p_slope) = q_side, p_side
    features, wide = projection.shape[1], expand.shape[2]
    tokens = (q_rows.shape[0], p_rows.shape[0])
    all_tokens = sum(tokens)
    small = jax.ShapeDtypeStruct((2 * (-(-(8 + wide // features) // 8) * 8), features), jnp.float32)
    most = max(tokens)
    chunks = 2 * encoder_chunks
    tile = (panel_rows, lane)
    low = jnp.bfloat16
    dma = pltpu.SemaphoreType.DMA
    one, three = dma((chunks,)), dma((chunks, 3))
    block = lambda width, kind=low: pltpu.VMEM((block_tokens, width), kind)
    shape = jax.ShapeDtypeStruct
    return pl.pallas_call(
        partial(reduce_kernel, tokens),
        out_shape=[
            shape((all_tokens, features), low), shape((all_tokens, wide), low),
            shape((all_tokens, features), low), shape((all_tokens, 3 * features), low),
            shape(q_cot.shape, jnp.float32), shape(p_cot.shape, jnp.float32),
            shape((2, 48, 2304), jnp.float32),
            shape((2, 48, 768), jnp.float32),
            shape((2, 48, 3072), jnp.float32),
            shape((2, 192, 768), jnp.float32),
            small,
        ],
        in_specs=[pl.BlockSpec(memory_space=pl.ANY)] * 21 + [pl.BlockSpec(memory_space=pltpu.VMEM)] * 3,
        out_specs=[pl.BlockSpec(memory_space=pl.ANY)] * 6 + [pl.BlockSpec(memory_space=pltpu.VMEM)] * 5,
        scratch_shapes=[
            pltpu.VMEM((ring, chunk_panels, 4, 2) + tile, low),
            pltpu.VMEM((2, chunk_panels, 4, 2) + tile, low),
            pltpu.VMEM((2, chunk_panels, 4, 2) + tile, low),
            pltpu.VMEM((ring, 3, 4, 2) + tile, low),
            pltpu.VMEM((ring, 3, 4) + tile, low),
            pltpu.VMEM((ring, 3, 3) + tile, low),
            pltpu.VMEM((ring, 4, 4) + tile, low),
            pltpu.VMEM((ring, 3, 4) + tile, low),
            pltpu.VMEM((ring, 6) + tile, low),
            pltpu.VMEM((ring, 2, 4) + tile, low),
            pltpu.VMEM((most, 3072), low),
            pltpu.VMEM((3072, most), low),
            pltpu.VMEM((2, most, 1024), low),
            pltpu.VMEM((768, 256), jnp.float32),
            pltpu.VMEM((6,) + small.shape, jnp.float32),
            pltpu.VMEM((4,) + small.shape, jnp.float32),
            dma((5,)),
            one, one, one, one, one, one, three, three, one, one,
            one, one, three, three, one, one, dma((6,)), dma((6,)),
            pltpu.SemaphoreType.REGULAR,
        ] + [pltpu.VMEM(w.shape[1:], low) for w in (projection, mixing, expand, shrink)] + [
            dma((4,)), dma((3, 5)), dma((3, 4)),
            block(features), block(lane, jnp.float32), block(features), block(features), block(wide),
            block(features), block(wide), block(features), block(features, jnp.float32),
            pltpu.VMEM((HEADS, block_tokens, block_tokens), low), block(3 * features), block(features),
            block(features), block(features, jnp.float32), block(3 * features), block(features, jnp.float32),
            block(features),
        ],
        compiler_params=pltpu.CompilerParams(
            collective_id=1, has_side_effects=True, vmem_limit_bytes=vmem_bytes
        ),
        cost_estimate=pl.CostEstimate(flops=50 * 10**9, bytes_accessed=200 * 10**6, transcendentals=0),
    )(
        q_active, p_active, first, context, q_rows, p_rows, q_cot, p_cot, chances, q_stats, p_stats, packed, n1,
        q_n2, p_n2, q_slope, p_slope, projection, mixing, expand, shrink, lengths, cls_grad, gains,
    )


def finish_kernel(*refs):
    count = len(refs) // 2 - 2
    small, outs = refs[count], refs[count + 1 :]
    biases, gains, widening = outs[count:]
    for src, dst in zip(refs[:count], outs[:count]):
        dst[...] = src[...]
    mine = lax.axis_index("pa")
    rows, features = small.shape[0] // 2, small.shape[1]
    share, wide = biases.shape[2], widening.shape[1]
    per_row = features // wide
    turned = pltpu.roll(small[...], features - mine * share, 1)[:, :share]
    for e in range(2):
        biases[e] = turned[e * rows : e * rows + 6]
        gains[e] = turned[e * rows + 6 : e * rows + 8]
        row = small[pl.ds(e * rows + 8 + mine // per_row, 1), :]
        widening[pl.ds(e, 1), :] = pltpu.roll(row, features - mine % per_row * wide, 1)[:, :wide]


def finish_all(arrays, small, wide):
    shape = jax.ShapeDtypeStruct
    size_pa = lax.axis_size("pa")
    features = small.shape[1]
    share, wide = features // size_pa, wide // size_pa
    steps = 4

    def cut(array):
        block = array.shape[:-2] + (array.shape[-2] // steps, array.shape[-1])
        axis = len(block) - 2
        return pl.BlockSpec(block, lambda i: tuple(i if d == axis else 0 for d in range(len(block))))

    def whole(dims):
        return pl.BlockSpec(dims, lambda i: (0,) * len(dims))

    cuts = [cut(a) if a.shape[-2] % (16 * steps) == 0 else whole(a.shape) for a in arrays]
    own = [(2, 6, share), (2, 2, share), (2, wide)]
    return pl.pallas_call(
        finish_kernel,
        out_shape=[shape(a.shape, a.dtype) for a in arrays] + [shape(dims, jnp.float32) for dims in own],
        grid=(steps,),
        in_specs=cuts + [whole(small.shape)],
        out_specs=cuts + [whole(dims) for dims in own],
        compiler_params=pltpu.CompilerParams(vmem_limit_bytes=vmem_bytes),
    )(*arrays, small)


def backward_all(lengths, q_rows, p_rows, q_cot, p_cot, cls_grad, saved, stacked, p_states):
    size_pa, size_pb = lax.axis_size("pa"), lax.axis_size("pb")
    features = q_rows.shape[1]
    if size_pa == 16 and size_pb == 2:
        reduced = reduce_by_kernel(lengths, q_rows, p_rows, q_cot, p_cot, cls_grad, saved, stacked)
        p_states, q_grad, p_grad, *totals = finish_all(
            (p_states, *reduced[4:10]), reduced[10], stacked[6].shape[1]
        )
        return p_states, q_grad, p_grad, tuple(totals)
    chances, packed, context, first, n1, q_side, p_side = saved
    cut = q_rows.shape[0]
    stats, n2, active, slope = (jnp.concatenate([q_part[:cut], p_part]) for q_part, p_part in zip(q_side, p_side))
    q_grad, p_grad, second, hidden, branch, packed_grad, small = encode_all_back(
        lengths, q_cot, p_cot, cls_grad, (chances, stats, packed, context, n1, n2, slope), stacked
    )
    products = []
    cut = q_rows.shape[0]
    for rows, part in ((q_rows, slice(None, cut)), (p_rows, slice(cut, None))):
        pairs = ((rows, packed_grad[part]), (context[part], branch[part]), (first[part], hidden[part]), (active[part], second[part]))
        products.append([contract_rows(*pair) for pair in pairs])
    projection, mixing, expand, shrink = (
        lax.psum(
            jnp.stack(
                [
                    lax.psum_scatter(products[e][i], "pa", scatter_dimension=0, tiled=True)
                    for e in range(2)
                ]
            ),
            "pb",
        )
        for i in range(4)
    )
    small = lax.psum(small, ("pb", "pa"))
    mine = lax.axis_index("pa")
    share = features // size_pa
    columns = lax.dynamic_slice_in_dim(small[:, :8], mine * share, share, 2)
    widening = small[:, 8:].reshape(2, -1)
    wide = widening.shape[1] // size_pa
    widening = lax.dynamic_slice_in_dim(widening, mine * wide, wide, 1)
    return p_states, q_grad, p_grad, (projection, mixing, expand, shrink, columns[:, :6], columns[:, 6:], widening)


def body(
    question_rows,
    passage_rows,
    segment_lengths,
    positives,
    negatives,
    question_cotangent,
    passage_cotangent,
    loss_weight,
    projection,
    mixing,
    expand,
    shrink,
    biases,
    gains,
    widening,
):
    stacked = (projection, mixing, expand, shrink, biases, gains, widening)
    question_count, _, features = question_rows.shape
    q_rows = question_rows.reshape(-1, features)
    p_rows = passage_rows.reshape(-1, features)
    (
        q_states, cls, chances, stats, packed, context, first, n1, wide_first, q_n2, q_active, q_slope,
    ) = encode_all(segment_lengths, q_rows, p_rows, stacked)
    cls_grad, question_loss, p_states, p_side = contrast(
        cls, question_count, positives, loss_weight, negatives, first, wide_first, stats, stacked
    )
    q_side = (stats, q_n2, q_active, q_slope)
    saved = (chances, packed, context, first, n1, q_side, p_side)
    p_states, q_grad, p_grad, totals = backward_all(
        segment_lengths,
        q_rows,
        p_rows,
        question_cotangent.reshape(-1, features),
        passage_cotangent.reshape(-1, features),
        cls_grad,
        saved,
        stacked,
        p_states,
    )
    return (
        q_states.reshape(question_rows.shape),
        p_states.reshape(passage_rows.shape),
        question_loss,
        q_grad.reshape(question_rows.shape),
        p_grad.reshape(passage_rows.shape),
    ) + totals


def solution(mesh):
    return jax.shard_map(
        body,
        mesh=mesh,
        in_specs=(
            P(("pb", "pa"), None, None),
            P(("pb", "pa"), None, None),
            P(("pb", "pa"), None),
            P("pb"),
            P("pa", None),
            P(("pb", "pa"), None, None),
            P(("pb", "pa"), None, None),
            P("pb"),
            P(),
            P(),
            P(),
            P(),
            P(),
            P(),
            P(),
        ),
        out_specs=(
            P(("pb", "pa"), None, None),
            P(("pb", "pa"), None, None),
            P("pb"),
            P(("pb", "pa"), None, None),
            P(("pb", "pa"), None, None),
            P(None, "pa", None),
            P(None, "pa", None),
            P(None, "pa", None),
            P(None, "pa", None),
            P(None, None, "pa"),
            P(None, None, "pa"),
            P(None, "pa"),
        ),
        check_vma=False,
    )
```
